32 devices in a mesh: group: 2 (over x), dp: 16 (over z, y, core).
Axes of the slice: x: 2, y: 2, z: 4, core: 2. Of those that a mesh axis runs over, the one named last changes fastest.
Arguments:
- states: bfloat16 [8192, 8192], P(('group', 'dp')), parts along dimension 0, may hold values from -6 to 6
- queries: bfloat16 [8192, 4096], P(('group', 'dp')), parts along dimension 0, may hold values from -160 to 160
- kv_weight: bfloat16 [8192, 1024], P('dp'), may hold values from -0.0625 to 0.0625
- kv_bias: float32 [1024], replicated, may hold values from -3 to 3
- lengths: int32 [32], P(('group', 'dp')), parts along dimension 0, may hold values from 2 to 32, as said below
- bounds: int32 [32, 2], P(('group', 'dp')), parts along dimension 0, may hold values from 1 to 255, as said below
- balance: int32 [32, 32], P(('group', 'dp')), parts along dimension 0, may hold values from 0 to 15, as said below
Outputs:
- context: bfloat16 [8192, 4096], P(('group', 'dp')), parts along dimension 0
- work_rows: bfloat16 [6144, 1024], P(('group', 'dp')), parts along dimension 0
The draws below stay inside these ranges and needn't reach their ends.
There are 2 independent parts, one for each index of `group`. The reference program is written for one: setup_inputs(seed, part) draws one part's arguments, and reference() takes and returns one part's arrays. A program takes and returns all parts, laid end to end along the dimension named above; an argument that names none is the same for every part. Nothing has to cross between parts.
Inputs may be any that keep to these rules, and one draw needn't show every extreme that they name: `lengths`: half of the replicas, drawn from the seed, hold 24 or more spans, the others at most 16; one replica holds 32. balance[r, j] = r for j < 24 and for slots past the pair; the slots from 24 up to the pair's end go to other replicas with fewer than 24 spans; a replica sends at most one span to any other, and no replica computes more than 24 spans, one exactly 24. 1 <= bounds[r, 0] < bounds[r, 1] < lengths[r] * 8.
All inputs are finite; a program needn't handle non-finite values.
Results may differ from the reference program's by a relative error of at most 0.012.
The reference program's roundings to bfloat16 on the way count: a program that leaves them out, or rounds other values in their place, can miss the bound.
Values may be sent and summed in bfloat16 or wider, within the bound.
No kernel may reach another device: no remote copies, remote signals or barrier semaphores. Data moves between devices by JAX's collectives and lax.ppermute only.
A program may use at most 128 MiB of HBM per device.

```python
import math
import jax
import jax.numpy as jnp
from jax import lax

D = 8192
HEAD = 128
Q_HEADS = 32
SPAN = 8
HOME = 32
WORK = 24
QW = 4096
KVW = 1024
TOKENS = 4096
N_DP = 16


def pair_plan(key):
    replicas = N_DP
    half_count = replicas // 2
    order = jax.random.permutation(jax.random.fold_in(key, 11), replicas).astype(jnp.int32)
    heavy = order < half_count
    light_len = jax.random.randint(jax.random.fold_in(key, 12), (replicas,), 2, 2 * WORK - HOME + 1)
    heavy_len = jax.random.randint(jax.random.fold_in(key, 13), (replicas,), WORK, HOME + 1)
    lengths = jnp.where(heavy, heavy_len, light_len)
    lengths = jnp.where(order == 0, HOME, lengths).astype(jnp.int32)
    inverse = jnp.zeros((replicas,), jnp.int32).at[order].set(jnp.arange(replicas, dtype=jnp.int32))
    slot_ids = jnp.arange(HOME, dtype=jnp.int32)
    surplus = (slot_ids[None, :] >= WORK) & (slot_ids[None, :] < lengths[:, None])
    flat = surplus.reshape(-1).astype(jnp.int32)
    index = jnp.cumsum(flat) - flat
    receiver = inverse[half_count + index % half_count].reshape(replicas, HOME)
    owners = jnp.broadcast_to(jnp.arange(replicas, dtype=jnp.int32)[:, None], (replicas, HOME))
    destination = jnp.where(surplus, receiver, owners).astype(jnp.int32)
    return (lengths, destination, order)


def draw_lengths(key, part):
    lengths, destination, order = pair_plan(key)
    return lengths


def draw_balance(key, part):
    lengths, destination, order = pair_plan(key)
    return destination


def draw_bounds(key, part):
    lengths, destination, order = pair_plan(key)
    key = jax.random.fold_in(key, 21)
    total = lengths * SPAN
    chosen = jax.random.randint(jax.random.fold_in(key, 1), (N_DP,), 1, total // 2)
    chosen = jnp.where(order == 1, 1, chosen)
    rejected = jax.random.randint(jax.random.fold_in(key, 2), (N_DP,), chosen + 1, total)
    rejected = jnp.where(order == 0, total - 1, rejected)
    return jnp.stack([chosen, rejected], axis=1).astype(jnp.int32)


def draw_queries(key, part):
    key = jax.random.fold_in(key, 31)
    shape = (N_DP * HOME * SPAN, Q_HEADS * HEAD)
    normal_draw = jax.random.truncated_normal(jax.random.fold_in(key, 1), -4.0, 4.0, shape, jnp.float32)
    return normal_draw.astype(jnp.bfloat16)


def block_scale(own_key, dims, cuts, smallest, largest):
    gain = 1.0
    for dim, parts in cuts:
        heights = jax.random.uniform(jax.random.fold_in(jax.random.fold_in(own_key, 6), dim), (parts,), jnp.float32, smallest / len(cuts), largest / len(cuts))
        gain = gain * jnp.repeat(jnp.exp(heights), dims[dim] // parts).reshape((-1,) + (1,) * (len(dims) - 1 - dim))
    return gain


def centred(stream_key, dims, deviation, bound, pieces=(), held_as=jnp.bfloat16):
    level = block_scale(stream_key, dims, pieces, -0.22, 0.18) if pieces else 1.0
    array = jax.random.normal(stream_key, dims, jnp.float32) * deviation * level
    return jnp.minimum(jnp.maximum(array, -bound), bound).astype(held_as)


def setup_inputs(seed: int = 0, part: int = 0) -> dict:
    key_list = jax.random.split(jax.random.key(seed), 8)
    part_splits = jax.random.split(jax.random.fold_in(key_list[7], part), 8)
    states = centred(part_splits[0], (TOKENS, D), 1.0, 6.0, ((0, 16),))
    queries = draw_queries(jax.random.fold_in(jax.random.fold_in(key_list[7], part), 71), part)
    kv_weight = centred(key_list[2], (D, KVW), D ** -0.5, 0.0625, ((0, 16),))
    kv_bias = centred(key_list[3], (KVW,), 0.5, 3.0, (), jnp.float32)
    lengths = draw_lengths(jax.random.fold_in(jax.random.fold_in(key_list[7], part), 71), part)
    bounds = draw_bounds(jax.random.fold_in(jax.random.fold_in(key_list[7], part), 71), part)
    balance = draw_balance(jax.random.fold_in(jax.random.fold_in(key_list[7], part), 71), part)
    return dict(states=states, queries=queries, kv_weight=kv_weight, kv_bias=kv_bias, lengths=lengths, bounds=bounds, balance=balance)


def pair_layout(all_lengths, all_plans):
    replicas = all_lengths.shape[0]
    slot_ids = jnp.arange(HOME, dtype=jnp.int32)
    replica_ids = jnp.arange(replicas, dtype=jnp.int32)
    live_slot = slot_ids[None, :] < all_lengths[:, None]
    moved_slot = live_slot & (all_plans != replica_ids[:, None])
    kept_count = jnp.sum((live_slot & jnp.logical_not(moved_slot)).astype(jnp.int32), axis=1)
    onehot = ((all_plans[:, :, None] == replica_ids[None, None, :]) & moved_slot[:, :, None]).astype(jnp.int32)
    send_count = jnp.sum(onehot, axis=1)
    before = jnp.cumsum(send_count, axis=0) - send_count
    rank_moved = jnp.sum(onehot * (kept_count[None, None, :] + before[:, None, :]), axis=2)
    work_rank = jnp.where(moved_slot, rank_moved, slot_ids[None, :])
    return live_slot, moved_slot, work_rank


def rotate(key_rows, position):
    half_head = key_rows.shape[-1] // 2
    frequency = jnp.exp(jnp.arange(half_head, dtype=jnp.float32) * (-2.0 * math.log(1e6) / key_rows.shape[-1]))
    angles = position.astype(jnp.float32)[:, None] * frequency[None, :]
    cosines = jnp.cos(angles)[:, None, :]
    sines = jnp.sin(angles)[:, None, :]
    first = key_rows[..., :half_head]
    second = key_rows[..., half_head:]
    return jnp.concatenate([first * cosines - second * sines, second * cosines + first * sines], axis=-1)


def attend(query_rows, kv_rows, length, chosen_start, rejected_start):
    row_count = query_rows.shape[0]
    kv_heads = kv_rows.shape[1] // (2 * HEAD)
    group_size = query_rows.shape[1] // (kv_heads * HEAD)
    token_ids = jnp.arange(row_count, dtype=jnp.int32)
    segment = (token_ids >= chosen_start).astype(jnp.int32) + (token_ids >= rejected_start).astype(jnp.int32)
    position = jnp.where(token_ids >= rejected_start, token_ids - (rejected_start - chosen_start), token_ids)
    is_live = token_ids < length * SPAN
    key_rows = kv_rows[:, :kv_heads * HEAD].astype(jnp.float32).reshape(row_count, kv_heads, HEAD)
    key_rows = rotate(key_rows, position).astype(jnp.bfloat16)
    value_rows = kv_rows[:, kv_heads * HEAD:].reshape(row_count, kv_heads, HEAD)
    query_heads = query_rows.reshape(row_count, kv_heads, group_size, HEAD)
    scores = jnp.einsum("tkgh,skh->kgts", query_heads.astype(jnp.float32), key_rows.astype(jnp.float32)) * (HEAD ** -0.5)
    allowed = (token_ids[None, :] <= token_ids[:, None]) & is_live[None, :] & ((segment[None, :] == segment[:, None]) | (segment[None, :] == 0))
    allowed = allowed | (token_ids[None, :] == token_ids[:, None])
    scores = jnp.where(allowed[None, None], scores, -1e30)
    row_max = jnp.max(scores, axis=-1, keepdims=True)
    weights = jnp.exp(scores - row_max)
    weights = (weights / jnp.sum(weights, axis=-1, keepdims=True)).astype(jnp.bfloat16)
    mixed = jnp.einsum("kgts,skh->tkgh", weights.astype(jnp.float32), value_rows.astype(jnp.float32))
    mixed = mixed.reshape(row_count, -1)
    return jnp.where(is_live[:, None], mixed, 0.0).astype(jnp.bfloat16)


def reference(states, queries, kv_weight, kv_bias, lengths, bounds, balance):
    replicas = lengths.shape[0]
    live_slot, moved_slot, work_rank = pair_layout(lengths, balance)

    def project_one(row_block):
        return (jnp.dot(row_block, kv_weight, preferred_element_type=jnp.float32) + kv_bias[None, :]).astype(jnp.bfloat16)

    home_kv = lax.map(project_one, states.reshape(replicas, HOME * SPAN, D))
    home_kv = home_kv.reshape(replicas, HOME, SPAN, KVW)
    home_kv = jnp.where(live_slot[:, :, None, None], home_kv, jnp.zeros((), jnp.bfloat16))
    target_slot = jnp.where(live_slot, balance * WORK + work_rank, replicas * WORK).astype(jnp.int32)
    work_kv = jnp.zeros((replicas * WORK + 1, SPAN, KVW), jnp.bfloat16)
    work_kv = work_kv.at[target_slot.reshape(-1)].set(home_kv.reshape(replicas * HOME, SPAN, KVW))
    work_rows = work_kv[:-1].reshape(replicas * WORK * SPAN, KVW)

    def attend_one(packed):
        return attend(packed[0], packed[1], packed[2], packed[3], packed[4])

    context = lax.map(attend_one, (queries.reshape(replicas, HOME * SPAN, QW), home_kv.reshape(replicas, HOME * SPAN, KVW), lengths, bounds[:, 0], bounds[:, 1]))
    return context.reshape(replicas * HOME * SPAN, QW), work_rows
```

```python
import math

import jax
import jax.numpy as jnp
from jax import lax
from jax.experimental import pallas as pl
from jax.experimental.pallas import tpu as pltpu
from jax.sharding import PartitionSpec as P

HEAD = 128
SPAN = 8
HOME = 32
WORK = 24
ABSENT = 1e30
MASKED = -1e30
MIB = 1 << 20


def ring_place(ring, position):
    return jnp.where(2 * position < ring, 2 * position, 2 * (ring - 1 - position) + 1)


class Links:
    def __init__(self, replicas, groups):
        ring = replicas // 4
        places = [p for p in range(0, ring, 2)] + [p for p in range(1, ring, 2)][::-1]
        ahead = {places[i]: places[(i + 1) % ring] for i in range(ring)}
        steps = [
            ((z * 2 + y) * 2 + c, (ahead[z] * 2 + y) * 2 + c)
            for z in range(ring)
            for y in range(2)
            for c in range(2)
        ]
        self.routes = {
            "fore": ("z", "dp", steps),
            "back": ("z", "dp", [(d, s) for s, d in steps]),
            "y": ("y", "dp", [(i, i ^ 2) for i in range(replicas)]),
            "x": ("x", "group", [(i, i ^ 1) for i in range(groups)]),
        }
        self.last = {}

    def send(self, value, route):
        link, axis, pairs = self.routes[route]
        if link in self.last:
            value = lax.optimization_barrier((value, self.last[link]))[0]
        self.last[link] = lax.ppermute(value, axis, pairs)
        return self.last[link]


def core_swap(value, replicas):
    return lax.ppermute(value, "dp", [(i, i ^ 1) for i in range(replicas)])


def multiply(own_states, peer_states, pieces, blocks, start=None):
    count = len(pieces)
    depth, columns = pieces[0].shape
    tokens = own_states.shape[0]

    def kernel(block_ref, own_ref, peer_ref, *refs):
        piece_refs = refs[:count]
        refs = refs[count:]
        if start is not None:
            start_refs, refs = refs[:2], refs[2:]
        own_out, peer_out, left, right, sems = refs
        copies = []
        for i in range(count):
            span = pl.ds(pl.multiple_of(block_ref[i] * depth, 128), depth)
            group = (
                pltpu.make_async_copy(piece_refs[i], right.at[i], sems.at[3 * i]),
                pltpu.make_async_copy(
                    own_ref.at[:, span], left.at[i, pl.ds(0, tokens)], sems.at[3 * i + 1]
                ),
                pltpu.make_async_copy(
                    peer_ref.at[:, span], left.at[i, pl.ds(tokens, tokens)], sems.at[3 * i + 2]
                ),
            )
            for copy in group:
                copy.start()
            copies.append(group)
        for i in range(count):
            for copy in copies[i]:
                copy.wait()
            product = jnp.dot(left[i], right[i], preferred_element_type=jnp.float32)
            for out, part, first in (
                (own_out, product[:tokens], 0),
                (peer_out, product[tokens:], 1),
            ):
                if i == 0:
                    out[...] = part if start is None else start_refs[first][...] + part
                else:
                    out[...] += part

    anywhere = pl.BlockSpec(memory_space=pl.ANY)
    inside = pl.BlockSpec(memory_space=pltpu.VMEM)
    total = jax.ShapeDtypeStruct((tokens, columns), jnp.float32)
    return pl.pallas_call(
        kernel,
        out_shape=(total, total),
        in_specs=[pl.BlockSpec(memory_space=pltpu.SMEM)]
        + [anywhere] * (2 + count)
        + [inside] * (0 if start is None else 2),
        out_specs=(inside, inside),
        scratch_shapes=[
            pltpu.VMEM((count, 2 * tokens, depth), jnp.bfloat16),
            pltpu.VMEM((count, depth, columns), jnp.bfloat16),
            pltpu.SemaphoreType.DMA((3 * count,)),
        ],
        compiler_params=pltpu.CompilerParams(vmem_limit_bytes=32 * MIB),
        cost_estimate=pl.CostEstimate(
            flops=4 * count * tokens * depth * columns,
            bytes_accessed=count * (4 * tokens * depth + 2 * depth * columns),
            transcendentals=0,
        ),
    )(blocks, own_states, peer_states, *pieces, *(() if start is None else start))


def finish(own_part, peer_part, bias, cosines, sines, destination, live_rows, replicas):
    tokens, columns = own_part.shape
    keys = columns // 2
    rows = replicas * SPAN

    def kernel(own_ref, peer_ref, bias_ref, cos_ref, sin_ref, dest_ref, live_ref, kv_ref, key_ref, out_ref):
        kv = (own_ref[...] + peer_ref[...] + bias_ref[...]).astype(jnp.bfloat16)
        kv = jnp.where(live_ref[...] > 0.5, kv.astype(jnp.float32), 0.0)
        kept = kv.astype(jnp.bfloat16)
        kv_ref[...] = kept
        row = lax.broadcasted_iota(jnp.int32, (rows, tokens), 0)
        token = lax.broadcasted_iota(jnp.int32, (rows, tokens), 1)
        match = (dest_ref[...] == row // SPAN) & (token % SPAN == row % SPAN)
        pick = jnp.where(match, 1.0, 0.0)
        found = jnp.sum(pick, axis=1, keepdims=True)
        spans = jnp.dot(pick.astype(jnp.bfloat16), kept, preferred_element_type=jnp.float32)
        out_ref[...] = jnp.where(found > 0.5, spans, ABSENT).astype(jnp.bfloat16)
        for head in range(keys // HEAD):
            part = kv[:, head * HEAD : (head + 1) * HEAD]
            turned = part * cos_ref[...] + pltpu.roll(part, HEAD // 2, 1) * sin_ref[...]
            key_ref[:, head * HEAD : (head + 1) * HEAD] = turned.astype(jnp.bfloat16)

    return pl.pallas_call(
        kernel,
        out_shape=(
            jax.ShapeDtypeStruct((tokens, columns), jnp.bfloat16),
            jax.ShapeDtypeStruct((tokens, keys), jnp.bfloat16),
            jax.ShapeDtypeStruct((rows, columns), jnp.bfloat16),
        ),
        compiler_params=pltpu.CompilerParams(vmem_limit_bytes=16 * MIB),
        cost_estimate=pl.CostEstimate(
            flops=2 * rows * tokens * columns,
            bytes_accessed=10 * tokens * columns,
            transcendentals=0,
        ),
    )(own_part, peer_part, bias, cosines, sines, destination, live_rows)


def attend(scalars, queries, keys, kv, context=None):
    tokens = queries.shape[0]
    heads = keys.shape[1] // HEAD
    width = queries.shape[1] // (2 * heads)
    half_tokens = tokens // 2

    def kernel(scalar_ref, query_ref, key_ref, value_ref, *refs):
        context_ref, mask_ref = refs[-2:]
        live = scalar_ref[1]

        @pl.when(pl.program_id(0) == 0)
        def _():
            target = lax.broadcasted_iota(jnp.int32, (tokens, tokens), 0)
            source = lax.broadcasted_iota(jnp.int32, (tokens, tokens), 1)

            def segment(token):
                return jnp.where(token >= scalar_ref[2], 1, 0) + jnp.where(
                    token >= scalar_ref[3], 1, 0
                )

            near = (segment(source) == segment(target)) | (segment(source) == 0)
            allowed = ((source <= target) & (source < live) & near) | (source == target)
            mask_ref[...] = jnp.where(allowed, 0.0, MASKED)

        scale = HEAD**-0.5 * math.log2(math.e)
        key = key_ref[...]
        value = value_ref[...]
        for start, reach in ((0, half_tokens), (half_tokens, tokens)):
            rows = slice(start, start + half_tokens)
            mask = mask_ref[rows, :reach]
            is_live = (
                lax.broadcasted_iota(jnp.int32, (half_tokens, HEAD), 0) + start < live
            )
            for head in range(width // HEAD):
                lanes = slice(head * HEAD, (head + 1) * HEAD)
                scores = lax.dot_general(
                    query_ref[rows, lanes],
                    key[:reach],
                    (((1,), (1,)), ((), ())),
                    preferred_element_type=jnp.float32,
                )
                scores = scores * scale + mask
                weights = jnp.exp2(scores - jnp.max(scores, axis=1, keepdims=True))
                inverse = 1.0 / jnp.sum(weights, axis=1, keepdims=True)
                weights = (weights * inverse).astype(jnp.bfloat16)
                mixed = jnp.dot(weights, value[:reach], preferred_element_type=jnp.float32)
                context_ref[rows, lanes] = jnp.where(is_live, mixed, 0.0).astype(jnp.bfloat16)

    wide = pl.BlockSpec((tokens, width), lambda i, s: (0, s[0] * heads + i))
    in_specs = [
        wide,
        pl.BlockSpec((tokens, HEAD), lambda i, s: (0, i)),
        pl.BlockSpec((tokens, HEAD), lambda i, s: (0, heads + i)),
    ]
    arguments = [scalars, queries, keys, kv]
    if context is not None:
        in_specs.append(pl.BlockSpec(memory_space=pl.ANY))
        arguments.append(context)
    return pl.pallas_call(
        kernel,
        out_shape=jax.ShapeDtypeStruct(queries.shape, jnp.bfloat16),
        grid_spec=pltpu.PrefetchScalarGridSpec(
            num_scalar_prefetch=1,
            grid=(heads,),
            in_specs=in_specs,
            out_specs=wide,
            scratch_shapes=[pltpu.VMEM((tokens, tokens), jnp.float32)],
        ),
        input_output_aliases={} if context is None else {4: 0},
        compiler_params=pltpu.CompilerParams(vmem_limit_bytes=16 * MIB),
        cost_estimate=pl.CostEstimate(
            flops=4 * tokens * tokens * heads * width,
            bytes_accessed=4 * tokens * heads * width,
            transcendentals=tokens * tokens * heads * width // HEAD,
        ),
    )(*arguments)


def place(half, kept_count, keep_rows, mine, other, mine_spans, other_spans):
    rows = WORK * SPAN
    slots, columns = mine_spans.shape
    part = columns // 2

    def kernel(half_ref, kept_ref, keep_ref, mine_ref, other_ref, mine_in, other_in, out_ref):
        present = jnp.where(other_in[:, :HEAD].astype(jnp.float32) > 0.5 * ABSENT, 0.0, 1.0)
        row = lax.broadcasted_iota(jnp.int32, (slots, slots), 0)
        column = lax.broadcasted_iota(jnp.int32, (slots, slots), 1)
        before = (column // SPAN < row // SPAN) & (column % SPAN == 0)
        before = jnp.where(before, 1.0, 0.0).astype(jnp.bfloat16)
        earlier = jnp.dot(
            before, present.astype(jnp.bfloat16), preferred_element_type=jnp.float32
        )
        rank = earlier[:, :1].astype(jnp.int32) + kept_ref[0]
        work = lax.broadcasted_iota(jnp.int32, (slots, rows), 1)
        sender = lax.broadcasted_iota(jnp.int32, (slots, rows), 0)
        hit = (work // SPAN == rank) & (work % SPAN == sender % SPAN) & (present[:, :1] > 0.5)
        hit = jnp.where(hit, 1.0, 0.0).astype(jnp.bfloat16)
        keep = keep_ref[...] > 0.5
        own = half_ref[0]
        for home, spans, which in ((mine_ref, mine_in, own), (other_ref, other_in, 1 - own)):
            moved = lax.dot_general(
                hit, spans[...], (((0,), (0,)), ((), ())), preferred_element_type=jnp.float32
            )
            total = jnp.where(keep, home[...].astype(jnp.float32), moved).astype(jnp.bfloat16)
            out_ref[:, pl.ds(pl.multiple_of(which * part, HEAD), part)] = total[:, :part]
            out_ref[:, pl.ds(pl.multiple_of((2 + which) * part, HEAD), part)] = total[:, part:]

    inside = pl.BlockSpec(memory_space=pltpu.VMEM)
    scalar = pl.BlockSpec(memory_space=pltpu.SMEM)
    home_rows = pl.BlockSpec((rows, columns), lambda i: (0, 0))
    whole = pl.BlockSpec((slots, columns), lambda i: (0, 0))
    return pl.pallas_call(
        kernel,
        grid=(1,),
        out_shape=jax.ShapeDtypeStruct((rows, 2 * columns), jnp.bfloat16),
        in_specs=[
            scalar,
            scalar,
            pl.BlockSpec((rows, 1), lambda i: (0, 0)),
            home_rows,
            home_rows,
            whole,
            whole,
        ],
        out_specs=pl.BlockSpec((rows, 2 * columns), lambda i: (0, 0)),
        compiler_params=pltpu.CompilerParams(vmem_limit_bytes=16 * MIB),
        cost_estimate=pl.CostEstimate(
            flops=4 * rows * slots * columns,
            bytes_accessed=8 * rows * columns,
            transcendentals=0,
        ),
    )(half, kept_count, keep_rows, mine, other, mine_spans, other_spans)


def per_device(states, queries, kv_weight, kv_bias, lengths, bounds, balance):
    replicas = lax.axis_size("dp")
    own_index = lax.axis_index("dp")
    half = lax.axis_index("group") % 2
    core = own_index % 2
    own_y = own_index // 2 % 2
    own_z = own_index // 4
    ring = replicas // 4
    position = jnp.where(own_z % 2 == 0, own_z // 2, ring - 1 - own_z // 2)
    tokens = states.shape[0]
    width = kv_weight.shape[1]
    quarter = width // 4

    def columns_of(array, which):
        parts = [
            lax.dynamic_slice_in_dim(array, (2 * j + which) * quarter, quarter, array.ndim - 1)
            for j in range(2)
        ]
        return jnp.concatenate(parts, axis=-1)

    def block(offset, across):
        z = ring_place(ring, (position - offset + ring) % ring)
        y = own_y if not across else 1 - own_y
        return ((z * 2 + y) * 2 + core).astype(jnp.int32)

    links = Links(replicas, lax.axis_size("group"))
    mine_weight = columns_of(kv_weight, half)
    other_weight = columns_of(kv_weight, 1 - half)
    peer_states = core_swap(states, replicas)
    fore = ring // 2
    order = [k for j in range(1, ring) for k in (j, -j)][: ring - 1]
    held = {0: mine_weight}
    mine = [(mine_weight, block(0, False))]
    other = [(other_weight, block(0, False))]
    late = []
    across = links.send(mine_weight, "y")
    mine.append((across, block(0, True)))
    for k in order:
        held[k] = links.send(held[k - 1], "fore") if k > 0 else links.send(held[k + 1], "back")
        mine.append((held[k], block(k, False)))
        across = links.send(held[k], "y")
        mine.append((across, block(k, True)))
        if 1 <= k < fore:
            other.append((links.send(held[k], "x"), block(k, False)))
        piece = (links.send(across, "x"), block(k, True))
        (late if k == order[-1] else other).append(piece)
    moving = other_weight
    for j in range(1, ring - fore + 1):
        moving = links.send(moving, "back")
        (late if j == ring - fore else other).append((moving, block(-j, False)))
    late.append((links.send(other_weight, "y"), block(0, True)))

    def project(pieces, start=None):
        blocks = jnp.stack([b for _, b in pieces])
        return multiply(states, peer_states, [p for p, _ in pieces], blocks, start)

    mine_own, mine_peer = project(mine[-1:], project(mine[:-1]))
    other_own, other_peer = project(late, project(other))

    token_ids = jnp.arange(tokens, dtype=jnp.int32)
    live_tokens = lengths[0] * SPAN
    is_live = token_ids < live_tokens
    owner = jnp.repeat(balance[0], SPAN)
    is_moved = is_live & (owner != own_index)
    destination = jnp.where(is_moved, owner, -1)[None, :]
    live_rows = is_live.astype(jnp.float32)[:, None]
    keep = is_live & jnp.logical_not(is_moved)
    keep_rows = keep.astype(jnp.float32)[:, None]
    kept_count = (jnp.sum(keep.astype(jnp.int32)) // SPAN)[None]
    chosen, rejected = bounds[0, 0], bounds[0, 1]
    place_ids = jnp.where(token_ids >= rejected, token_ids - (rejected - chosen), token_ids)
    frequency = jnp.exp(
        jnp.arange(HEAD // 2, dtype=jnp.float32) * (-2.0 * math.log(1000000.0) / HEAD)
    )
    angles = place_ids.astype(jnp.float32)[:, None] * frequency[None, :]
    cosines, sines = jnp.cos(angles), jnp.sin(angles)
    cosines = jnp.concatenate([cosines, cosines], axis=1)
    sines = jnp.concatenate([-sines, sines], axis=1)

    def complete(own_part, peer_part, which):
        return finish(
            own_part,
            core_swap(peer_part, replicas),
            columns_of(kv_bias, which)[None, :],
            cosines,
            sines,
            destination,
            live_rows,
            replicas,
        )

    def exchange(spans):
        spans = spans.reshape(replicas, SPAN, width // 2)
        spans = lax.all_to_all(spans, "dp", split_axis=0, concat_axis=0, tiled=True)
        return spans.reshape(replicas * SPAN, width // 2)

    def scalars(which):
        return jnp.stack([which, live_tokens, chosen, rejected]).astype(jnp.int32)

    mine_kv, mine_keys, mine_spans = complete(mine_own, mine_peer, half)
    other_kv, other_keys, other_spans = complete(other_own, other_peer, 1 - half)
    mine_spans = exchange(mine_spans)
    other_spans = exchange(other_spans)
    context = attend(scalars(half), queries, mine_keys, mine_kv)
    context = attend(scalars(1 - half), queries, other_keys, other_kv, context)
    work_rows = place(
        half[None].astype(jnp.int32),
        kept_count,
        keep_rows,
        mine_kv,
        other_kv,
        mine_spans,
        other_spans,
    )
    return (context, work_rows)


def solution(mesh):
    in_specs = (
        P(("group", "dp"), None),
        P(("group", "dp"), None),
        P("dp", None),
        P(),
        P(("group", "dp")),
        P(("group", "dp"), None),
        P(("group", "dp"), None),
    )
    out_specs = (P(("group", "dp"), None), P(("group", "dp"), None))
    return jax.shard_map(
        per_device, mesh=mesh, in_specs=in_specs, out_specs=out_specs, check_vma=False
    )
```

```python
import math

import jax
import jax.numpy as jnp
from jax import lax
from jax.experimental import pallas as pl
from jax.experimental.pallas import tpu as pltpu
from jax.sharding import PartitionSpec as P

HEAD = 128
SPAN = 8
HOME = 32
WORK = 24
ABSENT = 1e30
MASKED = -1e30
MIB = 1 << 20


def ring_place(ring, position):
    return jnp.where(2 * position < ring, 2 * position, 2 * (ring - 1 - position) + 1)


def after(value, *before):
    return lax.optimization_barrier((value, *before))[0] if before else value


class Links:
    def __init__(self, replicas, groups):
        ring = replicas // 4
        places = [p for p in range(0, ring, 2)] + [p for p in range(1, ring, 2)][::-1]
        ahead = {places[i]: places[(i + 1) % ring] for i in range(ring)}
        steps = [
            ((z * 2 + y) * 2 + c, (ahead[z] * 2 + y) * 2 + c)
            for z in range(ring)
            for y in range(2)
            for c in range(2)
        ]
        self.routes = {
            "fore": ("z", "dp", steps),
            "back": ("z", "dp", [(d, s) for s, d in steps]),
            "y": ("y", "dp", [(i, i ^ 2) for i in range(replicas)]),
            "x": ("x", "group", [(i, i ^ 1) for i in range(groups)]),
        }
        self.last = {}

    def send(self, value, route, before=()):
        link, axis, pairs = self.routes[route]
        if link in self.last:
            before = (self.last[link], *before)
        self.last[link] = lax.ppermute(after(value, *before), axis, pairs)
        return self.last[link]


def core_swap(value, replicas):
    return lax.ppermute(value, "dp", [(i, i ^ 1) for i in range(replicas)])


def halves(weight, half):
    depth, width = weight.shape
    quarter = width // 4

    def kernel(half_ref, weight_ref, mine_ref, other_ref, sems):
        copies = []
        for i, out in enumerate((mine_ref, other_ref)):
            which = half_ref[0] if i == 0 else 1 - half_ref[0]
            for j in range(2):
                start = pl.multiple_of((2 * j + which) * quarter, HEAD)
                copies.append(
                    pltpu.make_async_copy(
                        weight_ref.at[:, pl.ds(start, quarter)],
                        out.at[:, pl.ds(j * quarter, quarter)],
                        sems.at[2 * i + j],
                    )
                )
        for copy in copies:
            copy.start()
        for copy in copies:
            copy.wait()

    anywhere = pl.BlockSpec(memory_space=pl.ANY)
    out = jax.ShapeDtypeStruct((depth, width // 2), weight.dtype)
    return pl.pallas_call(
        kernel,
        out_shape=(out, out),
        in_specs=[pl.BlockSpec(memory_space=pltpu.SMEM), anywhere],
        out_specs=(anywhere, anywhere),
        scratch_shapes=[pltpu.SemaphoreType.DMA((4,))],
        cost_estimate=pl.CostEstimate(
            flops=0, bytes_accessed=4 * depth * width, transcendentals=0
        ),
    )(half, weight)


def core_columns(states, core, depth):
    tokens, width = states.shape
    count = width // (2 * depth)

    def kernel(core_ref, states_ref, out_ref, sems):
        copies = []
        for i in range(count):
            start = pl.multiple_of((2 * i + core_ref[0]) * depth, HEAD)
            copies.append(
                pltpu.make_async_copy(
                    states_ref.at[:, pl.ds(start, depth)],
                    out_ref.at[:, pl.ds(i * depth, depth)],
                    sems.at[i],
                )
            )
        for copy in copies:
            copy.start()
        for copy in copies:
            copy.wait()

    anywhere = pl.BlockSpec(memory_space=pl.ANY)
    return pl.pallas_call(
        kernel,
        out_shape=jax.ShapeDtypeStruct((tokens, width // 2), states.dtype),
        in_specs=[pl.BlockSpec(memory_space=pltpu.SMEM), anywhere],
        out_specs=anywhere,
        scratch_shapes=[pltpu.SemaphoreType.DMA((count,))],
        cost_estimate=pl.CostEstimate(
            flops=0, bytes_accessed=2 * tokens * width, transcendentals=0
        ),
    )(core, states)


def multiply(own_states, peer_states, core, pieces, blocks, start=None):
    count = len(pieces)
    depth, columns = pieces[0].shape
    tokens = own_states.shape[0]
    batch = 4

    def kernel(core_ref, block_ref, own_ref, peer_ref, *refs):
        piece_refs = refs[:count]
        refs = refs[count:]
        if start is not None:
            start_refs, refs = refs[:2], refs[2:]
        own_out, peer_out, left, right, sems = refs
        copies = []
        for i in range(count):
            own_at = pl.multiple_of((2 * block_ref[i] + core_ref[0]) * depth, HEAD)
            peer_at = pl.multiple_of(block_ref[i] * depth, HEAD)
            deep = pl.ds(i * depth, depth)
            copies += [
                pltpu.make_async_copy(piece_refs[i], right.at[deep], sems.at[3 * i]),
                pltpu.make_async_copy(
                    own_ref.at[:, pl.ds(own_at, depth)],
                    left.at[pl.ds(0, tokens), deep],
                    sems.at[3 * i + 1],
                ),
                pltpu.make_async_copy(
                    peer_ref.at[:, pl.ds(peer_at, depth)],
                    left.at[pl.ds(tokens, tokens), deep],
                    sems.at[3 * i + 2],
                ),
            ]
        for copy in copies:
            copy.start()
        for i in range(0, count, batch):
            stop = min(i + batch, count)
            for copy in copies[3 * i : 3 * stop]:
                copy.wait()
            deep = slice(i * depth, stop * depth)
            for j, out in enumerate((own_out, peer_out)):
                part = jnp.dot(
                    left[j * tokens : (j + 1) * tokens, deep],
                    right[deep],
                    preferred_element_type=jnp.float32,
                )
                if i > 0:
                    out[...] += part
                elif start is None:
                    out[...] = part
                else:
                    out[...] = start_refs[j][...] + part

    anywhere = pl.BlockSpec(memory_space=pl.ANY)
    inside = pl.BlockSpec(memory_space=pltpu.VMEM)
    scalar = pl.BlockSpec(memory_space=pltpu.SMEM)
    total = jax.ShapeDtypeStruct((tokens, columns), jnp.float32)
    return pl.pallas_call(
        kernel,
        out_shape=(total, total),
        in_specs=[scalar, scalar]
        + [anywhere] * (2 + count)
        + [inside] * (0 if start is None else 2),
        out_specs=(inside, inside),
        scratch_shapes=[
            pltpu.VMEM((2 * tokens, count * depth), jnp.bfloat16),
            pltpu.VMEM((count * depth, columns), jnp.bfloat16),
            pltpu.SemaphoreType.DMA((3 * count,)),
        ],
        compiler_params=pltpu.CompilerParams(vmem_limit_bytes=48 * MIB),
        cost_estimate=pl.CostEstimate(
            flops=4 * count * tokens * depth * columns,
            bytes_accessed=count * (4 * tokens * depth + 2 * depth * columns),
            transcendentals=0,
        ),
    )(core, blocks, own_states, peer_states, *pieces, *(() if start is None else start))


def finish(own_part, peer_part, bias, cosines, sines, destination, live_rows, replicas):
    tokens, columns = own_part.shape
    keys = columns // 2
    rows = replicas * SPAN

    def kernel(own_ref, peer_ref, bias_ref, cos_ref, sin_ref, dest_ref, live_ref, kv_ref, key_ref, out_ref):
        kv = (own_ref[...] + peer_ref[...] + bias_ref[...]).astype(jnp.bfloat16)
        kv = jnp.where(live_ref[...] > 0.5, kv.astype(jnp.float32), 0.0)
        kept = kv.astype(jnp.bfloat16)
        kv_ref[...] = kept
        row = lax.broadcasted_iota(jnp.int32, (rows, tokens), 0)
        token = lax.broadcasted_iota(jnp.int32, (rows, tokens), 1)
        match = (dest_ref[...] == row // SPAN) & (token % SPAN == row % SPAN)
        pick = jnp.where(match, 1.0, 0.0)
        found = jnp.sum(pick, axis=1, keepdims=True)
        spans = jnp.dot(pick.astype(jnp.bfloat16), kept, preferred_element_type=jnp.float32)
        out_ref[...] = jnp.where(found > 0.5, spans, ABSENT).astype(jnp.bfloat16)
        cosine = jnp.concatenate([cos_ref[...], cos_ref[...]], axis=1)
        sine = jnp.concatenate([-sin_ref[...], sin_ref[...]], axis=1)
        for head in range(keys // HEAD):
            part = kv[:, head * HEAD : (head + 1) * HEAD]
            turned = part * cosine + pltpu.roll(part, HEAD // 2, 1) * sine
            key_ref[:, head * HEAD : (head + 1) * HEAD] = turned.astype(jnp.bfloat16)

    return pl.pallas_call(
        kernel,
        out_shape=(
            jax.ShapeDtypeStruct((tokens, columns), jnp.bfloat16),
            jax.ShapeDtypeStruct((tokens, keys), jnp.bfloat16),
            jax.ShapeDtypeStruct((rows, columns), jnp.bfloat16),
        ),
        compiler_params=pltpu.CompilerParams(vmem_limit_bytes=16 * MIB),
        cost_estimate=pl.CostEstimate(
            flops=2 * rows * tokens * columns,
            bytes_accessed=10 * tokens * columns,
            transcendentals=0,
        ),
    )(own_part, peer_part, bias, cosines, sines, destination, live_rows)


def attend(half, flip, mask, live_rows, queries, keys, kv, context=None):
    tokens = queries.shape[0]
    heads = keys.shape[1] // HEAD
    width = queries.shape[1] // (2 * heads)

    def kernel(half_ref, mask_ref, live_ref, query_ref, key_ref, value_ref, *refs):
        context_ref = refs[-1]
        scale = HEAD**-0.5 * math.log2(math.e)
        lanes = [slice(h * HEAD, (h + 1) * HEAD) for h in range(width // HEAD)]
        scores = [
            lax.dot_general(
                query_ref[:, lane],
                key_ref[...],
                (((1,), (1,)), ((), ())),
                preferred_element_type=jnp.float32,
            )
            for lane in lanes
        ]
        weights = []
        for score in scores:
            score = score * scale + mask_ref[...]
            weight = jnp.exp2(score - jnp.max(score, axis=1, keepdims=True))
            inverse = 1.0 / jnp.sum(weight, axis=1, keepdims=True)
            weights.append((weight * inverse).astype(jnp.bfloat16))
        is_live = live_ref[...] > 0.5
        for lane, weight in zip(lanes, weights):
            mixed = jnp.dot(weight, value_ref[...], preferred_element_type=jnp.float32)
            context_ref[:, lane] = jnp.where(is_live, mixed, 0.0).astype(jnp.bfloat16)

    def wide_at(i, s):
        return (0, (1 - s[0] if flip else s[0]) * heads + i)

    in_specs = [
        pl.BlockSpec((tokens, tokens), lambda i, s: (0, 0)),
        pl.BlockSpec((tokens, 1), lambda i, s: (0, 0)),
        pl.BlockSpec((tokens, width), wide_at),
        pl.BlockSpec((tokens, HEAD), lambda i, s: (0, i)),
        pl.BlockSpec((tokens, HEAD), lambda i, s: (0, heads + i)),
    ]
    arguments = [half, mask, live_rows, queries, keys, kv]
    if context is not None:
        in_specs.append(pl.BlockSpec(memory_space=pl.ANY))
        arguments.append(context)
    return pl.pallas_call(
        kernel,
        out_shape=jax.ShapeDtypeStruct(queries.shape, jnp.bfloat16),
        grid_spec=pltpu.PrefetchScalarGridSpec(
            num_scalar_prefetch=1,
            grid=(heads,),
            in_specs=in_specs,
            out_specs=pl.BlockSpec((tokens, width), wide_at),
        ),
        input_output_aliases={} if context is None else {6: 0},
        compiler_params=pltpu.CompilerParams(vmem_limit_bytes=32 * MIB),
        cost_estimate=pl.CostEstimate(
            flops=4 * tokens * tokens * heads * width,
            bytes_accessed=4 * tokens * heads * width,
            transcendentals=tokens * tokens * heads * width // HEAD,
        ),
    )(*arguments)


def place(half, kept_count, keep_rows, mine, other, mine_spans, other_spans):
    rows = WORK * SPAN
    slots, columns = mine_spans.shape
    part = columns // 2

    def kernel(half_ref, kept_ref, keep_ref, mine_ref, other_ref, mine_in, other_in, out_ref):
        present = jnp.where(other_in[:, :HEAD].astype(jnp.float32) > 0.5 * ABSENT, 0.0, 1.0)
        row = lax.broadcasted_iota(jnp.int32, (slots, slots), 0)
        column = lax.broadcasted_iota(jnp.int32, (slots, slots), 1)
        before = (column // SPAN < row // SPAN) & (column % SPAN == 0)
        before = jnp.where(before, 1.0, 0.0).astype(jnp.bfloat16)
        earlier = jnp.dot(
            before, present.astype(jnp.bfloat16), preferred_element_type=jnp.float32
        )
        rank = earlier[:, :1].astype(jnp.int32) + kept_ref[0]
        work = lax.broadcasted_iota(jnp.int32, (slots, rows), 1)
        sender = lax.broadcasted_iota(jnp.int32, (slots, rows), 0)
        hit = (work // SPAN == rank) & (work % SPAN == sender % SPAN) & (present[:, :1] > 0.5)
        hit = jnp.where(hit, 1.0, 0.0).astype(jnp.bfloat16)
        keep = keep_ref[...] > 0.5
        own = half_ref[0]
        for home, spans, which in ((mine_ref, mine_in, own), (other_ref, other_in, 1 - own)):
            moved = lax.dot_general(
                hit, spans[...], (((0,), (0,)), ((), ())), preferred_element_type=jnp.float32
            )
            total = jnp.where(keep, home[...].astype(jnp.float32), moved).astype(jnp.bfloat16)
            out_ref[:, pl.ds(pl.multiple_of(which * part, HEAD), part)] = total[:, :part]
            out_ref[:, pl.ds(pl.multiple_of((2 + which) * part, HEAD), part)] = total[:, part:]

    inside = pl.BlockSpec(memory_space=pltpu.VMEM)
    scalar = pl.BlockSpec(memory_space=pltpu.SMEM)
    home_rows = pl.BlockSpec((rows, columns), lambda i: (0, 0))
    whole = pl.BlockSpec((slots, columns), lambda i: (0, 0))
    return pl.pallas_call(
        kernel,
        grid=(1,),
        out_shape=jax.ShapeDtypeStruct((rows, 2 * columns), jnp.bfloat16),
        in_specs=[
            scalar,
            scalar,
            pl.BlockSpec((rows, 1), lambda i: (0, 0)),
            home_rows,
            home_rows,
            whole,
            whole,
        ],
        out_specs=pl.BlockSpec((rows, 2 * columns), lambda i: (0, 0)),
        compiler_params=pltpu.CompilerParams(vmem_limit_bytes=16 * MIB),
        cost_estimate=pl.CostEstimate(
            flops=4 * rows * slots * columns,
            bytes_accessed=8 * rows * columns,
            transcendentals=0,
        ),
    )(half, kept_count, keep_rows, mine, other, mine_spans, other_spans)


def per_device(states, queries, kv_weight, kv_bias, lengths, bounds, balance):
    replicas = lax.axis_size("dp")
    own_index = lax.axis_index("dp")
    half = (lax.axis_index("group") % 2).astype(jnp.int32)[None]
    core = (own_index % 2).astype(jnp.int32)[None]
    own_y = own_index // 2 % 2
    own_z = own_index // 4
    ring = replicas // 4
    position = jnp.where(own_z % 2 == 0, own_z // 2, ring - 1 - own_z // 2)
    tokens = states.shape[0]
    depth, width = kv_weight.shape
    quarter = width // 4

    def block(offset, across):
        z = ring_place(ring, (position - offset + ring) % ring)
        return (z * 2 + (1 - own_y if across else own_y)).astype(jnp.int32)

    token_ids = jnp.arange(tokens, dtype=jnp.int32)
    is_live = token_ids < lengths[0] * SPAN
    owner = jnp.repeat(balance[0], SPAN)
    is_moved = is_live & (owner != own_index)
    destination = jnp.where(is_moved, owner, -1)[None, :]
    live_rows = is_live.astype(jnp.float32)[:, None]
    keep = is_live & jnp.logical_not(is_moved)
    keep_rows = keep.astype(jnp.float32)[:, None]
    kept_count = (jnp.sum(keep.astype(jnp.int32)) // SPAN)[None]
    chosen, rejected = bounds[0, 0], bounds[0, 1]
    segment = (token_ids >= chosen).astype(jnp.int32) + (token_ids >= rejected).astype(jnp.int32)
    place_ids = jnp.where(token_ids >= rejected, token_ids - (rejected - chosen), token_ids)
    target, source = token_ids[:, None], token_ids[None, :]
    near = (segment[None, :] == segment[:, None]) | (segment[None, :] == 0)
    allowed = ((source <= target) & is_live[None, :] & near) | (source == target)
    mask = jnp.where(allowed, 0.0, MASKED).astype(jnp.float32)
    frequency = jnp.exp(
        jnp.arange(HEAD // 2, dtype=jnp.float32) * (-2.0 * math.log(1000000.0) / HEAD)
    )
    angles = place_ids.astype(jnp.float32)[:, None] * frequency[None, :]
    cosines, sines = jnp.cos(angles), jnp.sin(angles)
    plan = (cosines, sines, destination, live_rows, keep_rows, kept_count, mask)

    links = Links(replicas, lax.axis_size("group"))
    mine_weight, other_weight = halves(kv_weight, half)
    peer_states = core_swap(core_columns(states, 1 - core, depth), replicas)

    def project(pieces, start=None):
        blocks = jnp.stack([b for _, b in pieces])
        return multiply(states, peer_states, core, [p for p, _ in pieces], blocks, start)

    fore = ring // 2
    order = [k for j in range(1, ring) for k in (j, -j)][: ring - 1]
    held = {0: mine_weight}
    mine = [(mine_weight, block(0, False))]
    other = [(other_weight, block(0, False))]
    middle, late = [], []
    crossed = links.send(mine_weight, "y")
    mine.append((crossed, block(0, True)))
    moving = other_weight
    for k in order:
        final = k == order[-1]
        nearer = held[k - 1] if k > 0 else held[k + 1]
        held[k] = links.send(nearer, "fore" if k > 0 else "back", plan if final else ())
        mine.append((held[k], block(k, False)))
        crossed = links.send(held[k], "y")
        if 1 <= k < fore:
            other.append((links.send(held[k], "x"), block(k, False)))
        if final:
            mine_part = project(mine)
            other_part = project(other)
            for j in range(1, ring - fore):
                moving = links.send(moving, "back")
                middle.append((moving, block(-j, False)))
            ready = (*mine_part, *other_part)
            moving = links.send(moving, "back", ready)
            late.append((moving, block(fore - ring, False)))
            late.append((links.send(other_weight, "y", ready), block(0, True)))
            late.append((links.send(crossed, "x", ready), block(k, True)))
            mine_own, mine_peer = project([(crossed, block(k, True))], mine_part)
        else:
            mine.append((crossed, block(k, True)))
            piece = (links.send(crossed, "x"), block(k, True))
            (middle if k == order[-2] else other).append(piece)

    def complete(own_part, peer_part, flip):
        which = 1 - half[0] if flip else half[0]
        bias = jnp.concatenate(
            [
                lax.dynamic_slice_in_dim(kv_bias, (2 * j + which) * quarter, quarter)
                for j in range(2)
            ]
        )
        peer_part = core_swap(peer_part, replicas)
        return finish(own_part, peer_part, bias[None, :], *plan[:4], replicas)

    def exchange(spans):
        spans = spans.reshape(replicas, SPAN, width // 2)
        spans = lax.all_to_all(spans, "dp", split_axis=0, concat_axis=0, tiled=True)
        return spans.reshape(replicas * SPAN, width // 2)

    mine_kv, mine_keys, mine_spans = complete(mine_own, mine_peer, False)
    mine_spans = exchange(mine_spans)
    other_part = project(middle, other_part)
    late = [(after(p, mine_kv, *other_part), b) for p, b in late]
    other_kv, other_keys, other_spans = complete(*project(late, other_part), True)
    other_spans = exchange(other_spans)
    context = attend(half, False, mask, live_rows, queries, mine_keys, mine_kv)
    context = attend(half, True, mask, live_rows, queries, other_keys, other_kv, context)
    work_rows = place(
        half, kept_count, keep_rows, mine_kv, other_kv, mine_spans, other_spans
    )
    return (context, work_rows)


def solution(mesh):
    in_specs = (
        P(("group", "dp"), None),
        P(("group", "dp"), None),
        P("dp", None),
        P(),
        P(("group", "dp")),
        P(("group", "dp"), None),
        P(("group", "dp"), None),
    )
    out_specs = (P(("group", "dp"), None), P(("group", "dp"), None))
    return jax.shard_map(
        per_device, mesh=mesh, in_specs=in_specs, out_specs=out_specs, check_vma=False
    )
```

```python
import math

import jax
import jax.numpy as jnp
from jax import lax
from jax.experimental import pallas as pl
from jax.experimental.pallas import tpu as pltpu
from jax.sharding import PartitionSpec as P

HEAD = 128
SPAN = 8
HOME = 32
WORK = 24
ABSENT = 1e30
MASKED = -1e30
LIMIT = 18 << 20
LIVE, DESTINATION, KEEP = HEAD, HEAD + 1, HEAD + 2


def ring_place(ring, position):
    return jnp.where(2 * position < ring, 2 * position, 2 * (ring - 1 - position) + 1)


def after(value, *before):
    return lax.optimization_barrier((value, *before))[0] if before else value


class Links:
    def __init__(self, replicas, groups):
        ring = replicas // 4
        places = [p for p in range(0, ring, 2)] + [p for p in range(1, ring, 2)][::-1]
        ahead = {places[i]: places[(i + 1) % ring] for i in range(ring)}
        steps = [
            ((z * 2 + y) * 2 + c, (ahead[z] * 2 + y) * 2 + c)
            for z in range(ring)
            for y in range(2)
            for c in range(2)
        ]
        self.routes = {
            "fore": ("z", "dp", steps),
            "back": ("z", "dp", [(d, s) for s, d in steps]),
            "y": ("y", "dp", [(i, i ^ 2) for i in range(replicas)]),
            "x": ("x", "group", [(i, i ^ 1) for i in range(groups)]),
        }
        self.last = {}

    def send(self, value, route, before=()):
        link, axis, pairs = self.routes[route]
        if link in self.last:
            before = (self.last[link], *before)
        self.last[link] = lax.ppermute(after(value, *before), axis, pairs)
        return self.last[link]


def core_swap(value, replicas):
    return lax.ppermute(value, "dp", [(i, i ^ 1) for i in range(replicas)])


def halves(weight, half):
    depth, width = weight.shape
    quarter = width // 4

    def kernel(half_ref, weight_ref, mine_ref, other_ref, sems):
        copies = []
        for i, out in enumerate((mine_ref, other_ref)):
            which = half_ref[0] if i == 0 else 1 - half_ref[0]
            for j in range(2):
                start = pl.multiple_of((2 * j + which) * quarter, HEAD)
                copies.append(
                    pltpu.make_async_copy(
                        weight_ref.at[:, pl.ds(start, quarter)],
                        out.at[:, pl.ds(j * quarter, quarter)],
                        sems.at[2 * i + j],
                    )
                )
        for copy in copies:
            copy.start()
        for copy in copies:
            copy.wait()

    anywhere = pl.BlockSpec(memory_space=pl.ANY)
    inside = pl.BlockSpec(memory_space=pltpu.VMEM)
    out = jax.ShapeDtypeStruct((depth, width // 2), weight.dtype)
    return pl.pallas_call(
        kernel,
        out_shape=(out, out),
        in_specs=[pl.BlockSpec(memory_space=pltpu.SMEM), anywhere],
        out_specs=(inside, inside),
        scratch_shapes=[pltpu.SemaphoreType.DMA((4,))],
        cost_estimate=pl.CostEstimate(
            flops=0, bytes_accessed=4 * depth * width, transcendentals=0
        ),
    )(half, weight)


def core_columns(states, core, depth):
    tokens, width = states.shape
    count = width // (2 * depth)

    def kernel(core_ref, states_ref, out_ref, sems):
        copies = []
        for i in range(count):
            start = pl.multiple_of((2 * i + core_ref[0]) * depth, HEAD)
            copies.append(
                pltpu.make_async_copy(
                    states_ref.at[:, pl.ds(start, depth)],
                    out_ref.at[:, pl.ds(i * depth, depth)],
                    sems.at[i],
                )
            )
        for copy in copies:
            copy.start()
        for copy in copies:
            copy.wait()

    anywhere = pl.BlockSpec(memory_space=pl.ANY)
    return pl.pallas_call(
        kernel,
        out_shape=jax.ShapeDtypeStruct((tokens, width // 2), states.dtype),
        in_specs=[pl.BlockSpec(memory_space=pltpu.SMEM), anywhere],
        out_specs=pl.BlockSpec(memory_space=pltpu.VMEM),
        scratch_shapes=[pltpu.SemaphoreType.DMA((count,))],
        cost_estimate=pl.CostEstimate(
            flops=0, bytes_accessed=2 * tokens * width, transcendentals=0
        ),
    )(core, states)


def accumulate(states, scalars, pieces, places, bias=None, start=None, later=0):
    count = len(pieces)
    depth, columns = pieces[0].shape
    tokens = states[0].shape[0]
    batch = 5
    begun = 4 if start is not None else 1

    def kernel(scalar_ref, *refs):
        state_refs, refs = refs[:2], refs[2:]
        piece_refs, refs = refs[:count], refs[count:]
        start_refs, refs = refs[:begun], refs[begun:]
        if later:
            totals, lefts, refs = refs[:4], refs[4:6], refs[6:]
        else:
            outs, totals, refs = refs[:4], refs[4:8], refs[8:]
        left, right, bias_ref, sems = refs
        used = 0

        def begin(source, target):
            nonlocal used
            copy = pltpu.make_async_copy(source, target, sems.at[used])
            copy.start()
            used += 1
            return copy

        def columns_at(side, index):
            at = scalar_ref[2 + index]
            at = 2 * at + scalar_ref[0] if side else at
            return state_refs[side].at[:, pl.ds(pl.multiple_of(at * depth, HEAD), depth)]

        waits = []
        if start is None:
            first = [begin(start_refs[0], bias_ref)]
        else:
            first = [begin(source, target) for source, target in zip(start_refs, totals)]
        for i in range(count):
            deep = pl.ds(i * depth, depth)
            waits.append(
                [begin(piece_refs[i], right.at[deep])]
                + [begin(columns_at(side, i), left.at[side, :, deep]) for side in range(2)]
            )
        rest = [
            begin(columns_at(side, count + i), lefts[side].at[:, pl.ds(i * depth, depth)])
            for i in range(later)
            for side in range(2)
        ]
        for copy in first:
            copy.wait()
        touched = [start is not None] * 4
        for i in range(0, count, batch):
            stop = min(i + batch, count)
            for copies in waits[i:stop]:
                for copy in copies:
                    copy.wait()
            for j in range(i, stop):
                deep = slice(j * depth, (j + 1) * depth)
                for side in range(2):
                    which = 2 * places[j] + side
                    part = jnp.dot(
                        left[side, :, deep], right[deep], preferred_element_type=jnp.float32
                    )
                    if touched[which]:
                        totals[which][...] += part
                    elif side == 0:
                        totals[which][...] = part
                    else:
                        own = scalar_ref[1] if places[j] == 0 else 1 - scalar_ref[1]
                        part_width = columns // 2
                        for k in range(2):
                            at = pl.multiple_of((2 * k + own) * part_width, HEAD)
                            lanes = slice(k * part_width, (k + 1) * part_width)
                            totals[which][:, lanes] = (
                                part[:, lanes] + bias_ref[:, pl.ds(at, part_width)]
                            )
                    touched[which] = True
        if not later:
            rest += [begin(source, target) for source, target in zip(totals, outs)]
        for copy in rest:
            copy.wait()

    outside = pl.BlockSpec(memory_space=pltpu.HBM)
    inside = pl.BlockSpec(memory_space=pltpu.VMEM)
    sums = (tokens, columns)
    if later:
        out_shape = [jax.ShapeDtypeStruct(sums, jnp.float32)] * 4
        out_shape += [jax.ShapeDtypeStruct((tokens, later * depth), jnp.bfloat16)] * 2
        out_specs, scratch = [inside] * 6, []
    else:
        out_shape = [pltpu.HBM(sums, jnp.float32)] * 4
        out_specs, scratch = [outside] * 4, [pltpu.VMEM(sums, jnp.float32)] * 4
    outer = [*states, *pieces, *((bias,) if start is None else start)]
    return pl.pallas_call(
        kernel,
        out_shape=out_shape,
        in_specs=[pl.BlockSpec(memory_space=pltpu.SMEM)] + [outside] * len(outer),
        out_specs=out_specs,
        scratch_shapes=scratch
        + [
            pltpu.VMEM((2, tokens, count * depth), jnp.bfloat16),
            pltpu.VMEM((count * depth, columns), jnp.bfloat16),
            pltpu.VMEM((1, 2 * columns), jnp.float32),
            pltpu.SemaphoreType.DMA((3 * count + 2 * later + 8,)),
        ],
        compiler_params=pltpu.CompilerParams(vmem_limit_bytes=LIMIT),
        cost_estimate=pl.CostEstimate(
            flops=4 * count * tokens * depth * columns,
            bytes_accessed=count * (4 * tokens * depth + 2 * depth * columns),
            transcendentals=0,
        ),
    )(scalars, *(pltpu.with_memory_space_constraint(a, pltpu.HBM) for a in outer))


def complete(left, pieces, total):
    depth = pieces[0].shape[0]

    def kernel(left_ref, total_ref, *refs):
        out_ref = refs[-1]
        for i, piece in enumerate(refs[:-1]):
            part = jnp.dot(
                left_ref[:, i * depth : (i + 1) * depth],
                piece[...],
                preferred_element_type=jnp.float32,
            )
            out_ref[...] = (total_ref if i == 0 else out_ref)[...] + part

    inside = pl.BlockSpec(memory_space=pltpu.VMEM)
    return pl.pallas_call(
        kernel,
        out_shape=jax.ShapeDtypeStruct(total.shape, total.dtype),
        in_specs=[inside] * (2 + len(pieces)),
        out_specs=inside,
        compiler_params=pltpu.CompilerParams(vmem_limit_bytes=LIMIT),
        cost_estimate=pl.CostEstimate(
            flops=2 * left.size * total.shape[1],
            bytes_accessed=2 * left.size,
            transcendentals=0,
        ),
    )(left, total, *pieces)


def finish(own_part, peer_part, table, replicas, earlier=None):
    tokens, columns = own_part.shape
    keys = columns // 2
    rows = replicas * SPAN

    def kernel(own_ref, peer_ref, table_in, *refs):
        kv_ref, key_ref, out_ref, table_ref, sem = refs[-5:]
        copy = pltpu.make_async_copy(table_in, table_ref, sem)
        copy.start()
        kv = (own_ref[...] + peer_ref[...]).astype(jnp.bfloat16).astype(jnp.float32)
        copy.wait()
        kv = jnp.where(table_ref[:, LIVE : LIVE + 1] > 0.5, kv, 0.0)
        kept = kv.astype(jnp.bfloat16)
        kv_ref[...] = kept
        destination = table_ref[:, DESTINATION : DESTINATION + 1].astype(jnp.int32)
        token = lax.broadcasted_iota(jnp.int32, (tokens, rows), 0)
        row = lax.broadcasted_iota(jnp.int32, (tokens, rows), 1)
        match = (destination == row // SPAN) & (token % SPAN == row % SPAN)
        pick = jnp.where(match, 1.0, 0.0).astype(jnp.bfloat16)
        over_tokens = (((0,), (0,)), ((), ()))
        found = lax.dot_general(
            pick,
            jnp.ones((tokens, HEAD), jnp.bfloat16),
            over_tokens,
            preferred_element_type=jnp.float32,
        )
        spans = lax.dot_general(pick, kept, over_tokens, preferred_element_type=jnp.float32)
        spans = jnp.where(found[:, :1] > 0.5, spans, ABSENT).astype(jnp.bfloat16)
        if earlier is None:
            out_ref[...] = spans
        else:
            out_ref[:, :columns] = refs[0][...]
            out_ref[:, columns:] = spans
        cosine, sine = table_ref[:, : HEAD // 2], table_ref[:, HEAD // 2 : HEAD]
        cosine = jnp.concatenate([cosine, cosine], axis=1)
        sine = jnp.concatenate([-sine, sine], axis=1)
        for head in range(keys // HEAD):
            part = kv[:, head * HEAD : (head + 1) * HEAD]
            turned = part * cosine + pltpu.roll(part, HEAD // 2, 1) * sine
            key_ref[:, head * HEAD : (head + 1) * HEAD] = turned.astype(jnp.bfloat16)

    inside = pl.BlockSpec(memory_space=pltpu.VMEM)
    sent = columns if earlier is None else 2 * columns
    more = () if earlier is None else (earlier,)
    return pl.pallas_call(
        kernel,
        out_shape=(
            jax.ShapeDtypeStruct((tokens, columns), jnp.bfloat16),
            jax.ShapeDtypeStruct((tokens, keys), jnp.bfloat16),
            jax.ShapeDtypeStruct((rows, sent), jnp.bfloat16),
        ),
        in_specs=[inside] * 2 + [pl.BlockSpec(memory_space=pltpu.HBM)] + [inside] * len(more),
        out_specs=(inside,) * 3,
        scratch_shapes=[pltpu.VMEM(table.shape, table.dtype), pltpu.SemaphoreType.DMA],
        compiler_params=pltpu.CompilerParams(vmem_limit_bytes=LIMIT),
        cost_estimate=pl.CostEstimate(
            flops=2 * rows * tokens * columns,
            bytes_accessed=10 * tokens * columns,
            transcendentals=0,
        ),
    )(own_part, peer_part, pltpu.with_memory_space_constraint(table, pltpu.HBM), *more)


def attend(half, flip, mask, table, queries, keys, kv, context=None):
    tokens = queries.shape[0]
    heads = keys.shape[1] // HEAD
    width = queries.shape[1] // (2 * heads)

    def kernel(half_ref, mask_ref, table_ref, query_ref, key_ref, value_ref, *refs):
        context_ref = refs[-1]
        scale = HEAD**-0.5 * math.log2(math.e)
        lanes = [slice(h * HEAD, (h + 1) * HEAD) for h in range(width // HEAD)]
        scores = [
            lax.dot_general(
                query_ref[:, lane],
                key_ref[...],
                (((1,), (1,)), ((), ())),
                preferred_element_type=jnp.float32,
            )
            for lane in lanes
        ]
        weights = []
        for score in scores:
            score = score * scale + mask_ref[...]
            weight = jnp.exp2(score - jnp.max(score, axis=1, keepdims=True))
            inverse = 1.0 / jnp.sum(weight, axis=1, keepdims=True)
            weights.append((weight * inverse).astype(jnp.bfloat16))
        is_live = table_ref[:, LIVE - HEAD : LIVE - HEAD + 1] > 0.5
        for lane, weight in zip(lanes, weights):
            mixed = jnp.dot(weight, value_ref[...], preferred_element_type=jnp.float32)
            context_ref[:, lane] = jnp.where(is_live, mixed, 0.0).astype(jnp.bfloat16)

    def wide_at(i, s):
        return (0, (1 - s[0] if flip else s[0]) * heads + i)

    in_specs = [
        pl.BlockSpec((tokens, tokens), lambda i, s: (0, 0)),
        pl.BlockSpec((tokens, HEAD), lambda i, s: (0, 1)),
        pl.BlockSpec((tokens, width), wide_at),
        pl.BlockSpec((tokens, HEAD), lambda i, s: (0, i)),
        pl.BlockSpec((tokens, HEAD), lambda i, s: (0, heads + i)),
    ]
    arguments = [half, mask, table, queries, keys, kv]
    if context is not None:
        in_specs.append(pl.BlockSpec(memory_space=pl.ANY))
        arguments.append(context)
    return pl.pallas_call(
        kernel,
        out_shape=jax.ShapeDtypeStruct(queries.shape, jnp.bfloat16),
        grid_spec=pltpu.PrefetchScalarGridSpec(
            num_scalar_prefetch=1,
            grid=(heads,),
            in_specs=in_specs,
            out_specs=pl.BlockSpec((tokens, width), wide_at),
        ),
        input_output_aliases={} if context is None else {6: 0},
        compiler_params=pltpu.CompilerParams(vmem_limit_bytes=LIMIT),
        cost_estimate=pl.CostEstimate(
            flops=4 * tokens * tokens * heads * width,
            bytes_accessed=4 * tokens * heads * width,
            transcendentals=tokens * tokens * heads * width // HEAD,
        ),
    )(*arguments)


def place(scalars, table, mine, other, spans):
    rows = WORK * SPAN
    slots, width = spans.shape
    part = width // 4

    def kernel(scalar_ref, table_ref, mine_ref, other_ref, spans_ref, out_ref, total_ref):
        @pl.when(pl.program_id(0) == 0)
        def _():
            present = spans_ref[:, :HEAD].astype(jnp.float32)
            present = jnp.where(present > 0.5 * ABSENT, 0.0, 1.0)
            row = lax.broadcasted_iota(jnp.int32, (slots, slots), 0)
            column = lax.broadcasted_iota(jnp.int32, (slots, slots), 1)
            before = (column // SPAN < row // SPAN) & (column % SPAN == 0)
            before = jnp.where(before, 1.0, 0.0).astype(jnp.bfloat16)
            earlier = jnp.dot(
                before, present.astype(jnp.bfloat16), preferred_element_type=jnp.float32
            )
            rank = earlier[:, :1].astype(jnp.int32) + scalar_ref[1]
            target = lax.broadcasted_iota(jnp.int32, (slots, rows), 1)
            sender = lax.broadcasted_iota(jnp.int32, (slots, rows), 0)
            hit = (target // SPAN == rank) & (target % SPAN == sender % SPAN)
            hit = jnp.where(hit & (present[:, :1] > 0.5), 1.0, 0.0).astype(jnp.bfloat16)
            moved = lax.dot_general(
                hit, spans_ref[...], (((0,), (0,)), ((), ())), preferred_element_type=jnp.float32
            ).astype(jnp.bfloat16)
            keep = table_ref[:, KEEP : KEEP + 1] > 0.5
            for i in range(4):
                home = (mine_ref, other_ref)[i // 2][:, (i % 2) * part : (i % 2 + 1) * part]
                home = home.astype(jnp.float32)
                came = moved[:, i * part : (i + 1) * part].astype(jnp.float32)
                total_ref[i] = jnp.where(keep, home, came).astype(jnp.bfloat16)

        out_ref[...] = total_ref[pl.program_id(0)]

    def out_at(i, s):
        return (0, 2 * (i % 2) + jnp.where(i < 2, s[0], 1 - s[0]))

    home = pl.BlockSpec((rows, width // 2), lambda i, s: (0, 0))
    return pl.pallas_call(
        kernel,
        out_shape=jax.ShapeDtypeStruct((rows, width), jnp.bfloat16),
        grid_spec=pltpu.PrefetchScalarGridSpec(
            num_scalar_prefetch=1,
            grid=(4,),
            in_specs=[
                pl.BlockSpec((rows, table.shape[1]), lambda i, s: (0, 0)),
                home,
                home,
                pl.BlockSpec((slots, width), lambda i, s: (0, 0)),
            ],
            out_specs=pl.BlockSpec((rows, part), out_at),
            scratch_shapes=[pltpu.VMEM((4, rows, part), jnp.bfloat16)],
        ),
        compiler_params=pltpu.CompilerParams(vmem_limit_bytes=LIMIT),
        cost_estimate=pl.CostEstimate(
            flops=2 * rows * slots * width,
            bytes_accessed=4 * rows * width,
            transcendentals=0,
        ),
    )(scalars, table, mine, other, spans)


def per_device(states, queries, kv_weight, kv_bias, lengths, bounds, balance):
    replicas = lax.axis_size("dp")
    own_index = lax.axis_index("dp")
    half = (lax.axis_index("group") % 2).astype(jnp.int32)[None]
    core = (own_index % 2).astype(jnp.int32)[None]
    own_y = own_index // 2 % 2
    own_z = own_index // 4
    ring = replicas // 4
    position = jnp.where(own_z % 2 == 0, own_z // 2, ring - 1 - own_z // 2)
    tokens = states.shape[0]
    depth, width = kv_weight.shape

    def block(offset, across):
        z = ring_place(ring, (position - offset + ring) % ring)
        return (z * 2 + (1 - own_y if across else own_y)).astype(jnp.int32)

    token_ids = jnp.arange(tokens, dtype=jnp.int32)
    is_live = token_ids < lengths[0] * SPAN
    owner = jnp.repeat(balance[0], SPAN)
    is_moved = is_live & (owner != own_index)
    destination = jnp.where(is_moved, owner, -1)
    keep = is_live & jnp.logical_not(is_moved)
    kept_count = jnp.sum(keep.astype(jnp.int32)) // SPAN
    chosen, rejected = bounds[0, 0], bounds[0, 1]
    segment = (token_ids >= chosen).astype(jnp.int32) + (token_ids >= rejected).astype(jnp.int32)
    place_ids = jnp.where(token_ids >= rejected, token_ids - (rejected - chosen), token_ids)
    target, source = token_ids[:, None], token_ids[None, :]
    near = (segment[None, :] == segment[:, None]) | (segment[None, :] == 0)
    allowed = ((source <= target) & is_live[None, :] & near) | (source == target)
    mask = jnp.where(allowed, 0.0, MASKED).astype(jnp.float32)
    frequency = jnp.exp(
        jnp.arange(HEAD // 2, dtype=jnp.float32) * (-2.0 * math.log(1000000.0) / HEAD)
    )
    angles = place_ids.astype(jnp.float32)[:, None] * frequency[None, :]
    columns = [jnp.cos(angles), jnp.sin(angles)]
    columns += [c.astype(jnp.float32)[:, None] for c in (is_live, destination, keep)]
    columns.append(jnp.zeros((tokens, HEAD - 3), jnp.float32))
    table = jnp.concatenate(columns, axis=1)
    scalars = jnp.stack([half[0], kept_count])
    plan = (table, mask, scalars)

    links = Links(replicas, lax.axis_size("group"))
    mine_weight, other_weight = halves(kv_weight, half)
    peer_states = core_swap(core_columns(states, 1 - core, depth), replicas)

    both = (peer_states, states)

    def listed(pieces):
        return jnp.stack([core[0], half[0]] + [b for _, b in pieces])

    fore = ring // 2
    order = [k for j in range(1, ring) for k in (j, -j)][: ring - 1]
    held = {0: mine_weight}
    mine = [(mine_weight, block(0, False))]
    other = [(other_weight, block(0, False))]
    middle, late = [], []
    crossed = links.send(mine_weight, "y")
    mine.append((crossed, block(0, True)))
    moving = other_weight
    for k in order:
        final = k == order[-1]
        nearer = held[k - 1] if k > 0 else held[k + 1]
        held[k] = links.send(nearer, "fore" if k > 0 else "back", plan if final else ())
        mine.append((held[k], block(k, False)))
        crossed = links.send(held[k], "y")
        if 1 <= k < fore:
            other.append((links.send(held[k], "x"), block(k, False)))
        if final:
            early = mine + other
            sums = accumulate(
                both,
                listed(early),
                [p for p, _ in early],
                [0] * len(mine) + [1] * len(other),
                bias=kv_bias[None, :],
            )
            for j in range(1, ring - fore):
                moving = links.send(moving, "back")
                middle.append((moving, block(-j, False)))
            moving = links.send(moving, "back", sums)
            late.append((moving, block(fore - ring, False)))
            late.append((links.send(other_weight, "y", sums), block(0, True)))
            late.append((links.send(crossed, "x", sums), block(k, True)))
            middle = [(crossed, block(k, True))] + middle
            mine_peer, mine_own, other_peer, other_own, left_peer, left_own = accumulate(
                both,
                listed(middle + late),
                [p for p, _ in middle],
                [0] + [1] * (len(middle) - 1),
                start=sums,
                later=len(late),
            )
        else:
            mine.append((crossed, block(k, True)))
            piece = (links.send(crossed, "x"), block(k, True))
            (middle if k == order[-2] else other).append(piece)

    mine_peer = core_swap(mine_peer, replicas)
    mine_kv, mine_keys, mine_spans = finish(mine_own, mine_peer, table, replicas)
    last = [p for p, _ in late]
    other_peer = core_swap(complete(left_peer, last, other_peer), replicas)
    other_own = complete(left_own, last, other_own)
    other_kv, other_keys, spans = finish(other_own, other_peer, table, replicas, mine_spans)
    spans = spans.reshape(replicas, SPAN, width)
    spans = lax.all_to_all(spans, "dp", split_axis=0, concat_axis=0, tiled=True)
    spans = spans.reshape(replicas * SPAN, width)
    context = attend(half, False, mask, table, queries, mine_keys, mine_kv)
    context = attend(half, True, mask, table, queries, other_keys, other_kv, context)
    work_rows = place(scalars, table, mine_kv, other_kv, spans)
    return (context, work_rows)


def solution(mesh):
    in_specs = (
        P(("group", "dp"), None),
        P(("group", "dp"), None),
        P("dp", None),
        P(),
        P(("group", "dp")),
        P(("group", "dp"), None),
        P(("group", "dp"), None),
    )
    out_specs = (P(("group", "dp"), None), P(("group", "dp"), None))
    return jax.shard_map(
        per_device, mesh=mesh, in_specs=in_specs, out_specs=out_specs, check_vma=False
    )
```

```python
import math

import jax
import jax.numpy as jnp
from jax import lax
from jax.experimental import pallas as pl
from jax.experimental.pallas import tpu as pltpu
from jax.sharding import PartitionSpec as P

HEAD = 128
SPAN = 8
HOME = 32
WORK = 24
ABSENT = 1e30
MASKED = -1e30
LIMIT = 18 << 20
LAG = {"x": 1, "y": 2, "z": 1}
LIVE, DESTINATION, KEEP = HEAD, HEAD + 1, HEAD + 2


def ring_place(ring, position):
    return jnp.where(2 * position < ring, 2 * position, 2 * (ring - 1 - position) + 1)


def after(value, *before):
    return lax.optimization_barrier((value, *before))[0] if before else value


class Links:
    def __init__(self, replicas, groups):
        ring = replicas // 4
        places = [p for p in range(0, ring, 2)] + [p for p in range(1, ring, 2)][::-1]
        ahead = {places[i]: places[(i + 1) % ring] for i in range(ring)}
        steps = [
            ((z * 2 + y) * 2 + c, (ahead[z] * 2 + y) * 2 + c)
            for z in range(ring)
            for y in range(2)
            for c in range(2)
        ]
        self.routes = {
            "fore": ("z", "dp", steps),
            "back": ("z", "dp", [(d, s) for s, d in steps]),
            "y": ("y", "dp", [(i, i ^ 2) for i in range(replicas)]),
            "x": ("x", "group", [(i, i ^ 1) for i in range(groups)]),
        }
        self.sent = {"x": [], "y": [], "z": []}

    def send(self, value, route, before=(), lag=None):
        link, axis, pairs = self.routes[route]
        sent = self.sent[link]
        lag = LAG[link] if lag is None else lag
        if len(sent) >= lag:
            before = (sent[-lag], *before)
        sent.append(lax.ppermute(after(value, *before), axis, pairs))
        return sent[-1]


def core_swap(value, replicas):
    return lax.ppermute(value, "dp", [(i, i ^ 1) for i in range(replicas)])


def halves(weight, half):
    depth, width = weight.shape
    quarter = width // 4

    def kernel(half_ref, weight_ref, mine_ref, other_ref, sems):
        copies = []
        for i, out in enumerate((mine_ref, other_ref)):
            which = half_ref[0] if i == 0 else 1 - half_ref[0]
            for j in range(2):
                start = pl.multiple_of((2 * j + which) * quarter, HEAD)
                copies.append(
                    pltpu.make_async_copy(
                        weight_ref.at[:, pl.ds(start, quarter)],
                        out.at[:, pl.ds(j * quarter, quarter)],
                        sems.at[2 * i + j],
                    )
                )
        for copy in copies:
            copy.start()
        for copy in copies:
            copy.wait()

    anywhere = pl.BlockSpec(memory_space=pl.ANY)
    inside = pl.BlockSpec(memory_space=pltpu.VMEM)
    out = jax.ShapeDtypeStruct((depth, width // 2), weight.dtype)
    return pl.pallas_call(
        kernel,
        out_shape=(out, out),
        in_specs=[pl.BlockSpec(memory_space=pltpu.SMEM), anywhere],
        out_specs=(inside, inside),
        scratch_shapes=[pltpu.SemaphoreType.DMA((4,))],
        cost_estimate=pl.CostEstimate(
            flops=0, bytes_accessed=4 * depth * width, transcendentals=0
        ),
    )(half, weight)


def core_columns(states, core, depth):
    tokens, width = states.shape
    count = width // (2 * depth)

    def kernel(core_ref, states_ref, out_ref, sems):
        copies = []
        for i in range(count):
            start = pl.multiple_of((2 * i + core_ref[0]) * depth, HEAD)
            copies.append(
                pltpu.make_async_copy(
                    states_ref.at[:, pl.ds(start, depth)],
                    out_ref.at[:, pl.ds(i * depth, depth)],
                    sems.at[i],
                )
            )
        for copy in copies:
            copy.start()
        for copy in copies:
            copy.wait()

    anywhere = pl.BlockSpec(memory_space=pl.ANY)
    return pl.pallas_call(
        kernel,
        out_shape=jax.ShapeDtypeStruct((tokens, width // 2), states.dtype),
        in_specs=[pl.BlockSpec(memory_space=pltpu.SMEM), anywhere],
        out_specs=pl.BlockSpec(memory_space=pltpu.VMEM),
        scratch_shapes=[pltpu.SemaphoreType.DMA((count,))],
        cost_estimate=pl.CostEstimate(
            flops=0, bytes_accessed=2 * tokens * width, transcendentals=0
        ),
    )(core, states)


def accumulate(states, scalars, pieces, places, bias=None, start=None, later=0):
    count = len(pieces)
    depth, columns = pieces[0].shape
    tokens = states[0].shape[0]
    batch = 5
    begun = 4 if start is not None else 1

    def kernel(scalar_ref, *refs):
        state_refs, refs = refs[:2], refs[2:]
        piece_refs, refs = refs[:count], refs[count:]
        start_refs, refs = refs[:begun], refs[begun:]
        if later:
            totals, lefts, refs = refs[:4], refs[4:6], refs[6:]
        else:
            outs, totals, refs = refs[:4], refs[4:8], refs[8:]
        left, right, bias_ref, sems = refs
        used = 0

        def begin(source, target):
            nonlocal used
            copy = pltpu.make_async_copy(source, target, sems.at[used])
            copy.start()
            used += 1
            return copy

        def columns_at(side, index):
            at = scalar_ref[2 + index]
            at = 2 * at + scalar_ref[0] if side else at
            return state_refs[side].at[:, pl.ds(pl.multiple_of(at * depth, HEAD), depth)]

        waits = []
        if start is None:
            first = [begin(start_refs[0], bias_ref)]
        else:
            first = [begin(source, target) for source, target in zip(start_refs, totals)]
        for i in range(count):
            deep = pl.ds(i * depth, depth)
            waits.append(
                [begin(piece_refs[i], right.at[deep])]
                + [begin(columns_at(side, i), left.at[side, :, deep]) for side in range(2)]
            )
        rest = [
            begin(columns_at(side, count + i), lefts[side].at[:, pl.ds(i * depth, depth)])
            for i in range(later)
            for side in range(2)
        ]
        for copy in first:
            copy.wait()
        touched = [start is not None] * 4
        for i in range(0, count, batch):
            stop = min(i + batch, count)
            for copies in waits[i:stop]:
                for copy in copies:
                    copy.wait()
            for j in range(i, stop):
                deep = slice(j * depth, (j + 1) * depth)
                for side in range(2):
                    which = 2 * places[j] + side
                    part = jnp.dot(
                        left[side, :, deep], right[deep], preferred_element_type=jnp.float32
                    )
                    if touched[which]:
                        totals[which][...] += part
                    elif side == 0:
                        totals[which][...] = part
                    else:
                        own = scalar_ref[1] if places[j] == 0 else 1 - scalar_ref[1]
                        part_width = columns // 2
                        for k in range(2):
                            at = pl.multiple_of((2 * k + own) * part_width, HEAD)
                            lanes = slice(k * part_width, (k + 1) * part_width)
                            totals[which][:, lanes] = (
                                part[:, lanes] + bias_ref[:, pl.ds(at, part_width)]
                            )
                    touched[which] = True
        if not later:
            rest += [begin(source, target) for source, target in zip(totals, outs)]
        for copy in rest:
            copy.wait()

    outside = pl.BlockSpec(memory_space=pltpu.HBM)
    inside = pl.BlockSpec(memory_space=pltpu.VMEM)
    sums = (tokens, columns)
    if later:
        out_shape = [jax.ShapeDtypeStruct(sums, jnp.float32)] * 4
        out_shape += [jax.ShapeDtypeStruct((tokens, later * depth), jnp.bfloat16)] * 2
        out_specs, scratch = [inside] * 6, []
    else:
        out_shape = [pltpu.HBM(sums, jnp.float32)] * 4
        out_specs, scratch = [outside] * 4, [pltpu.VMEM(sums, jnp.float32)] * 4
    outer = [*states, *pieces, *((bias,) if start is None else start)]
    return pl.pallas_call(
        kernel,
        out_shape=out_shape,
        in_specs=[pl.BlockSpec(memory_space=pltpu.SMEM)] + [outside] * len(outer),
        out_specs=out_specs,
        scratch_shapes=scratch
        + [
            pltpu.VMEM((2, tokens, count * depth), jnp.bfloat16),
            pltpu.VMEM((count * depth, columns), jnp.bfloat16),
            pltpu.VMEM((1, 2 * columns), jnp.float32),
            pltpu.SemaphoreType.DMA((3 * count + 2 * later + 8,)),
        ],
        compiler_params=pltpu.CompilerParams(vmem_limit_bytes=LIMIT),
        cost_estimate=pl.CostEstimate(
            flops=4 * count * tokens * depth * columns,
            bytes_accessed=count * (4 * tokens * depth + 2 * depth * columns),
            transcendentals=0,
        ),
    )(scalars, *(pltpu.with_memory_space_constraint(a, pltpu.HBM) for a in outer))


def complete(left, pieces, total):
    depth = pieces[0].shape[0]

    def kernel(left_ref, total_ref, *refs):
        out_ref = refs[-1]
        for i, piece in enumerate(refs[:-1]):
            part = jnp.dot(
                left_ref[:, i * depth : (i + 1) * depth],
                piece[...],
                preferred_element_type=jnp.float32,
            )
            out_ref[...] = (total_ref if i == 0 else out_ref)[...] + part

    inside = pl.BlockSpec(memory_space=pltpu.VMEM)
    return pl.pallas_call(
        kernel,
        out_shape=jax.ShapeDtypeStruct(total.shape, total.dtype),
        in_specs=[inside] * (2 + len(pieces)),
        out_specs=inside,
        compiler_params=pltpu.CompilerParams(vmem_limit_bytes=LIMIT),
        cost_estimate=pl.CostEstimate(
            flops=2 * left.size * total.shape[1],
            bytes_accessed=2 * left.size,
            transcendentals=0,
        ),
    )(left, total, *pieces)


def finish(own_part, peer_part, table, replicas, earlier=None):
    tokens, columns = own_part.shape
    keys = columns // 2
    rows = replicas * SPAN

    def kernel(own_ref, peer_ref, table_in, *refs):
        kv_ref, key_ref, out_ref, table_ref, sem = refs[-5:]
        copy = pltpu.make_async_copy(table_in, table_ref, sem)
        copy.start()
        kv = (own_ref[...] + peer_ref[...]).astype(jnp.bfloat16).astype(jnp.float32)
        copy.wait()
        kv = jnp.where(table_ref[:, LIVE : LIVE + 1] > 0.5, kv, 0.0)
        kept = kv.astype(jnp.bfloat16)
        kv_ref[...] = kept
        destination = table_ref[:, DESTINATION : DESTINATION + 1].astype(jnp.int32)
        token = lax.broadcasted_iota(jnp.int32, (tokens, rows), 0)
        row = lax.broadcasted_iota(jnp.int32, (tokens, rows), 1)
        match = (destination == row // SPAN) & (token % SPAN == row % SPAN)
        pick = jnp.where(match, 1.0, 0.0).astype(jnp.bfloat16)
        over_tokens = (((0,), (0,)), ((), ()))
        found = lax.dot_general(
            pick,
            jnp.ones((tokens, HEAD), jnp.bfloat16),
            over_tokens,
            preferred_element_type=jnp.float32,
        )
        spans = lax.dot_general(pick, kept, over_tokens, preferred_element_type=jnp.float32)
        spans = jnp.where(found[:, :1] > 0.5, spans, ABSENT).astype(jnp.bfloat16)
        if earlier is None:
            out_ref[...] = spans
        else:
            out_ref[:, :columns] = refs[0][...]
            out_ref[:, columns:] = spans
        cosine, sine = table_ref[:, : HEAD // 2], table_ref[:, HEAD // 2 : HEAD]
        cosine = jnp.concatenate([cosine, cosine], axis=1)
        sine = jnp.concatenate([-sine, sine], axis=1)
        for head in range(keys // HEAD):
            part = kv[:, head * HEAD : (head + 1) * HEAD]
            turned = part * cosine + pltpu.roll(part, HEAD // 2, 1) * sine
            key_ref[:, head * HEAD : (head + 1) * HEAD] = turned.astype(jnp.bfloat16)

    inside = pl.BlockSpec(memory_space=pltpu.VMEM)
    sent = columns if earlier is None else 2 * columns
    more = () if earlier is None else (earlier,)
    return pl.pallas_call(
        kernel,
        out_shape=(
            jax.ShapeDtypeStruct((tokens, columns), jnp.bfloat16),
            jax.ShapeDtypeStruct((tokens, keys), jnp.bfloat16),
            jax.ShapeDtypeStruct((rows, sent), jnp.bfloat16),
        ),
        in_specs=[inside] * 2 + [pl.BlockSpec(memory_space=pltpu.HBM)] + [inside] * len(more),
        out_specs=(inside,) * 3,
        scratch_shapes=[pltpu.VMEM(table.shape, table.dtype), pltpu.SemaphoreType.DMA],
        compiler_params=pltpu.CompilerParams(vmem_limit_bytes=LIMIT),
        cost_estimate=pl.CostEstimate(
            flops=2 * rows * tokens * columns,
            bytes_accessed=10 * tokens * columns,
            transcendentals=0,
        ),
    )(own_part, peer_part, pltpu.with_memory_space_constraint(table, pltpu.HBM), *more)


def attend(half, flip, mask, table, queries, keys, kv, context=None):
    tokens = queries.shape[0]
    heads = keys.shape[1] // HEAD
    width = queries.shape[1] // (2 * heads)

    def kernel(half_ref, mask_ref, table_ref, query_ref, key_ref, value_ref, *refs):
        context_ref = refs[-1]
        scale = HEAD**-0.5 * math.log2(math.e)
        lanes = [slice(h * HEAD, (h + 1) * HEAD) for h in range(width // HEAD)]
        scores = [
            lax.dot_general(
                query_ref[:, lane],
                key_ref[...],
                (((1,), (1,)), ((), ())),
                preferred_element_type=jnp.float32,
            )
            for lane in lanes
        ]
        weights = []
        for score in scores:
            score = score * scale + mask_ref[...]
            weight = jnp.exp2(score - jnp.max(score, axis=1, keepdims=True))
            inverse = 1.0 / jnp.sum(weight, axis=1, keepdims=True)
            weights.append((weight * inverse).astype(jnp.bfloat16))
        is_live = table_ref[:, LIVE - HEAD : LIVE - HEAD + 1] > 0.5
        for lane, weight in zip(lanes, weights):
            mixed = jnp.dot(weight, value_ref[...], preferred_element_type=jnp.float32)
            context_ref[:, lane] = jnp.where(is_live, mixed, 0.0).astype(jnp.bfloat16)

    def wide_at(i, s):
        return (0, (1 - s[0] if flip else s[0]) * heads + i)

    in_specs = [
        pl.BlockSpec((tokens, tokens), lambda i, s: (0, 0)),
        pl.BlockSpec((tokens, HEAD), lambda i, s: (0, 1)),
        pl.BlockSpec((tokens, width), wide_at),
        pl.BlockSpec((tokens, HEAD), lambda i, s: (0, i)),
        pl.BlockSpec((tokens, HEAD), lambda i, s: (0, heads + i)),
    ]
    arguments = [half, mask, table, queries, keys, kv]
    if context is not None:
        in_specs.append(pl.BlockSpec(memory_space=pl.ANY))
        arguments.append(context)
    return pl.pallas_call(
        kernel,
        out_shape=jax.ShapeDtypeStruct(queries.shape, jnp.bfloat16),
        grid_spec=pltpu.PrefetchScalarGridSpec(
            num_scalar_prefetch=1,
            grid=(heads,),
            in_specs=in_specs,
            out_specs=pl.BlockSpec((tokens, width), wide_at),
        ),
        input_output_aliases={} if context is None else {6: 0},
        compiler_params=pltpu.CompilerParams(vmem_limit_bytes=LIMIT),
        cost_estimate=pl.CostEstimate(
            flops=4 * tokens * tokens * heads * width,
            bytes_accessed=4 * tokens * heads * width,
            transcendentals=tokens * tokens * heads * width // HEAD,
        ),
    )(*arguments)


def place(scalars, table, mine, other, spans):
    rows = WORK * SPAN
    slots, width = spans.shape
    part = width // 4

    def kernel(scalar_ref, table_ref, mine_ref, other_ref, spans_ref, out_ref, total_ref):
        @pl.when(pl.program_id(0) == 0)
        def _():
            present = spans_ref[:, :HEAD].astype(jnp.float32)
            present = jnp.where(present > 0.5 * ABSENT, 0.0, 1.0)
            row = lax.broadcasted_iota(jnp.int32, (slots, slots), 0)
            column = lax.broadcasted_iota(jnp.int32, (slots, slots), 1)
            before = (column // SPAN < row // SPAN) & (column % SPAN == 0)
            before = jnp.where(before, 1.0, 0.0).astype(jnp.bfloat16)
            earlier = jnp.dot(
                before, present.astype(jnp.bfloat16), preferred_element_type=jnp.float32
            )
            rank = earlier[:, :1].astype(jnp.int32) + scalar_ref[1]
            target = lax.broadcasted_iota(jnp.int32, (slots, rows), 1)
            sender = lax.broadcasted_iota(jnp.int32, (slots, rows), 0)
            hit = (target // SPAN == rank) & (target % SPAN == sender % SPAN)
            hit = jnp.where(hit & (present[:, :1] > 0.5), 1.0, 0.0).astype(jnp.bfloat16)
            moved = lax.dot_general(
                hit, spans_ref[...], (((0,), (0,)), ((), ())), preferred_element_type=jnp.float32
            ).astype(jnp.bfloat16)
            keep = table_ref[:, KEEP : KEEP + 1] > 0.5
            for i in range(4):
                home = (mine_ref, other_ref)[i // 2][:, (i % 2) * part : (i % 2 + 1) * part]
                home = home.astype(jnp.float32)
                came = moved[:, i * part : (i + 1) * part].astype(jnp.float32)
                total_ref[i] = jnp.where(keep, home, came).astype(jnp.bfloat16)

        out_ref[...] = total_ref[pl.program_id(0)]

    def out_at(i, s):
        return (0, 2 * (i % 2) + jnp.where(i < 2, s[0], 1 - s[0]))

    home = pl.BlockSpec((rows, width // 2), lambda i, s: (0, 0))
    return pl.pallas_call(
        kernel,
        out_shape=jax.ShapeDtypeStruct((rows, width), jnp.bfloat16),
        grid_spec=pltpu.PrefetchScalarGridSpec(
            num_scalar_prefetch=1,
            grid=(4,),
            in_specs=[
                pl.BlockSpec((rows, table.shape[1]), lambda i, s: (0, 0)),
                home,
                home,
                pl.BlockSpec((slots, width), lambda i, s: (0, 0)),
            ],
            out_specs=pl.BlockSpec((rows, part), out_at),
            scratch_shapes=[pltpu.VMEM((4, rows, part), jnp.bfloat16)],
        ),
        compiler_params=pltpu.CompilerParams(vmem_limit_bytes=LIMIT),
        cost_estimate=pl.CostEstimate(
            flops=2 * rows * slots * width,
            bytes_accessed=4 * rows * width,
            transcendentals=0,
        ),
    )(scalars, table, mine, other, spans)


def per_device(states, queries, kv_weight, kv_bias, lengths, bounds, balance):
    replicas = lax.axis_size("dp")
    own_index = lax.axis_index("dp")
    half = (lax.axis_index("group") % 2).astype(jnp.int32)[None]
    core = (own_index % 2).astype(jnp.int32)[None]
    own_y = own_index // 2 % 2
    own_z = own_index // 4
    ring = replicas // 4
    position = jnp.where(own_z % 2 == 0, own_z // 2, ring - 1 - own_z // 2)
    tokens = states.shape[0]
    depth, width = kv_weight.shape

    def block(offset, across):
        z = ring_place(ring, (position - offset + ring) % ring)
        return (z * 2 + (1 - own_y if across else own_y)).astype(jnp.int32)

    token_ids = jnp.arange(tokens, dtype=jnp.int32)
    is_live = token_ids < lengths[0] * SPAN
    owner = jnp.repeat(balance[0], SPAN)
    is_moved = is_live & (owner != own_index)
    destination = jnp.where(is_moved, owner, -1)
    keep = is_live & jnp.logical_not(is_moved)
    kept_count = jnp.sum(keep.astype(jnp.int32)) // SPAN
    chosen, rejected = bounds[0, 0], bounds[0, 1]
    segment = (token_ids >= chosen).astype(jnp.int32) + (token_ids >= rejected).astype(jnp.int32)
    place_ids = jnp.where(token_ids >= rejected, token_ids - (rejected - chosen), token_ids)
    target, source = token_ids[:, None], token_ids[None, :]
    near = (segment[None, :] == segment[:, None]) | (segment[None, :] == 0)
    allowed = ((source <= target) & is_live[None, :] & near) | (source == target)
    mask = jnp.where(allowed, 0.0, MASKED).astype(jnp.float32)
    frequency = jnp.exp(
        jnp.arange(HEAD // 2, dtype=jnp.float32) * (-2.0 * math.log(1000000.0) / HEAD)
    )
    angles = place_ids.astype(jnp.float32)[:, None] * frequency[None, :]
    columns = [jnp.cos(angles), jnp.sin(angles)]
    columns += [c.astype(jnp.float32)[:, None] for c in (is_live, destination, keep)]
    columns.append(jnp.zeros((tokens, HEAD - 3), jnp.float32))
    table = jnp.concatenate(columns, axis=1)
    scalars = jnp.stack([half[0], kept_count])
    plan = (table, mask, scalars)

    links = Links(replicas, lax.axis_size("group"))
    mine_weight, other_weight = halves(kv_weight, half)
    peer_columns = core_columns(states, 1 - core, depth)
    peer_states = core_swap(peer_columns, replicas)

    both = (peer_states, states)

    def listed(pieces):
        return jnp.stack([core[0], half[0]] + [b for _, b in pieces])

    fore = ring // 2
    order = [k for j in range(1, ring) for k in (j, -j)][: ring - 1]
    held = {0: mine_weight}
    mine = [(mine_weight, block(0, False))]
    other = [(other_weight, block(0, False))]
    middle, late = [], []
    crossed = links.send(mine_weight, "y")
    mine.append((crossed, block(0, True)))
    moving = other_weight
    for k in order:
        final = k == order[-1]
        nearer = held[k - 1] if k > 0 else held[k + 1]
        second = k == order[1]
        before = (peer_columns,) if second else plan if final else ()
        held[k] = links.send(nearer, "fore" if k > 0 else "back", before, lag=2 if second else None)
        mine.append((held[k], block(k, False)))
        crossed = links.send(held[k], "y")
        if 1 <= k < fore:
            other.append((links.send(held[k], "x"), block(k, False)))
        if final:
            early = mine + other
            sums = accumulate(
                both,
                listed(early),
                [p for p, _ in early],
                [0] * len(mine) + [1] * len(other),
                bias=kv_bias[None, :],
            )
            for j in range(1, ring - fore):
                moving = links.send(moving, "back")
                middle.append((moving, block(-j, False)))
            moving = links.send(moving, "back", sums)
            late.append((moving, block(fore - ring, False)))
            late.append((links.send(other_weight, "y", sums), block(0, True)))
            late.append((links.send(crossed, "x", sums), block(k, True)))
            middle = [(crossed, block(k, True))] + middle
            mine_peer, mine_own, other_peer, other_own, left_peer, left_own = accumulate(
                both,
                listed(middle + late),
                [p for p, _ in middle],
                [0] + [1] * (len(middle) - 1),
                start=sums,
                later=len(late),
            )
        else:
            mine.append((crossed, block(k, True)))
            piece = (links.send(crossed, "x"), block(k, True))
            (middle if k == order[-2] else other).append(piece)

    mine_peer = core_swap(mine_peer, replicas)
    last = [p for p, _ in late]
    other_peer = core_swap(complete(left_peer, last, other_peer), replicas)
    other_own = complete(left_own, last, other_own)
    mine_own = after(mine_own, other_own)
    mine_kv, mine_keys, mine_spans = finish(mine_own, mine_peer, table, replicas)
    other_kv, other_keys, spans = finish(other_own, other_peer, table, replicas, mine_spans)
    spans = spans.reshape(replicas, SPAN, width)
    spans = lax.all_to_all(spans, "dp", split_axis=0, concat_axis=0, tiled=True)
    spans = spans.reshape(replicas * SPAN, width)
    context = attend(half, False, mask, table, queries, mine_keys, mine_kv)
    context = attend(half, True, mask, table, queries, other_keys, other_kv, context)
    work_rows = place(scalars, table, mine_kv, other_kv, spans)
    return (context, work_rows)


def solution(mesh):
    in_specs = (
        P(("group", "dp"), None),
        P(("group", "dp"), None),
        P("dp", None),
        P(),
        P(("group", "dp")),
        P(("group", "dp"), None),
        P(("group", "dp"), None),
    )
    out_specs = (P(("group", "dp"), None), P(("group", "dp"), None))
    return jax.shard_map(
        per_device, mesh=mesh, in_specs=in_specs, out_specs=out_specs, check_vma=False
    )
```

```python
import math

import jax
import jax.numpy as jnp
from jax import lax
from jax.experimental import pallas as pl
from jax.experimental.pallas import tpu as pltpu
from jax.sharding import PartitionSpec as P

HEAD = 128
SPAN = 8
HOME = 32
WORK = 24
ABSENT = 1e30
MASKED = -1e30
LIMIT = 18 << 20
LAG = {"x": 1, "y": 2, "z": 1}
LIVE, DESTINATION, KEEP = HEAD, HEAD + 1, HEAD + 2


def ring_place(ring, position):
    return jnp.where(2 * position < ring, 2 * position, 2 * (ring - 1 - position) + 1)


def after(value, *before):
    return lax.optimization_barrier((value, *before))[0] if before else value


class Links:
    def __init__(self, replicas, groups):
        ring = replicas // 4
        places = [p for p in range(0, ring, 2)] + [p for p in range(1, ring, 2)][::-1]
        ahead = {places[i]: places[(i + 1) % ring] for i in range(ring)}
        steps = [
            ((z * 2 + y) * 2 + c, (ahead[z] * 2 + y) * 2 + c)
            for z in range(ring)
            for y in range(2)
            for c in range(2)
        ]
        self.routes = {
            "fore": ("z", "dp", steps),
            "back": ("z", "dp", [(d, s) for s, d in steps]),
            "y": ("y", "dp", [(i, i ^ 2) for i in range(replicas)]),
            "x": ("x", "group", [(i, i ^ 1) for i in range(groups)]),
        }
        self.sent = {"x": [], "y": [], "z": []}

    def send(self, value, route, before=(), lag=None):
        link, axis, pairs = self.routes[route]
        sent = self.sent[link]
        lag = LAG[link] if lag is None else lag
        if len(sent) >= lag:
            before = (sent[-lag], *before)
        sent.append(lax.ppermute(after(value, *before), axis, pairs))
        return sent[-1]


def core_swap(value, replicas):
    return lax.ppermute(value, "dp", [(i, i ^ 1) for i in range(replicas)])


def halves(weight, half):
    depth, width = weight.shape
    quarter = width // 4

    def kernel(half_ref, weight_ref, mine_ref, other_ref, sems):
        copies = []
        for i, out in enumerate((mine_ref, other_ref)):
            which = half_ref[0] if i == 0 else 1 - half_ref[0]
            for j in range(2):
                start = pl.multiple_of((2 * j + which) * quarter, HEAD)
                copies.append(
                    pltpu.make_async_copy(
                        weight_ref.at[:, pl.ds(start, quarter)],
                        out.at[:, pl.ds(j * quarter, quarter)],
                        sems.at[2 * i + j],
                    )
                )
        for copy in copies:
            copy.start()
        for copy in copies:
            copy.wait()

    anywhere = pl.BlockSpec(memory_space=pl.ANY)
    inside = pl.BlockSpec(memory_space=pltpu.VMEM)
    out = jax.ShapeDtypeStruct((depth, width // 2), weight.dtype)
    return pl.pallas_call(
        kernel,
        out_shape=(out, out),
        in_specs=[pl.BlockSpec(memory_space=pltpu.SMEM), anywhere],
        out_specs=(inside, inside),
        scratch_shapes=[pltpu.SemaphoreType.DMA((4,))],
        cost_estimate=pl.CostEstimate(
            flops=0, bytes_accessed=4 * depth * width, transcendentals=0
        ),
    )(half, weight)


def core_columns(states, core, depth):
    tokens, width = states.shape
    count = width // (2 * depth)

    def kernel(core_ref, states_ref, out_ref, sems):
        copies = []
        for i in range(count):
            start = pl.multiple_of((2 * i + core_ref[0]) * depth, HEAD)
            copies.append(
                pltpu.make_async_copy(
                    states_ref.at[:, pl.ds(start, depth)],
                    out_ref.at[:, pl.ds(i * depth, depth)],
                    sems.at[i],
                )
            )
        for copy in copies:
            copy.start()
        for copy in copies:
            copy.wait()

    anywhere = pl.BlockSpec(memory_space=pl.ANY)
    return pl.pallas_call(
        kernel,
        out_shape=jax.ShapeDtypeStruct((tokens, width // 2), states.dtype),
        in_specs=[pl.BlockSpec(memory_space=pltpu.SMEM), anywhere],
        out_specs=pl.BlockSpec(memory_space=pltpu.VMEM),
        scratch_shapes=[pltpu.SemaphoreType.DMA((count,))],
        cost_estimate=pl.CostEstimate(
            flops=0, bytes_accessed=2 * tokens * width, transcendentals=0
        ),
    )(core, states)


def accumulate(states, scalars, pieces, places, bias=None, start=None, later=0, table=None, rows=0):
    count = len(pieces)
    depth, columns = pieces[0].shape
    tokens = states[0].shape[0]
    batch = 5
    begun = 4 if start is not None else 1

    def kernel(scalar_ref, *refs):
        state_refs, refs = refs[:2], refs[2:]
        piece_refs, refs = refs[:count], refs[count:]
        start_refs, refs = refs[:begun], refs[begun:]
        if later:
            table_in, totals, lefts, pick_ref = refs[0], refs[1:5], refs[5:7], refs[7]
            table_ref, refs = refs[8], refs[9:]
        else:
            outs, totals, refs = refs[:4], refs[4:8], refs[8:]
        left, right, bias_ref, sems = refs
        used = 0

        def begin(source, target):
            nonlocal used
            copy = pltpu.make_async_copy(source, target, sems.at[used])
            copy.start()
            used += 1
            return copy

        def columns_at(side, index):
            at = scalar_ref[2 + index]
            at = 2 * at + scalar_ref[0] if side else at
            return state_refs[side].at[:, pl.ds(pl.multiple_of(at * depth, HEAD), depth)]

        waits = []
        if start is None:
            first = [begin(start_refs[0], bias_ref)]
        else:
            first = [begin(source, target) for source, target in zip(start_refs, totals)]
        for i in range(count):
            deep = pl.ds(i * depth, depth)
            waits.append(
                [begin(piece_refs[i], right.at[deep])]
                + [begin(columns_at(side, i), left.at[side, :, deep]) for side in range(2)]
            )
        rest = [
            begin(columns_at(side, count + i), lefts[side].at[:, pl.ds(i * depth, depth)])
            for i in range(later)
            for side in range(2)
        ]
        if later:
            table_copy = begin(table_in, table_ref)
        for copy in first:
            copy.wait()
        if later:
            table_copy.wait()
            destination = table_ref[:, DESTINATION : DESTINATION + 1].astype(jnp.int32)
            token = lax.broadcasted_iota(jnp.int32, (tokens, rows), 0)
            row = lax.broadcasted_iota(jnp.int32, (tokens, rows), 1)
            match = (destination == row // SPAN) & (token % SPAN == row % SPAN)
            pick_ref[...] = jnp.where(match, 1.0, 0.0).astype(jnp.bfloat16)
        touched = [start is not None] * 4
        for i in range(0, count, batch):
            stop = min(i + batch, count)
            for copies in waits[i:stop]:
                for copy in copies:
                    copy.wait()
            for j in range(i, stop):
                deep = slice(j * depth, (j + 1) * depth)
                for side in range(2):
                    which = 2 * places[j] + side
                    part = jnp.dot(
                        left[side, :, deep], right[deep], preferred_element_type=jnp.float32
                    )
                    if touched[which]:
                        totals[which][...] += part
                    elif side == 0:
                        totals[which][...] = part
                    else:
                        own = scalar_ref[1] if places[j] == 0 else 1 - scalar_ref[1]
                        part_width = columns // 2
                        for k in range(2):
                            at = pl.multiple_of((2 * k + own) * part_width, HEAD)
                            lanes = slice(k * part_width, (k + 1) * part_width)
                            totals[which][:, lanes] = (
                                part[:, lanes] + bias_ref[:, pl.ds(at, part_width)]
                            )
                    touched[which] = True
        if not later:
            rest += [begin(source, target) for source, target in zip(totals, outs)]
        for copy in rest:
            copy.wait()

    outside = pl.BlockSpec(memory_space=pltpu.HBM)
    inside = pl.BlockSpec(memory_space=pltpu.VMEM)
    sums = (tokens, columns)
    if later:
        out_shape = [jax.ShapeDtypeStruct(sums, jnp.float32)] * 4
        out_shape += [jax.ShapeDtypeStruct((tokens, later * depth), jnp.bfloat16)] * 2
        out_shape += [jax.ShapeDtypeStruct((tokens, rows), jnp.bfloat16)]
        out_specs, scratch = [inside] * 7, [pltpu.VMEM(table.shape, table.dtype)]
    else:
        out_shape = [pltpu.HBM(sums, jnp.float32)] * 4
        out_specs, scratch = [outside] * 4, [pltpu.VMEM(sums, jnp.float32)] * 4
    outer = [*states, *pieces, *((bias,) if start is None else start)]
    outer += [table] if later else []
    return pl.pallas_call(
        kernel,
        out_shape=out_shape,
        in_specs=[pl.BlockSpec(memory_space=pltpu.SMEM)] + [outside] * len(outer),
        out_specs=out_specs,
        scratch_shapes=scratch
        + [
            pltpu.VMEM((2, tokens, count * depth), jnp.bfloat16),
            pltpu.VMEM((count * depth, columns), jnp.bfloat16),
            pltpu.VMEM((1, 2 * columns), jnp.float32),
            pltpu.SemaphoreType.DMA((3 * count + 2 * later + 8,)),
        ],
        compiler_params=pltpu.CompilerParams(vmem_limit_bytes=LIMIT),
        cost_estimate=pl.CostEstimate(
            flops=4 * count * tokens * depth * columns,
            bytes_accessed=count * (4 * tokens * depth + 2 * depth * columns),
            transcendentals=0,
        ),
    )(scalars, *(pltpu.with_memory_space_constraint(a, pltpu.HBM) for a in outer))


def complete(left, pieces, total):
    depth = pieces[0].shape[0]

    def kernel(left_ref, total_ref, *refs):
        out_ref = refs[-1]
        for i, piece in enumerate(refs[:-1]):
            part = jnp.dot(
                left_ref[:, i * depth : (i + 1) * depth],
                piece[...],
                preferred_element_type=jnp.float32,
            )
            out_ref[...] = (total_ref if i == 0 else out_ref)[...] + part

    inside = pl.BlockSpec(memory_space=pltpu.VMEM)
    return pl.pallas_call(
        kernel,
        out_shape=jax.ShapeDtypeStruct(total.shape, total.dtype),
        in_specs=[inside] * (2 + len(pieces)),
        out_specs=inside,
        compiler_params=pltpu.CompilerParams(vmem_limit_bytes=LIMIT),
        cost_estimate=pl.CostEstimate(
            flops=2 * left.size * total.shape[1],
            bytes_accessed=2 * left.size,
            transcendentals=0,
        ),
    )(left, total, *pieces)


def finish(own_part, peer_part, pick, earlier=None):
    tokens, columns = own_part.shape
    rows = pick.shape[1]
    last = earlier is not None

    def kernel(own_ref, peer_ref, pick_ref, *refs):
        if last:
            earlier_ref, kv_ref, out_ref, spans_ref, sems = refs
            first = pltpu.make_async_copy(
                earlier_ref, out_ref.at[:, pl.ds(0, columns)], sems.at[0]
            )
            first.start()
        else:
            kv_ref, spans_ref = refs
        kv = (own_ref[...] + peer_ref[...]).astype(jnp.bfloat16)
        kv_ref[...] = kv
        over_tokens = (((0,), (0,)), ((), ()))
        found = lax.dot_general(
            pick_ref[...],
            jnp.ones((tokens, HEAD), jnp.bfloat16),
            over_tokens,
            preferred_element_type=jnp.float32,
        )
        spans = lax.dot_general(
            pick_ref[...], kv, over_tokens, preferred_element_type=jnp.float32
        )
        spans_ref[...] = jnp.where(found[:, :1] > 0.5, spans, ABSENT).astype(jnp.bfloat16)
        if last:
            second = pltpu.make_async_copy(
                spans_ref, out_ref.at[:, pl.ds(columns, columns)], sems.at[1]
            )
            second.start()
            first.wait()
            second.wait()

    inside = pl.BlockSpec(memory_space=pltpu.VMEM)
    kv_shape = jax.ShapeDtypeStruct((tokens, columns), jnp.bfloat16)
    if last:
        out_shape = (kv_shape, pltpu.HBM((rows, 2 * columns), jnp.bfloat16))
        out_specs = (inside, pl.BlockSpec(memory_space=pltpu.HBM))
        scratch = [pltpu.VMEM((rows, columns), jnp.bfloat16), pltpu.SemaphoreType.DMA((2,))]
    else:
        out_shape = (kv_shape, jax.ShapeDtypeStruct((rows, columns), jnp.bfloat16))
        out_specs, scratch = (inside, inside), []
    more = (earlier,) if last else ()
    return pl.pallas_call(
        kernel,
        out_shape=out_shape,
        in_specs=[inside] * (3 + len(more)),
        out_specs=out_specs,
        scratch_shapes=scratch,
        compiler_params=pltpu.CompilerParams(vmem_limit_bytes=LIMIT),
        cost_estimate=pl.CostEstimate(
            flops=2 * rows * tokens * columns,
            bytes_accessed=10 * tokens * columns,
            transcendentals=0,
        ),
    )(own_part, peer_part, pick, *more)


def attend(half, flip, mask, table, queries, kv, context=None):
    tokens = queries.shape[0]
    heads = kv.shape[1] // (2 * HEAD)
    width = queries.shape[1] // (2 * heads)

    def kernel(half_ref, mask_ref, table_ref, query_ref, key_ref, value_ref, *refs):
        context_ref = refs[-1]
        scale = HEAD**-0.5 * math.log2(math.e)
        lanes = [slice(h * HEAD, (h + 1) * HEAD) for h in range(width // HEAD)]
        is_live = table_ref[:, LIVE : LIVE + 1] > 0.5
        cosine, sine = table_ref[:, : HEAD // 2], table_ref[:, HEAD // 2 : HEAD]
        cosine = jnp.concatenate([cosine, cosine], axis=1)
        sine = jnp.concatenate([-sine, sine], axis=1)
        key = jnp.where(is_live, key_ref[...].astype(jnp.float32), 0.0)
        key = (key * cosine + pltpu.roll(key, HEAD // 2, 1) * sine).astype(jnp.bfloat16)
        value = jnp.where(is_live, value_ref[...].astype(jnp.float32), 0.0).astype(jnp.bfloat16)
        scores = [
            lax.dot_general(
                query_ref[:, lane],
                key,
                (((1,), (1,)), ((), ())),
                preferred_element_type=jnp.float32,
            )
            for lane in lanes
        ]
        weights = []
        for score in scores:
            score = score * scale + mask_ref[...]
            weight = jnp.exp2(score - jnp.max(score, axis=1, keepdims=True))
            inverse = 1.0 / jnp.sum(weight, axis=1, keepdims=True)
            weights.append((weight * inverse).astype(jnp.bfloat16))
        for lane, weight in zip(lanes, weights):
            mixed = jnp.dot(weight, value, preferred_element_type=jnp.float32)
            context_ref[:, lane] = jnp.where(is_live, mixed, 0.0).astype(jnp.bfloat16)

    def wide_at(i, s):
        return (0, (1 - s[0] if flip else s[0]) * heads + i)

    in_specs = [
        pl.BlockSpec((tokens, tokens), lambda i, s: (0, 0)),
        pl.BlockSpec(table.shape, lambda i, s: (0, 0)),
        pl.BlockSpec((tokens, width), wide_at),
        pl.BlockSpec((tokens, HEAD), lambda i, s: (0, i)),
        pl.BlockSpec((tokens, HEAD), lambda i, s: (0, heads + i)),
    ]
    arguments = [half, mask, table, queries, kv, kv]
    if context is not None:
        in_specs.append(pl.BlockSpec(memory_space=pl.ANY))
        arguments.append(context)
    return pl.pallas_call(
        kernel,
        out_shape=jax.ShapeDtypeStruct(queries.shape, jnp.bfloat16),
        grid_spec=pltpu.PrefetchScalarGridSpec(
            num_scalar_prefetch=1,
            grid=(heads,),
            in_specs=in_specs,
            out_specs=pl.BlockSpec((tokens, width), wide_at),
        ),
        input_output_aliases={} if context is None else {6: 0},
        compiler_params=pltpu.CompilerParams(vmem_limit_bytes=LIMIT),
        cost_estimate=pl.CostEstimate(
            flops=4 * tokens * tokens * heads * width,
            bytes_accessed=4 * tokens * heads * width,
            transcendentals=tokens * tokens * heads * width // HEAD,
        ),
    )(*arguments)


def place(scalars, table, mine, other, spans):
    rows = WORK * SPAN
    slots, width = spans.shape
    part = width // 4

    def kernel(scalar_ref, table_ref, mine_ref, other_ref, spans_ref, out_ref, total_ref, sems):
        present = spans_ref[:, :HEAD].astype(jnp.float32)
        present = jnp.where(present > 0.5 * ABSENT, 0.0, 1.0)
        row = lax.broadcasted_iota(jnp.int32, (slots, slots), 0)
        column = lax.broadcasted_iota(jnp.int32, (slots, slots), 1)
        before = (column // SPAN < row // SPAN) & (column % SPAN == 0)
        before = jnp.where(before, 1.0, 0.0).astype(jnp.bfloat16)
        earlier = jnp.dot(before, present.astype(jnp.bfloat16), preferred_element_type=jnp.float32)
        rank = earlier[:, :1].astype(jnp.int32) + scalar_ref[1]
        target = lax.broadcasted_iota(jnp.int32, (slots, rows), 1)
        sender = lax.broadcasted_iota(jnp.int32, (slots, rows), 0)
        hit = (target // SPAN == rank) & (target % SPAN == sender % SPAN)
        hit = jnp.where(hit & (present[:, :1] > 0.5), 1.0, 0.0).astype(jnp.bfloat16)
        keep = table_ref[:, KEEP : KEEP + 1] > 0.5
        copies = []
        for i in range(4):
            lanes = slice(i * part, (i + 1) * part)
            came = lax.dot_general(
                hit,
                spans_ref[:, lanes],
                (((0,), (0,)), ((), ())),
                preferred_element_type=jnp.float32,
            )
            home = (mine_ref, other_ref)[i // 2][:, (i % 2) * part : (i % 2 + 1) * part]
            total_ref[i] = jnp.where(keep, home.astype(jnp.float32), came).astype(jnp.bfloat16)
            which = scalar_ref[0] if i < 2 else 1 - scalar_ref[0]
            at = pl.multiple_of((2 * (i % 2) + which) * part, HEAD)
            copies.append(
                pltpu.make_async_copy(total_ref.at[i], out_ref.at[:, pl.ds(at, part)], sems.at[i])
            )
            copies[-1].start()
        for copy in copies:
            copy.wait()

    home = pl.BlockSpec((rows, width // 2), lambda i, s: (0, 0))
    return pl.pallas_call(
        kernel,
        out_shape=jax.ShapeDtypeStruct((rows, width), jnp.bfloat16),
        grid_spec=pltpu.PrefetchScalarGridSpec(
            num_scalar_prefetch=1,
            grid=(1,),
            in_specs=[
                pl.BlockSpec((rows, table.shape[1]), lambda i, s: (0, 0)),
                home,
                home,
                pl.BlockSpec((slots, width), lambda i, s: (0, 0)),
            ],
            out_specs=pl.BlockSpec(memory_space=pl.ANY),
            scratch_shapes=[
                pltpu.VMEM((4, rows, part), jnp.bfloat16),
                pltpu.SemaphoreType.DMA((4,)),
            ],
        ),
        compiler_params=pltpu.CompilerParams(vmem_limit_bytes=LIMIT),
        cost_estimate=pl.CostEstimate(
            flops=2 * rows * slots * width,
            bytes_accessed=4 * rows * width,
            transcendentals=0,
        ),
    )(scalars, table, mine, other, spans)


def per_device(states, queries, kv_weight, kv_bias, lengths, bounds, balance):
    replicas = lax.axis_size("dp")
    own_index = lax.axis_index("dp")
    half = (lax.axis_index("group") % 2).astype(jnp.int32)[None]
    core = (own_index % 2).astype(jnp.int32)[None]
    own_y = own_index // 2 % 2
    own_z = own_index // 4
    ring = replicas // 4
    position = jnp.where(own_z % 2 == 0, own_z // 2, ring - 1 - own_z // 2)
    tokens = states.shape[0]
    depth, width = kv_weight.shape

    def block(offset, across):
        z = ring_place(ring, (position - offset + ring) % ring)
        return (z * 2 + (1 - own_y if across else own_y)).astype(jnp.int32)

    token_ids = jnp.arange(tokens, dtype=jnp.int32)
    is_live = token_ids < lengths[0] * SPAN
    owner = jnp.repeat(balance[0], SPAN)
    is_moved = is_live & (owner != own_index)
    destination = jnp.where(is_moved, owner, -1)
    keep = is_live & jnp.logical_not(is_moved)
    kept_count = jnp.sum(keep.astype(jnp.int32)) // SPAN
    chosen, rejected = bounds[0, 0], bounds[0, 1]
    segment = (token_ids >= chosen).astype(jnp.int32) + (token_ids >= rejected).astype(jnp.int32)
    place_ids = jnp.where(token_ids >= rejected, token_ids - (rejected - chosen), token_ids)
    target, source = token_ids[:, None], token_ids[None, :]
    near = (segment[None, :] == segment[:, None]) | (segment[None, :] == 0)
    allowed = ((source <= target) & is_live[None, :] & near) | (source == target)
    mask = jnp.where(allowed, 0.0, MASKED).astype(jnp.float32)
    frequency = jnp.exp(
        jnp.arange(HEAD // 2, dtype=jnp.float32) * (-2.0 * math.log(1000000.0) / HEAD)
    )
    angles = place_ids.astype(jnp.float32)[:, None] * frequency[None, :]
    columns = [jnp.cos(angles), jnp.sin(angles)]
    columns += [c.astype(jnp.float32)[:, None] for c in (is_live, destination, keep)]
    columns.append(jnp.zeros((tokens, HEAD - 3), jnp.float32))
    table = jnp.concatenate(columns, axis=1)
    scalars = jnp.stack([half[0], kept_count])
    plan = (table, mask, scalars)

    links = Links(replicas, lax.axis_size("group"))
    mine_weight, other_weight = halves(kv_weight, half)
    peer_columns = core_columns(states, 1 - core, depth)
    peer_states = core_swap(peer_columns, replicas)

    both = (peer_states, states)

    def listed(pieces):
        return jnp.stack([core[0], half[0]] + [b for _, b in pieces])

    fore = ring // 2
    order = [k for j in range(1, ring) for k in (j, -j)][: ring - 1]
    held = {0: mine_weight}
    mine = [(mine_weight, block(0, False))]
    other = [(other_weight, block(0, False))]
    middle, late = [], []
    crossed = links.send(mine_weight, "y")
    mine.append((crossed, block(0, True)))
    moving = other_weight
    for k in order:
        final = k == order[-1]
        nearer = held[k - 1] if k > 0 else held[k + 1]
        second = k == order[1]
        before = (peer_columns,) if second else plan if final else ()
        held[k] = links.send(nearer, "fore" if k > 0 else "back", before, lag=2 if second else None)
        mine.append((held[k], block(k, False)))
        crossed = links.send(held[k], "y")
        if 1 <= k < fore:
            other.append((links.send(held[k], "x"), block(k, False)))
        if final:
            early = mine + other
            sums = accumulate(
                both,
                listed(early),
                [p for p, _ in early],
                [0] * len(mine) + [1] * len(other),
                bias=kv_bias[None, :],
            )
            for j in range(1, ring - fore):
                moving = links.send(moving, "back")
                middle.append((moving, block(-j, False)))
            moving = links.send(moving, "back", sums)
            late.append((moving, block(fore - ring, False)))
            late.append((links.send(other_weight, "y", sums), block(0, True)))
            late.append((links.send(crossed, "x", sums), block(k, True)))
            middle = [(crossed, block(k, True))] + middle
            mine_peer, mine_own, other_peer, other_own, left_peer, left_own, pick = accumulate(
                both,
                listed(middle + late),
                [p for p, _ in middle],
                [0] + [1] * (len(middle) - 1),
                start=sums,
                later=len(late),
                table=table,
                rows=replicas * SPAN,
            )
        else:
            mine.append((crossed, block(k, True)))
            piece = (links.send(crossed, "x"), block(k, True))
            (middle if k == order[-2] else other).append(piece)

    mine_peer = core_swap(mine_peer, replicas)
    last = [p for p, _ in late]
    other_peer = core_swap(complete(left_peer, last, other_peer), replicas)
    other_own = complete(left_own, last, other_own)
    mine_own = after(mine_own, other_own)
    mine_kv, mine_spans = finish(mine_own, mine_peer, pick)
    other_kv, spans = finish(other_own, other_peer, pick, mine_spans)
    spans = spans.reshape(replicas, SPAN, width)
    spans = lax.all_to_all(spans, "dp", split_axis=0, concat_axis=0, tiled=True)
    spans = spans.reshape(replicas * SPAN, width)
    context = attend(half, False, mask, table, queries, mine_kv)
    context = attend(half, True, mask, table, queries, other_kv, context)
    work_rows = place(scalars, table, mine_kv, other_kv, spans)
    return (context, work_rows)


def solution(mesh):
    in_specs = (
        P(("group", "dp"), None),
        P(("group", "dp"), None),
        P("dp", None),
        P(),
        P(("group", "dp")),
        P(("group", "dp"), None),
        P(("group", "dp"), None),
    )
    out_specs = (P(("group", "dp"), None), P(("group", "dp"), None))
    return jax.shard_map(
        per_device, mesh=mesh, in_specs=in_specs, out_specs=out_specs, check_vma=False
    )
```

```python
import math

import jax
import jax.numpy as jnp
from jax import lax
from jax.experimental import pallas as pl
from jax.experimental.pallas import tpu as pltpu
from jax.sharding import PartitionSpec as P

HEAD = 128
SPAN = 8
HOME = 32
WORK = 24
ABSENT = 1e30
MASKED = -1e30
LIMIT = 18 << 20
LAG = {"x": 1, "y": 2, "z": 1}
LIVE, DESTINATION, KEEP = HEAD, HEAD + 1, HEAD + 2


def ring_place(ring, position):
    return jnp.where(2 * position < ring, 2 * position, 2 * (ring - 1 - position) + 1)


def after(value, *before):
    return lax.optimization_barrier((value, *before))[0] if before else value


class Links:
    def __init__(self, replicas, groups):
        ring = replicas // 4
        places = [p for p in range(0, ring, 2)] + [p for p in range(1, ring, 2)][::-1]
        ahead = {places[i]: places[(i + 1) % ring] for i in range(ring)}
        steps = [
            ((z * 2 + y) * 2 + c, (ahead[z] * 2 + y) * 2 + c)
            for z in range(ring)
            for y in range(2)
            for c in range(2)
        ]
        self.routes = {
            "fore": ("z", "dp", steps),
            "back": ("z", "dp", [(d, s) for s, d in steps]),
            "y": ("y", "dp", [(i, i ^ 2) for i in range(replicas)]),
            "x": ("x", "group", [(i, i ^ 1) for i in range(groups)]),
        }
        self.sent = {"x": [], "y": [], "z": []}

    def send(self, value, route, before=(), lag=None):
        link, axis, pairs = self.routes[route]
        sent = self.sent[link]
        lag = LAG[link] if lag is None else lag
        if len(sent) >= lag:
            before = (sent[-lag], *before)
        sent.append(lax.ppermute(after(value, *before), axis, pairs))
        return sent[-1]


def core_swap(value, replicas):
    return lax.ppermute(value, "dp", [(i, i ^ 1) for i in range(replicas)])


def head_pair(weight, half, flip):
    depth, width = weight.shape
    quarter = width // 4

    def kernel(half_ref, weight_ref, out_ref, sems):
        which = 1 - half_ref[0] if flip else half_ref[0]
        copies = [
            pltpu.make_async_copy(
                weight_ref.at[:, pl.ds(pl.multiple_of((2 * j + which) * quarter, HEAD), quarter)],
                out_ref.at[:, pl.ds(j * quarter, quarter)],
                sems.at[j],
            )
            for j in range(2)
        ]
        for copy in copies:
            copy.start()
        for copy in copies:
            copy.wait()

    return pl.pallas_call(
        kernel,
        out_shape=jax.ShapeDtypeStruct((depth, width // 2), weight.dtype),
        in_specs=[pl.BlockSpec(memory_space=pltpu.SMEM), pl.BlockSpec(memory_space=pl.ANY)],
        out_specs=pl.BlockSpec(memory_space=pltpu.VMEM),
        scratch_shapes=[pltpu.SemaphoreType.DMA((2,))],
        cost_estimate=pl.CostEstimate(
            flops=0, bytes_accessed=2 * depth * width, transcendentals=0
        ),
    )(half, weight)


def core_columns(states, core, depth):
    tokens, width = states.shape
    count = width // (2 * depth)

    def kernel(core_ref, states_ref, out_ref, sems):
        copies = []
        for i in range(count):
            start = pl.multiple_of((2 * i + core_ref[0]) * depth, HEAD)
            copies.append(
                pltpu.make_async_copy(
                    states_ref.at[:, pl.ds(start, depth)],
                    out_ref.at[:, pl.ds(i * depth, depth)],
                    sems.at[i],
                )
            )
        for copy in copies:
            copy.start()
        for copy in copies:
            copy.wait()

    anywhere = pl.BlockSpec(memory_space=pl.ANY)
    return pl.pallas_call(
        kernel,
        out_shape=jax.ShapeDtypeStruct((tokens, width // 2), states.dtype),
        in_specs=[pl.BlockSpec(memory_space=pltpu.SMEM), anywhere],
        out_specs=pl.BlockSpec(memory_space=pltpu.VMEM),
        scratch_shapes=[pltpu.SemaphoreType.DMA((count,))],
        cost_estimate=pl.CostEstimate(
            flops=0, bytes_accessed=2 * tokens * width, transcendentals=0
        ),
    )(core, states)


def accumulate(states, scalars, pieces, places, bias=None, start=None, later=0, table=None, rows=0):
    count = len(pieces)
    depth, columns = pieces[0].shape
    tokens = states[0].shape[0]
    batch = 5
    begun = 4 if start is not None else 1

    def kernel(scalar_ref, *refs):
        state_refs, refs = refs[:2], refs[2:]
        piece_refs, refs = refs[:count], refs[count:]
        start_refs, refs = refs[:begun], refs[begun:]
        if later:
            table_in, totals, lefts, pick_ref = refs[0], refs[1:5], refs[5:7], refs[7]
            table_ref, refs = refs[8], refs[9:]
        else:
            outs, totals, refs = refs[:4], refs[4:8], refs[8:]
        left, right, bias_ref, sems = refs
        used = 0

        def begin(source, target):
            nonlocal used
            copy = pltpu.make_async_copy(source, target, sems.at[used])
            copy.start()
            used += 1
            return copy

        def columns_at(side, index):
            at = scalar_ref[2 + index]
            at = 2 * at + scalar_ref[0] if side else at
            return state_refs[side].at[:, pl.ds(pl.multiple_of(at * depth, HEAD), depth)]

        waits = []
        if start is None:
            first = [begin(start_refs[0], bias_ref)]
        else:
            first = [begin(source, target) for source, target in zip(start_refs, totals)]
        for i in range(count):
            deep = pl.ds(i * depth, depth)
            waits.append(
                [begin(piece_refs[i], right.at[deep])]
                + [begin(columns_at(side, i), left.at[side, :, deep]) for side in range(2)]
            )
        rest = [
            begin(columns_at(side, count + i), lefts[side].at[:, pl.ds(i * depth, depth)])
            for i in range(later)
            for side in range(2)
        ]
        if later:
            table_copy = begin(table_in, table_ref)
        for copy in first:
            copy.wait()
        if later:
            table_copy.wait()
            destination = table_ref[:, DESTINATION : DESTINATION + 1].astype(jnp.int32)
            token = lax.broadcasted_iota(jnp.int32, (tokens, rows), 0)
            row = lax.broadcasted_iota(jnp.int32, (tokens, rows), 1)
            match = (destination == row // SPAN) & (token % SPAN == row % SPAN)
            pick_ref[...] = jnp.where(match, 1.0, 0.0).astype(jnp.bfloat16)
        touched = [start is not None] * 4
        for i in range(0, count, batch):
            stop = min(i + batch, count)
            for copies in waits[i:stop]:
                for copy in copies:
                    copy.wait()
            for j in range(i, stop):
                deep = slice(j * depth, (j + 1) * depth)
                for side in range(2):
                    which = 2 * places[j] + side
                    part = jnp.dot(
                        left[side, :, deep], right[deep], preferred_element_type=jnp.float32
                    )
                    if touched[which]:
                        totals[which][...] += part
                    elif side == 0:
                        totals[which][...] = part
                    else:
                        own = scalar_ref[1] if places[j] == 0 else 1 - scalar_ref[1]
                        part_width = columns // 2
                        for k in range(2):
                            at = pl.multiple_of((2 * k + own) * part_width, HEAD)
                            lanes = slice(k * part_width, (k + 1) * part_width)
                            totals[which][:, lanes] = (
                                part[:, lanes] + bias_ref[:, pl.ds(at, part_width)]
                            )
                    touched[which] = True
        if not later:
            rest += [begin(source, target) for source, target in zip(totals, outs)]
        for copy in rest:
            copy.wait()

    outside = pl.BlockSpec(memory_space=pltpu.HBM)
    inside = pl.BlockSpec(memory_space=pltpu.VMEM)
    sums = (tokens, columns)
    if later:
        out_shape = [jax.ShapeDtypeStruct(sums, jnp.float32)] * 4
        out_shape += [jax.ShapeDtypeStruct((tokens, later * depth), jnp.bfloat16)] * 2
        out_shape += [jax.ShapeDtypeStruct((tokens, rows), jnp.bfloat16)]
        out_specs, scratch = [inside] * 7, [pltpu.VMEM(table.shape, table.dtype)]
    else:
        out_shape = [pltpu.HBM(sums, jnp.float32)] * 4
        out_specs, scratch = [outside] * 4, [pltpu.VMEM(sums, jnp.float32)] * 4
    outer = [*states, *pieces, *((bias,) if start is None else start)]
    outer += [table] if later else []
    return pl.pallas_call(
        kernel,
        out_shape=out_shape,
        in_specs=[pl.BlockSpec(memory_space=pltpu.SMEM)] + [outside] * len(outer),
        out_specs=out_specs,
        scratch_shapes=scratch
        + [
            pltpu.VMEM((2, tokens, count * depth), jnp.bfloat16),
            pltpu.VMEM((count * depth, columns), jnp.bfloat16),
            pltpu.VMEM((1, 2 * columns), jnp.float32),
            pltpu.SemaphoreType.DMA((3 * count + 2 * later + 8,)),
        ],
        compiler_params=pltpu.CompilerParams(vmem_limit_bytes=LIMIT),
        cost_estimate=pl.CostEstimate(
            flops=4 * count * tokens * depth * columns,
            bytes_accessed=count * (4 * tokens * depth + 2 * depth * columns),
            transcendentals=0,
        ),
    )(scalars, *(pltpu.with_memory_space_constraint(a, pltpu.HBM) for a in outer))


def complete(left, pieces, total):
    depth = pieces[0].shape[0]

    def kernel(left_ref, total_ref, *refs):
        out_ref = refs[-1]
        for i, piece in enumerate(refs[:-1]):
            part = jnp.dot(
                left_ref[:, i * depth : (i + 1) * depth],
                piece[...],
                preferred_element_type=jnp.float32,
            )
            out_ref[...] = (total_ref if i == 0 else out_ref)[...] + part

    inside = pl.BlockSpec(memory_space=pltpu.VMEM)
    return pl.pallas_call(
        kernel,
        out_shape=jax.ShapeDtypeStruct(total.shape, total.dtype),
        in_specs=[inside] * (2 + len(pieces)),
        out_specs=inside,
        compiler_params=pltpu.CompilerParams(vmem_limit_bytes=LIMIT),
        cost_estimate=pl.CostEstimate(
            flops=2 * left.size * total.shape[1],
            bytes_accessed=2 * left.size,
            transcendentals=0,
        ),
    )(left, total, *pieces)


def finish(own_part, peer_part, pick, earlier=None):
    tokens, columns = own_part.shape
    rows = pick.shape[1]
    last = earlier is not None

    def kernel(own_ref, peer_ref, pick_ref, *refs):
        if last:
            earlier_ref, kv_ref, out_ref, spans_ref, sems = refs
            first = pltpu.make_async_copy(
                earlier_ref, out_ref.at[:, pl.ds(0, columns)], sems.at[0]
            )
            first.start()
        else:
            kv_ref, spans_ref = refs
        kv = (own_ref[...] + peer_ref[...]).astype(jnp.bfloat16)
        kv_ref[...] = kv
        over_tokens = (((0,), (0,)), ((), ()))
        found = lax.dot_general(
            pick_ref[...],
            jnp.ones((tokens, HEAD), jnp.bfloat16),
            over_tokens,
            preferred_element_type=jnp.float32,
        )
        spans = lax.dot_general(
            pick_ref[...], kv, over_tokens, preferred_element_type=jnp.float32
        )
        spans_ref[...] = jnp.where(found[:, :1] > 0.5, spans, ABSENT).astype(jnp.bfloat16)
        if last:
            second = pltpu.make_async_copy(
                spans_ref, out_ref.at[:, pl.ds(columns, columns)], sems.at[1]
            )
            second.start()
            first.wait()
            second.wait()

    inside = pl.BlockSpec(memory_space=pltpu.VMEM)
    kv_shape = jax.ShapeDtypeStruct((tokens, columns), jnp.bfloat16)
    if last:
        out_shape = (kv_shape, pltpu.HBM((rows, 2 * columns), jnp.bfloat16))
        out_specs = (inside, pl.BlockSpec(memory_space=pltpu.HBM))
        scratch = [pltpu.VMEM((rows, columns), jnp.bfloat16), pltpu.SemaphoreType.DMA((2,))]
    else:
        out_shape = (kv_shape, jax.ShapeDtypeStruct((rows, columns), jnp.bfloat16))
        out_specs, scratch = (inside, inside), []
    more = (earlier,) if last else ()
    return pl.pallas_call(
        kernel,
        out_shape=out_shape,
        in_specs=[inside] * (3 + len(more)),
        out_specs=out_specs,
        scratch_shapes=scratch,
        compiler_params=pltpu.CompilerParams(vmem_limit_bytes=LIMIT),
        cost_estimate=pl.CostEstimate(
            flops=2 * rows * tokens * columns,
            bytes_accessed=10 * tokens * columns,
            transcendentals=0,
        ),
    )(own_part, peer_part, pick, *more)


def attend(half, flip, mask, table, queries, kv, context=None):
    tokens = queries.shape[0]
    heads = kv.shape[1] // (2 * HEAD)
    width = queries.shape[1] // (2 * heads)

    def kernel(half_ref, mask_ref, table_ref, query_ref, key_ref, value_ref, *refs):
        context_ref = refs[-1]
        scale = HEAD**-0.5 * math.log2(math.e)
        lanes = [slice(h * HEAD, (h + 1) * HEAD) for h in range(width // HEAD)]
        is_live = table_ref[:, LIVE : LIVE + 1] > 0.5
        cosine, sine = table_ref[:, : HEAD // 2], table_ref[:, HEAD // 2 : HEAD]
        cosine = jnp.concatenate([cosine, cosine], axis=1)
        sine = jnp.concatenate([-sine, sine], axis=1)
        key = jnp.where(is_live, key_ref[...].astype(jnp.float32), 0.0)
        key = (key * cosine + pltpu.roll(key, HEAD // 2, 1) * sine).astype(jnp.bfloat16)
        value = jnp.where(is_live, value_ref[...].astype(jnp.float32), 0.0).astype(jnp.bfloat16)
        scores = [
            lax.dot_general(
                query_ref[:, lane],
                key,
                (((1,), (1,)), ((), ())),
                preferred_element_type=jnp.float32,
            )
            for lane in lanes
        ]
        weights = []
        for score in scores:
            score = score * scale + mask_ref[...]
            weight = jnp.exp2(score - jnp.max(score, axis=1, keepdims=True))
            inverse = 1.0 / jnp.sum(weight, axis=1, keepdims=True)
            weights.append((weight * inverse).astype(jnp.bfloat16))
        for lane, weight in zip(lanes, weights):
            mixed = jnp.dot(weight, value, preferred_element_type=jnp.float32)
            context_ref[:, lane] = jnp.where(is_live, mixed, 0.0).astype(jnp.bfloat16)

    def wide_at(i, s):
        return (0, (1 - s[0] if flip else s[0]) * heads + i)

    in_specs = [
        pl.BlockSpec((tokens, tokens), lambda i, s: (0, 0)),
        pl.BlockSpec(table.shape, lambda i, s: (0, 0)),
        pl.BlockSpec((tokens, width), wide_at),
        pl.BlockSpec((tokens, HEAD), lambda i, s: (0, i)),
        pl.BlockSpec((tokens, HEAD), lambda i, s: (0, heads + i)),
    ]
    arguments = [half, mask, table, queries, kv, kv]
    if context is not None:
        in_specs.append(pl.BlockSpec(memory_space=pl.ANY))
        arguments.append(context)
    return pl.pallas_call(
        kernel,
        out_shape=jax.ShapeDtypeStruct(queries.shape, jnp.bfloat16),
        grid_spec=pltpu.PrefetchScalarGridSpec(
            num_scalar_prefetch=1,
            grid=(heads,),
            in_specs=in_specs,
            out_specs=pl.BlockSpec((tokens, width), wide_at),
        ),
        input_output_aliases={} if context is None else {6: 0},
        compiler_params=pltpu.CompilerParams(vmem_limit_bytes=LIMIT),
        cost_estimate=pl.CostEstimate(
            flops=4 * tokens * tokens * heads * width,
            bytes_accessed=4 * tokens * heads * width,
            transcendentals=tokens * tokens * heads * width // HEAD,
        ),
    )(*arguments)


def place(scalars, table, mine, other, spans):
    rows = WORK * SPAN
    slots, width = spans.shape
    part = width // 4

    def kernel(scalar_ref, table_ref, mine_ref, other_ref, spans_ref, out_ref, total_ref, sems):
        present = spans_ref[:, :HEAD].astype(jnp.float32)
        present = jnp.where(present > 0.5 * ABSENT, 0.0, 1.0)
        row = lax.broadcasted_iota(jnp.int32, (slots, 2 * slots), 0)
        column = lax.broadcasted_iota(jnp.int32, (slots, 2 * slots), 1)
        before = (row // SPAN < column // SPAN) & (row % SPAN == 0)
        counts = ((column < slots) & before) | (row == column - slots)
        counts = lax.dot_general(
            present.astype(jnp.bfloat16),
            jnp.where(counts, 1.0, 0.0).astype(jnp.bfloat16),
            (((0,), (0,)), ((), ())),
            preferred_element_type=jnp.float32,
        )
        rank = counts[:1, :slots].astype(jnp.int32) + scalar_ref[1]
        target = lax.broadcasted_iota(jnp.int32, (rows, slots), 0)
        sender = lax.broadcasted_iota(jnp.int32, (rows, slots), 1)
        hit = (target // SPAN == rank) & (target % SPAN == sender % SPAN)
        hit = jnp.where(hit & (counts[:1, slots:] > 0.5), 1.0, 0.0).astype(jnp.bfloat16)
        keep = table_ref[:, KEEP : KEEP + 1] > 0.5
        copies = []
        for i in range(4):
            lanes = slice(i * part, (i + 1) * part)
            came = jnp.dot(hit, spans_ref[:, lanes], preferred_element_type=jnp.float32)
            home = (mine_ref, other_ref)[i // 2][:, (i % 2) * part : (i % 2 + 1) * part]
            total_ref[i] = jnp.where(keep, home.astype(jnp.float32), came).astype(jnp.bfloat16)
            which = scalar_ref[0] if i < 2 else 1 - scalar_ref[0]
            at = pl.multiple_of((2 * (i % 2) + which) * part, HEAD)
            copies.append(
                pltpu.make_async_copy(total_ref.at[i], out_ref.at[:, pl.ds(at, part)], sems.at[i])
            )
            copies[-1].start()
        for copy in copies:
            copy.wait()

    home = pl.BlockSpec((rows, width // 2), lambda i, s: (0, 0))
    return pl.pallas_call(
        kernel,
        out_shape=jax.ShapeDtypeStruct((rows, width), jnp.bfloat16),
        grid_spec=pltpu.PrefetchScalarGridSpec(
            num_scalar_prefetch=1,
            grid=(1,),
            in_specs=[
                pl.BlockSpec((rows, table.shape[1]), lambda i, s: (0, 0)),
                home,
                home,
                pl.BlockSpec((slots, width), lambda i, s: (0, 0)),
            ],
            out_specs=pl.BlockSpec(memory_space=pl.ANY),
            scratch_shapes=[
                pltpu.VMEM((4, rows, part), jnp.bfloat16),
                pltpu.SemaphoreType.DMA((4,)),
            ],
        ),
        compiler_params=pltpu.CompilerParams(vmem_limit_bytes=LIMIT),
        cost_estimate=pl.CostEstimate(
            flops=2 * rows * slots * width,
            bytes_accessed=4 * rows * width,
            transcendentals=0,
        ),
    )(scalars, table, mine, other, spans)


def per_device(states, queries, kv_weight, kv_bias, lengths, bounds, balance):
    replicas = lax.axis_size("dp")
    own_index = lax.axis_index("dp")
    half = (lax.axis_index("group") % 2).astype(jnp.int32)[None]
    core = (own_index % 2).astype(jnp.int32)[None]
    own_y = own_index // 2 % 2
    own_z = own_index // 4
    ring = replicas // 4
    position = jnp.where(own_z % 2 == 0, own_z // 2, ring - 1 - own_z // 2)
    tokens = states.shape[0]
    depth, width = kv_weight.shape

    def block(offset, across):
        z = ring_place(ring, (position - offset + ring) % ring)
        return (z * 2 + (1 - own_y if across else own_y)).astype(jnp.int32)

    token_ids = jnp.arange(tokens, dtype=jnp.int32)
    is_live = token_ids < lengths[0] * SPAN
    owner = jnp.repeat(balance[0], SPAN)
    is_moved = is_live & (owner != own_index)
    destination = jnp.where(is_moved, owner, -1)
    keep = is_live & jnp.logical_not(is_moved)
    kept_count = jnp.sum(keep.astype(jnp.int32)) // SPAN
    chosen, rejected = bounds[0, 0], bounds[0, 1]
    segment = (token_ids >= chosen).astype(jnp.int32) + (token_ids >= rejected).astype(jnp.int32)
    place_ids = jnp.where(token_ids >= rejected, token_ids - (rejected - chosen), token_ids)
    target, source = token_ids[:, None], token_ids[None, :]
    near = (segment[None, :] == segment[:, None]) | (segment[None, :] == 0)
    allowed = ((source <= target) & is_live[None, :] & near) | (source == target)
    mask = jnp.where(allowed, 0.0, MASKED).astype(jnp.float32)
    frequency = jnp.exp(
        jnp.arange(HEAD // 2, dtype=jnp.float32) * (-2.0 * math.log(1000000.0) / HEAD)
    )
    angles = place_ids.astype(jnp.float32)[:, None] * frequency[None, :]
    columns = [jnp.cos(angles), jnp.sin(angles)]
    columns += [c.astype(jnp.float32)[:, None] for c in (is_live, destination, keep)]
    columns.append(jnp.zeros((tokens, HEAD - 3), jnp.float32))
    table = jnp.concatenate(columns, axis=1)
    scalars = jnp.stack([half[0], kept_count])
    plan = (table, mask, scalars)

    links = Links(replicas, lax.axis_size("group"))
    mine_weight = head_pair(kv_weight, half, False)
    other_weight = head_pair(kv_weight, half, True)
    peer_columns = core_columns(states, 1 - core, depth)
    peer_states = core_swap(peer_columns, replicas)

    both = (peer_states, states)

    def listed(pieces):
        return jnp.stack([core[0], half[0]] + [b for _, b in pieces])

    fore = ring // 2
    order = [k for j in range(1, ring) for k in (j, -j)][: ring - 1]
    held = {0: mine_weight}
    mine = [(mine_weight, block(0, False))]
    other = [(other_weight, block(0, False))]
    middle, late = [], []
    crossed = links.send(mine_weight, "y")
    mine.append((crossed, block(0, True)))
    moving = other_weight
    for k in order:
        final = k == order[-1]
        nearer = held[k - 1] if k > 0 else held[k + 1]
        second = k == order[1]
        before = (peer_columns,) if second else plan if final else ()
        held[k] = links.send(nearer, "fore" if k > 0 else "back", before, lag=2 if second else None)
        mine.append((held[k], block(k, False)))
        crossed = links.send(held[k], "y")
        if 1 <= k < fore:
            other.append((links.send(held[k], "x"), block(k, False)))
        if final:
            early = mine + other
            sums = accumulate(
                both,
                listed(early),
                [p for p, _ in early],
                [0] * len(mine) + [1] * len(other),
                bias=kv_bias[None, :],
            )
            for j in range(1, ring - fore):
                moving = links.send(moving, "back")
                middle.append((moving, block(-j, False)))
            moving = links.send(moving, "back", sums)
            late.append((moving, block(fore - ring, False)))
            late.append((links.send(other_weight, "y"), block(0, True)))
            late.append((links.send(crossed, "x", sums), block(k, True)))
            middle = [(crossed, block(k, True))] + middle
            mine_peer, mine_own, other_peer, other_own, left_peer, left_own, pick = accumulate(
                both,
                listed(middle + late),
                [p for p, _ in middle],
                [0] + [1] * (len(middle) - 1),
                start=sums,
                later=len(late),
                table=table,
                rows=replicas * SPAN,
            )
        else:
            mine.append((crossed, block(k, True)))
            piece = (links.send(crossed, "x"), block(k, True))
            (middle if k == order[-2] else other).append(piece)

    mine_peer = core_swap(mine_peer, replicas)
    last = [p for p, _ in late]
    other_peer = core_swap(complete(left_peer, last, other_peer), replicas)
    other_own = complete(left_own, last, other_own)
    mine_own = after(mine_own, other_own)
    mine_kv, mine_spans = finish(mine_own, mine_peer, pick)
    other_kv, spans = finish(other_own, other_peer, pick, mine_spans)
    spans = spans.reshape(replicas, SPAN, width)
    spans = lax.all_to_all(spans, "dp", split_axis=0, concat_axis=0, tiled=True)
    spans = spans.reshape(replicas * SPAN, width)
    context = attend(half, False, mask, table, queries, mine_kv)
    context = attend(half, True, mask, table, queries, other_kv, context)
    work_rows = place(scalars, table, mine_kv, other_kv, spans)
    return (context, work_rows)


def solution(mesh):
    in_specs = (
        P(("group", "dp"), None),
        P(("group", "dp"), None),
        P("dp", None),
        P(),
        P(("group", "dp")),
        P(("group", "dp"), None),
        P(("group", "dp"), None),
    )
    out_specs = (P(("group", "dp"), None), P(("group", "dp"), None))
    return jax.shard_map(
        per_device, mesh=mesh, in_specs=in_specs, out_specs=out_specs, check_vma=False
    )
```

```python
import math

import jax
import jax.numpy as jnp
from jax import lax
from jax.experimental import pallas as pl
from jax.experimental.pallas import tpu as pltpu
from jax.sharding import PartitionSpec as P

HEAD = 128
SPAN = 8
HOME = 32
WORK = 24
ABSENT = 1e30
MASKED = -1e30
LIMIT = 18 << 20
LAG = {"x": 1, "y": 2, "z": 1}
LIVE, DESTINATION, KEEP = HEAD, HEAD + 1, HEAD + 2


def ring_place(ring, position):
    return jnp.where(2 * position < ring, 2 * position, 2 * (ring - 1 - position) + 1)


def after(value, *before):
    return lax.optimization_barrier((value, *before))[0] if before else value


class Links:
    def __init__(self, replicas, groups):
        ring = replicas // 4
        places = [p for p in range(0, ring, 2)] + [p for p in range(1, ring, 2)][::-1]
        ahead = {places[i]: places[(i + 1) % ring] for i in range(ring)}
        steps = [
            ((z * 2 + y) * 2 + c, (ahead[z] * 2 + y) * 2 + c)
            for z in range(ring)
            for y in range(2)
            for c in range(2)
        ]
        self.routes = {
            "fore": ("z", "dp", steps),
            "back": ("z", "dp", [(d, s) for s, d in steps]),
            "y": ("y", "dp", [(i, i ^ 2) for i in range(replicas)]),
            "x": ("x", "group", [(i, i ^ 1) for i in range(groups)]),
        }
        self.sent = {"x": [], "y": [], "z": []}

    def send(self, value, route, before=(), lag=None):
        link, axis, pairs = self.routes[route]
        sent = self.sent[link]
        lag = LAG[link] if lag is None else lag
        if len(sent) >= lag:
            before = (sent[-lag], *before)
        sent.append(lax.ppermute(after(value, *before), axis, pairs))
        return sent[-1]


def core_swap(value, replicas):
    return lax.ppermute(value, "dp", [(i, i ^ 1) for i in range(replicas)])


def head_pair(weight, half, flip):
    depth, width = weight.shape
    quarter = width // 4

    def kernel(half_ref, weight_ref, out_ref, sems):
        which = 1 - half_ref[0] if flip else half_ref[0]
        copies = [
            pltpu.make_async_copy(
                weight_ref.at[:, pl.ds(pl.multiple_of((2 * j + which) * quarter, HEAD), quarter)],
                out_ref.at[:, pl.ds(j * quarter, quarter)],
                sems.at[j],
            )
            for j in range(2)
        ]
        for copy in copies:
            copy.start()
        for copy in copies:
            copy.wait()

    return pl.pallas_call(
        kernel,
        out_shape=jax.ShapeDtypeStruct((depth, width // 2), weight.dtype),
        in_specs=[pl.BlockSpec(memory_space=pltpu.SMEM), pl.BlockSpec(memory_space=pl.ANY)],
        out_specs=pl.BlockSpec(memory_space=pltpu.VMEM),
        scratch_shapes=[pltpu.SemaphoreType.DMA((2,))],
        cost_estimate=pl.CostEstimate(
            flops=0, bytes_accessed=2 * depth * width, transcendentals=0
        ),
    )(half, weight)


def core_columns(states, core, depth):
    tokens, width = states.shape
    count = width // (2 * depth)

    def kernel(core_ref, states_ref, out_ref, sems):
        copies = []
        for i in range(count):
            start = pl.multiple_of((2 * i + core_ref[0]) * depth, HEAD)
            copies.append(
                pltpu.make_async_copy(
                    states_ref.at[:, pl.ds(start, depth)],
                    out_ref.at[:, pl.ds(i * depth, depth)],
                    sems.at[i],
                )
            )
        for copy in copies:
            copy.start()
        for copy in copies:
            copy.wait()

    anywhere = pl.BlockSpec(memory_space=pl.ANY)
    return pl.pallas_call(
        kernel,
        out_shape=jax.ShapeDtypeStruct((tokens, width // 2), states.dtype),
        in_specs=[pl.BlockSpec(memory_space=pltpu.SMEM), anywhere],
        out_specs=pl.BlockSpec(memory_space=pltpu.VMEM),
        scratch_shapes=[pltpu.SemaphoreType.DMA((count,))],
        cost_estimate=pl.CostEstimate(
            flops=0, bytes_accessed=2 * tokens * width, transcendentals=0
        ),
    )(core, states)


def accumulate(states, scalars, pieces, places, bias=None, start=None, later=0, table=None, rows=0):
    count = len(pieces)
    depth, columns = pieces[0].shape
    tokens = states[0].shape[0]
    batch = 5
    begun = 4 if start is not None else 1

    def kernel(scalar_ref, *refs):
        state_refs, refs = refs[:2], refs[2:]
        piece_refs, refs = refs[:count], refs[count:]
        start_refs, refs = refs[:begun], refs[begun:]
        if later:
            table_in, totals, lefts, pick_ref = refs[0], refs[1:5], refs[5:7], refs[7]
            table_ref, refs = refs[8], refs[9:]
        else:
            outs, totals, refs = refs[:4], refs[4:8], refs[8:]
        left, right, bias_ref, sems = refs
        used = 0

        def begin(source, target):
            nonlocal used
            copy = pltpu.make_async_copy(source, target, sems.at[used])
            copy.start()
            used += 1
            return copy

        def columns_at(side, index):
            at = scalar_ref[2 + index]
            at = 2 * at + scalar_ref[0] if side else at
            return state_refs[side].at[:, pl.ds(pl.multiple_of(at * depth, HEAD), depth)]

        waits = []
        if start is None:
            first = [begin(start_refs[0], bias_ref)]
        else:
            first = [begin(source, target) for source, target in zip(start_refs, totals)]
        for i in range(count):
            deep = pl.ds(i * depth, depth)
            waits.append(
                [begin(piece_refs[i], right.at[deep])]
                + [begin(columns_at(side, i), left.at[side, :, deep]) for side in range(2)]
            )
        rest = [
            begin(columns_at(side, count + i), lefts[side].at[:, pl.ds(i * depth, depth)])
            for i in range(later)
            for side in range(2)
        ]
        if later:
            table_copy = begin(table_in, table_ref)
        for copy in first:
            copy.wait()
        if later:
            table_copy.wait()
            destination = table_ref[:, DESTINATION : DESTINATION + 1].astype(jnp.int32)
            token = lax.broadcasted_iota(jnp.int32, (tokens, rows), 0)
            row = lax.broadcasted_iota(jnp.int32, (tokens, rows), 1)
            match = (destination == row // SPAN) & (token % SPAN == row % SPAN)
            pick_ref[...] = jnp.where(match, 1.0, 0.0).astype(jnp.bfloat16)
        touched = [start is not None] * 4
        for i in range(0, count, batch):
            stop = min(i + batch, count)
            for copies in waits[i:stop]:
                for copy in copies:
                    copy.wait()
            for j in range(i, stop):
                deep = slice(j * depth, (j + 1) * depth)
                for side in range(2):
                    which = 2 * places[j] + side
                    part = jnp.dot(
                        left[side, :, deep], right[deep], preferred_element_type=jnp.float32
                    )
                    if touched[which]:
                        totals[which][...] += part
                    elif side == 0:
                        totals[which][...] = part
                    else:
                        own = scalar_ref[1] if places[j] == 0 else 1 - scalar_ref[1]
                        part_width = columns // 2
                        for k in range(2):
                            at = pl.multiple_of((2 * k + own) * part_width, HEAD)
                            lanes = slice(k * part_width, (k + 1) * part_width)
                            totals[which][:, lanes] = (
                                part[:, lanes] + bias_ref[:, pl.ds(at, part_width)]
                            )
                    touched[which] = True
        if not later:
            rest += [begin(source, target) for source, target in zip(totals, outs)]
        for copy in rest:
            copy.wait()

    outside = pl.BlockSpec(memory_space=pltpu.HBM)
    inside = pl.BlockSpec(memory_space=pltpu.VMEM)
    sums = (tokens, columns)
    if later:
        out_shape = [jax.ShapeDtypeStruct(sums, jnp.float32)] * 4
        out_shape += [jax.ShapeDtypeStruct((tokens, later * depth), jnp.bfloat16)] * 2
        out_shape += [jax.ShapeDtypeStruct((tokens, rows), jnp.bfloat16)]
        out_specs, scratch = [inside] * 7, [pltpu.VMEM(table.shape, table.dtype)]
    else:
        out_shape = [pltpu.HBM(sums, jnp.float32)] * 4
        out_specs, scratch = [outside] * 4, [pltpu.VMEM(sums, jnp.float32)] * 4
    outer = [*states, *pieces, *((bias,) if start is None else start)]
    outer += [table] if later else []
    return pl.pallas_call(
        kernel,
        out_shape=out_shape,
        in_specs=[pl.BlockSpec(memory_space=pltpu.SMEM)] + [outside] * len(outer),
        out_specs=out_specs,
        scratch_shapes=scratch
        + [
            pltpu.VMEM((2, tokens, count * depth), jnp.bfloat16),
            pltpu.VMEM((count * depth, columns), jnp.bfloat16),
            pltpu.VMEM((1, 2 * columns), jnp.float32),
            pltpu.SemaphoreType.DMA((3 * count + 2 * later + 8,)),
        ],
        compiler_params=pltpu.CompilerParams(vmem_limit_bytes=LIMIT),
        cost_estimate=pl.CostEstimate(
            flops=4 * count * tokens * depth * columns,
            bytes_accessed=count * (4 * tokens * depth + 2 * depth * columns),
            transcendentals=0,
        ),
    )(scalars, *(pltpu.with_memory_space_constraint(a, pltpu.HBM) for a in outer))


def complete(left, pieces, total):
    depth = pieces[0].shape[0]

    def kernel(left_ref, total_ref, *refs):
        out_ref = refs[-1]
        for i, piece in enumerate(refs[:-1]):
            part = jnp.dot(
                left_ref[:, i * depth : (i + 1) * depth],
                piece[...],
                preferred_element_type=jnp.float32,
            )
            out_ref[...] = (total_ref if i == 0 else out_ref)[...] + part

    inside = pl.BlockSpec(memory_space=pltpu.VMEM)
    return pl.pallas_call(
        kernel,
        out_shape=jax.ShapeDtypeStruct(total.shape, total.dtype),
        in_specs=[inside] * (2 + len(pieces)),
        out_specs=inside,
        compiler_params=pltpu.CompilerParams(vmem_limit_bytes=LIMIT),
        cost_estimate=pl.CostEstimate(
            flops=2 * left.size * total.shape[1],
            bytes_accessed=2 * left.size,
            transcendentals=0,
        ),
    )(left, total, *pieces)


def finish(own_part, peer_part, pick, earlier=None):
    tokens, columns = own_part.shape
    rows = pick.shape[1]
    last = earlier is not None

    def kernel(own_ref, peer_ref, pick_ref, *refs):
        if last:
            earlier_ref, kv_ref, out_ref, spans_ref, sems = refs
            first = pltpu.make_async_copy(
                earlier_ref, out_ref.at[:, pl.ds(0, columns)], sems.at[0]
            )
            first.start()
        else:
            kv_ref, spans_ref = refs
        kv = (own_ref[...] + peer_ref[...]).astype(jnp.bfloat16)
        kv_ref[...] = kv
        over_tokens = (((0,), (0,)), ((), ()))
        found = lax.dot_general(
            pick_ref[...],
            jnp.ones((tokens, HEAD), jnp.bfloat16),
            over_tokens,
            preferred_element_type=jnp.float32,
        )
        spans = lax.dot_general(
            pick_ref[...], kv, over_tokens, preferred_element_type=jnp.float32
        )
        spans_ref[...] = jnp.where(found[:, :1] > 0.5, spans, ABSENT).astype(jnp.bfloat16)
        if last:
            second = pltpu.make_async_copy(
                spans_ref, out_ref.at[:, pl.ds(columns, columns)], sems.at[1]
            )
            second.start()
            first.wait()
            second.wait()

    inside = pl.BlockSpec(memory_space=pltpu.VMEM)
    kv_shape = jax.ShapeDtypeStruct((tokens, columns), jnp.bfloat16)
    if last:
        out_shape = (kv_shape, pltpu.HBM((rows, 2 * columns), jnp.bfloat16))
        out_specs = (inside, pl.BlockSpec(memory_space=pltpu.HBM))
        scratch = [pltpu.VMEM((rows, columns), jnp.bfloat16), pltpu.SemaphoreType.DMA((2,))]
    else:
        out_shape = (kv_shape, jax.ShapeDtypeStruct((rows, columns), jnp.bfloat16))
        out_specs, scratch = (inside, inside), []
    more = (earlier,) if last else ()
    return pl.pallas_call(
        kernel,
        out_shape=out_shape,
        in_specs=[inside] * (3 + len(more)),
        out_specs=out_specs,
        scratch_shapes=scratch,
        compiler_params=pltpu.CompilerParams(vmem_limit_bytes=LIMIT),
        cost_estimate=pl.CostEstimate(
            flops=2 * rows * tokens * columns,
            bytes_accessed=10 * tokens * columns,
            transcendentals=0,
        ),
    )(own_part, peer_part, pick, *more)


def attend(half, flip, mask, table, queries, kv, context=None):
    tokens = queries.shape[0]
    heads = kv.shape[1] // (2 * HEAD)
    width = queries.shape[1] // (2 * heads)

    def kernel(half_ref, mask_ref, table_ref, query_ref, key_ref, value_ref, *refs):
        context_ref = refs[-1]
        scale = HEAD**-0.5 * math.log2(math.e)
        lanes = [slice(h * HEAD, (h + 1) * HEAD) for h in range(width // HEAD)]
        is_live = table_ref[:, LIVE : LIVE + 1] > 0.5
        cosine, sine = table_ref[:, : HEAD // 2], table_ref[:, HEAD // 2 : HEAD]
        cosine = jnp.concatenate([cosine, cosine], axis=1)
        sine = jnp.concatenate([-sine, sine], axis=1)
        key = jnp.where(is_live, key_ref[...].astype(jnp.float32), 0.0)
        key = (key * cosine + pltpu.roll(key, HEAD // 2, 1) * sine).astype(jnp.bfloat16)
        value = jnp.where(is_live, value_ref[...].astype(jnp.float32), 0.0).astype(jnp.bfloat16)
        scores = [
            lax.dot_general(
                query_ref[:, lane],
                key,
                (((1,), (1,)), ((), ())),
                preferred_element_type=jnp.float32,
            )
            for lane in lanes
        ]
        weights = []
        for score in scores:
            score = score * scale + mask_ref[...]
            weight = jnp.exp2(score - jnp.max(score, axis=1, keepdims=True))
            inverse = 1.0 / jnp.sum(weight, axis=1, keepdims=True)
            weights.append((weight * inverse).astype(jnp.bfloat16))
        for lane, weight in zip(lanes, weights):
            mixed = jnp.dot(weight, value, preferred_element_type=jnp.float32)
            context_ref[:, lane] = jnp.where(is_live, mixed, 0.0).astype(jnp.bfloat16)

    def wide_at(i, s):
        return (0, (1 - s[0] if flip else s[0]) * heads + i)

    in_specs = [
        pl.BlockSpec((tokens, tokens), lambda i, s: (0, 0)),
        pl.BlockSpec(table.shape, lambda i, s: (0, 0)),
        pl.BlockSpec((tokens, width), wide_at),
        pl.BlockSpec((tokens, HEAD), lambda i, s: (0, i)),
        pl.BlockSpec((tokens, HEAD), lambda i, s: (0, heads + i)),
    ]
    arguments = [half, mask, table, queries, kv, kv]
    if context is not None:
        in_specs.append(pl.BlockSpec(memory_space=pl.ANY))
        arguments.append(context)
    return pl.pallas_call(
        kernel,
        out_shape=jax.ShapeDtypeStruct(queries.shape, jnp.bfloat16),
        grid_spec=pltpu.PrefetchScalarGridSpec(
            num_scalar_prefetch=1,
            grid=(heads,),
            in_specs=in_specs,
            out_specs=pl.BlockSpec((tokens, width), wide_at),
        ),
        input_output_aliases={} if context is None else {6: 0},
        compiler_params=pltpu.CompilerParams(vmem_limit_bytes=LIMIT),
        cost_estimate=pl.CostEstimate(
            flops=4 * tokens * tokens * heads * width,
            bytes_accessed=4 * tokens * heads * width,
            transcendentals=tokens * tokens * heads * width // HEAD,
        ),
    )(*arguments)


def place(scalars, table, mine, other, spans):
    rows = WORK * SPAN
    slots, width = spans.shape
    part = width // 4

    def kernel(scalar_ref, table_ref, mine_ref, other_ref, spans_ref, out_ref, total_ref, sems):
        present = spans_ref[:, :HEAD].astype(jnp.float32)
        present = jnp.where(present > 0.5 * ABSENT, 0.0, 1.0)
        row = lax.broadcasted_iota(jnp.int32, (slots, 2 * slots), 0)
        column = lax.broadcasted_iota(jnp.int32, (slots, 2 * slots), 1)
        before = (row // SPAN < column // SPAN) & (row % SPAN == 0)
        counts = ((column < slots) & before) | (row == column - slots)
        counts = lax.dot_general(
            present.astype(jnp.bfloat16),
            jnp.where(counts, 1.0, 0.0).astype(jnp.bfloat16),
            (((0,), (0,)), ((), ())),
            preferred_element_type=jnp.float32,
        )
        rank = counts[:1, :slots].astype(jnp.int32) + scalar_ref[1]
        target = lax.broadcasted_iota(jnp.int32, (rows, slots), 0)
        sender = lax.broadcasted_iota(jnp.int32, (rows, slots), 1)
        hit = (target // SPAN == rank) & (target % SPAN == sender % SPAN)
        hit = jnp.where(hit & (counts[:1, slots:] > 0.5), 1.0, 0.0).astype(jnp.bfloat16)
        keep = table_ref[:, KEEP : KEEP + 1] > 0.5
        copies = []
        for i in range(4):
            lanes = slice(i * part, (i + 1) * part)
            came = jnp.dot(hit, spans_ref[:, lanes], preferred_element_type=jnp.float32)
            home = (mine_ref, other_ref)[i // 2][:, (i % 2) * part : (i % 2 + 1) * part]
            total_ref[i] = jnp.where(keep, home.astype(jnp.float32), came).astype(jnp.bfloat16)
            which = scalar_ref[0] if i < 2 else 1 - scalar_ref[0]
            at = pl.multiple_of((2 * (i % 2) + which) * part, HEAD)
            copies.append(
                pltpu.make_async_copy(total_ref.at[i], out_ref.at[:, pl.ds(at, part)], sems.at[i])
            )
            copies[-1].start()
        for copy in copies:
            copy.wait()

    home = pl.BlockSpec((rows, width // 2), lambda i, s: (0, 0))
    return pl.pallas_call(
        kernel,
        out_shape=jax.ShapeDtypeStruct((rows, width), jnp.bfloat16),
        grid_spec=pltpu.PrefetchScalarGridSpec(
            num_scalar_prefetch=1,
            grid=(1,),
            in_specs=[
                pl.BlockSpec((rows, table.shape[1]), lambda i, s: (0, 0)),
                home,
                home,
                pl.BlockSpec((slots, width), lambda i, s: (0, 0)),
            ],
            out_specs=pl.BlockSpec(memory_space=pl.ANY),
            scratch_shapes=[
                pltpu.VMEM((4, rows, part), jnp.bfloat16),
                pltpu.SemaphoreType.DMA((4,)),
            ],
        ),
        compiler_params=pltpu.CompilerParams(vmem_limit_bytes=LIMIT),
        cost_estimate=pl.CostEstimate(
            flops=2 * rows * slots * width,
            bytes_accessed=4 * rows * width,
            transcendentals=0,
        ),
    )(scalars, table, mine, other, spans)


def per_device(states, queries, kv_weight, kv_bias, lengths, bounds, balance):
    replicas = lax.axis_size("dp")
    own_index = lax.axis_index("dp")
    half = (lax.axis_index("group") % 2).astype(jnp.int32)[None]
    core = (own_index % 2).astype(jnp.int32)[None]
    own_y = own_index // 2 % 2
    own_z = own_index // 4
    ring = replicas // 4
    position = jnp.where(own_z % 2 == 0, own_z // 2, ring - 1 - own_z // 2)
    tokens = states.shape[0]
    depth, width = kv_weight.shape

    def block(offset, across):
        z = ring_place(ring, (position - offset + ring) % ring)
        return (z * 2 + (1 - own_y if across else own_y)).astype(jnp.int32)

    token_ids = jnp.arange(tokens, dtype=jnp.int32)
    is_live = token_ids < lengths[0] * SPAN
    owner = jnp.repeat(balance[0], SPAN)
    is_moved = is_live & (owner != own_index)
    destination = jnp.where(is_moved, owner, -1)
    keep = is_live & jnp.logical_not(is_moved)
    kept_count = jnp.sum(keep.astype(jnp.int32)) // SPAN
    chosen, rejected = bounds[0, 0], bounds[0, 1]
    segment = (token_ids >= chosen).astype(jnp.int32) + (token_ids >= rejected).astype(jnp.int32)
    place_ids = jnp.where(token_ids >= rejected, token_ids - (rejected - chosen), token_ids)
    target, source = token_ids[:, None], token_ids[None, :]
    near = (segment[None, :] == segment[:, None]) | (segment[None, :] == 0)
    allowed = ((source <= target) & is_live[None, :] & near) | (source == target)
    mask = jnp.where(allowed, 0.0, MASKED).astype(jnp.float32)
    frequency = jnp.exp(
        jnp.arange(HEAD // 2, dtype=jnp.float32) * (-2.0 * math.log(1000000.0) / HEAD)
    )
    angles = place_ids.astype(jnp.float32)[:, None] * frequency[None, :]
    columns = [jnp.cos(angles), jnp.sin(angles)]
    columns += [c.astype(jnp.float32)[:, None] for c in (is_live, destination, keep)]
    columns.append(jnp.zeros((tokens, HEAD - 3), jnp.float32))
    table = jnp.concatenate(columns, axis=1)
    scalars = jnp.stack([half[0], kept_count])
    plan = (table, mask, scalars)

    links = Links(replicas, lax.axis_size("group"))
    quarter = width // 4
    mine_weight = jnp.concatenate(
        [
            lax.dynamic_slice_in_dim(kv_weight, (2 * j + half[0]) * quarter, quarter, 1)
            for j in range(2)
        ],
        axis=1,
    )
    other_weight = head_pair(kv_weight, half, True)
    peer_columns = core_columns(states, 1 - core, depth)
    peer_states = core_swap(peer_columns, replicas)

    both = (peer_states, states)

    def listed(pieces):
        return jnp.stack([core[0], half[0]] + [b for _, b in pieces])

    fore = ring // 2
    order = [k for j in range(1, ring) for k in (j, -j)][: ring - 1]
    held = {0: mine_weight}
    mine = [(mine_weight, block(0, False))]
    other = [(other_weight, block(0, False))]
    middle, late = [], []
    crossed = links.send(mine_weight, "y")
    mine.append((crossed, block(0, True)))
    moving = other_weight
    for k in order:
        final = k == order[-1]
        nearer = held[k - 1] if k > 0 else held[k + 1]
        second = k == order[1]
        before = (peer_columns,) if second else plan if final else ()
        held[k] = links.send(nearer, "fore" if k > 0 else "back", before, lag=2 if second else None)
        mine.append((held[k], block(k, False)))
        crossed = links.send(held[k], "y")
        if 1 <= k < fore:
            other.append((links.send(held[k], "x"), block(k, False)))
        if final:
            early = mine + other
            sums = accumulate(
                both,
                listed(early),
                [p for p, _ in early],
                [0] * len(mine) + [1] * len(other),
                bias=kv_bias[None, :],
            )
            for j in range(1, ring - fore):
                moving = links.send(moving, "back")
                middle.append((moving, block(-j, False)))
            moving = links.send(moving, "back", sums)
            late.append((moving, block(fore - ring, False)))
            late.append((links.send(other_weight, "y"), block(0, True)))
            late.append((links.send(crossed, "x", sums), block(k, True)))
            middle = [(crossed, block(k, True))] + middle
            mine_peer, mine_own, other_peer, other_own, left_peer, left_own, pick = accumulate(
                both,
                listed(middle + late),
                [p for p, _ in middle],
                [0] + [1] * (len(middle) - 1),
                start=sums,
                later=len(late),
                table=table,
                rows=replicas * SPAN,
            )
        else:
            mine.append((crossed, block(k, True)))
            piece = (links.send(crossed, "x"), block(k, True))
            (middle if k == order[-2] else other).append(piece)

    mine_peer = core_swap(mine_peer, replicas)
    last = [p for p, _ in late]
    other_peer = core_swap(complete(left_peer, last, other_peer), replicas)
    other_own = complete(left_own, last, other_own)
    mine_own = after(mine_own, other_own)
    mine_kv, mine_spans = finish(mine_own, mine_peer, pick)
    other_kv, spans = finish(other_own, other_peer, pick, mine_spans)
    spans = spans.reshape(replicas, SPAN, width)
    spans = lax.all_to_all(spans, "dp", split_axis=0, concat_axis=0, tiled=True)
    spans = spans.reshape(replicas * SPAN, width)
    context = attend(half, False, mask, table, queries, mine_kv)
    context = attend(half, True, mask, table, queries, other_kv, context)
    work_rows = place(scalars, table, mine_kv, other_kv, spans)
    return (context, work_rows)


def solution(mesh):
    in_specs = (
        P(("group", "dp"), None),
        P(("group", "dp"), None),
        P("dp", None),
        P(),
        P(("group", "dp")),
        P(("group", "dp"), None),
        P(("group", "dp"), None),
    )
    out_specs = (P(("group", "dp"), None), P(("group", "dp"), None))
    return jax.shard_map(
        per_device, mesh=mesh, in_specs=in_specs, out_specs=out_specs, check_vma=False
    )
```

```python
import math

import jax
import jax.numpy as jnp
from jax import lax
from jax.experimental import pallas as pl
from jax.experimental.pallas import tpu as pltpu
from jax.sharding import PartitionSpec as P

HEAD = 128
SPAN = 8
HOME = 32
WORK = 24
ABSENT = 1e30
MASKED = -1e30
LIMIT = 18 << 20
LAG = {"x": 1, "y": 2, "z": 1}
LIVE, DESTINATION, KEEP = HEAD, HEAD + 1, HEAD + 2


def ring_place(ring, position):
    return jnp.where(2 * position < ring, 2 * position, 2 * (ring - 1 - position) + 1)


def after(value, *before):
    return lax.optimization_barrier((value, *before))[0] if before else value


class Links:
    def __init__(self, replicas, groups):
        ring = replicas // 4
        places = [p for p in range(0, ring, 2)] + [p for p in range(1, ring, 2)][::-1]
        ahead = {places[i]: places[(i + 1) % ring] for i in range(ring)}
        steps = [
            ((z * 2 + y) * 2 + c, (ahead[z] * 2 + y) * 2 + c)
            for z in range(ring)
            for y in range(2)
            for c in range(2)
        ]
        self.routes = {
            "fore": ("z", "dp", steps),
            "back": ("z", "dp", [(d, s) for s, d in steps]),
            "y": ("y", "dp", [(i, i ^ 2) for i in range(replicas)]),
            "x": ("x", "group", [(i, i ^ 1) for i in range(groups)]),
        }
        self.sent = {"x": [], "y": [], "z": []}

    def send(self, value, route, before=(), lag=None):
        link, axis, pairs = self.routes[route]
        sent = self.sent[link]
        lag = LAG[link] if lag is None else lag
        if len(sent) >= lag:
            before = (sent[-lag], *before)
        sent.append(lax.ppermute(after(value, *before), axis, pairs))
        return sent[-1]


def core_swap(value, replicas):
    return lax.ppermute(value, "dp", [(i, i ^ 1) for i in range(replicas)])


def head_pair(weight, half, flip):
    depth, width = weight.shape
    quarter = width // 4

    def kernel(half_ref, weight_ref, out_ref, sems):
        which = 1 - half_ref[0] if flip else half_ref[0]
        copies = [
            pltpu.make_async_copy(
                weight_ref.at[:, pl.ds(pl.multiple_of((2 * j + which) * quarter, HEAD), quarter)],
                out_ref.at[:, pl.ds(j * quarter, quarter)],
                sems.at[j],
            )
            for j in range(2)
        ]
        for copy in copies:
            copy.start()
        for copy in copies:
            copy.wait()

    return pl.pallas_call(
        kernel,
        out_shape=jax.ShapeDtypeStruct((depth, width // 2), weight.dtype),
        in_specs=[pl.BlockSpec(memory_space=pltpu.SMEM), pl.BlockSpec(memory_space=pl.ANY)],
        out_specs=pl.BlockSpec(memory_space=pltpu.VMEM),
        scratch_shapes=[pltpu.SemaphoreType.DMA((2,))],
        cost_estimate=pl.CostEstimate(
            flops=0, bytes_accessed=2 * depth * width, transcendentals=0
        ),
    )(half, weight)


def core_columns(states, core, depth):
    tokens, width = states.shape
    count = width // (2 * depth)

    def kernel(core_ref, states_ref, out_ref, sems):
        copies = []
        for i in range(count):
            start = pl.multiple_of((2 * i + core_ref[0]) * depth, HEAD)
            copies.append(
                pltpu.make_async_copy(
                    states_ref.at[:, pl.ds(start, depth)],
                    out_ref.at[:, pl.ds(i * depth, depth)],
                    sems.at[i],
                )
            )
        for copy in copies:
            copy.start()
        for copy in copies:
            copy.wait()

    anywhere = pl.BlockSpec(memory_space=pl.ANY)
    return pl.pallas_call(
        kernel,
        out_shape=jax.ShapeDtypeStruct((tokens, width // 2), states.dtype),
        in_specs=[pl.BlockSpec(memory_space=pltpu.SMEM), anywhere],
        out_specs=pl.BlockSpec(memory_space=pltpu.VMEM),
        scratch_shapes=[pltpu.SemaphoreType.DMA((count,))],
        cost_estimate=pl.CostEstimate(
            flops=0, bytes_accessed=2 * tokens * width, transcendentals=0
        ),
    )(core, states)


def accumulate(states, scalars, pieces, places, bias=None, start=None, later=0, table=None, rows=0):
    count = len(pieces)
    depth, columns = pieces[0].shape
    tokens = states[0].shape[0]
    batch = 5
    begun = 4 if start is not None else 1

    def kernel(scalar_ref, *refs):
        state_refs, refs = refs[:2], refs[2:]
        piece_refs, refs = refs[:count], refs[count:]
        start_refs, refs = refs[:begun], refs[begun:]
        if later:
            table_in, totals, lefts, pick_ref = refs[0], refs[1:5], refs[5:7], refs[7]
            table_ref, refs = refs[8], refs[9:]
        else:
            outs, totals, refs = refs[:4], refs[4:8], refs[8:]
        left, right, bias_ref, sems = refs
        used = 0

        def begin(source, target):
            nonlocal used
            copy = pltpu.make_async_copy(source, target, sems.at[used])
            copy.start()
            used += 1
            return copy

        def columns_at(side, index):
            at = scalar_ref[2 + index]
            at = 2 * at + scalar_ref[0] if side else at
            return state_refs[side].at[:, pl.ds(pl.multiple_of(at * depth, HEAD), depth)]

        waits = []
        if start is None:
            first = [begin(start_refs[0], bias_ref)]
        else:
            first = [begin(source, target) for source, target in zip(start_refs, totals)]
        for i in range(count):
            deep = pl.ds(i * depth, depth)
            waits.append(
                [begin(piece_refs[i], right.at[deep])]
                + [begin(columns_at(side, i), left.at[side, :, deep]) for side in range(2)]
            )
        rest = [
            begin(columns_at(side, count + i), lefts[side].at[:, pl.ds(i * depth, depth)])
            for i in range(later)
            for side in range(2)
        ]
        if later:
            table_copy = begin(table_in, table_ref)
        for copy in first:
            copy.wait()
        if later:
            table_copy.wait()
            destination = table_ref[:, DESTINATION : DESTINATION + 1].astype(jnp.int32)
            token = lax.broadcasted_iota(jnp.int32, (tokens, rows), 0)
            row = lax.broadcasted_iota(jnp.int32, (tokens, rows), 1)
            match = (destination == row // SPAN) & (token % SPAN == row % SPAN)
            pick_ref[...] = jnp.where(match, 1.0, 0.0).astype(jnp.bfloat16)
        touched = [start is not None] * 4
        for i in range(0, count, batch):
            stop = min(i + batch, count)
            for copies in waits[i:stop]:
                for copy in copies:
                    copy.wait()
            for j in range(i, stop):
                deep = slice(j * depth, (j + 1) * depth)
                for side in range(2):
                    which = 2 * places[j] + side
                    part = jnp.dot(
                        left[side, :, deep], right[deep], preferred_element_type=jnp.float32
                    )
                    if touched[which]:
                        totals[which][...] += part
                    elif side == 0:
                        totals[which][...] = part
                    else:
                        own = scalar_ref[1] if places[j] == 0 else 1 - scalar_ref[1]
                        part_width = columns // 2
                        for k in range(2):
                            at = pl.multiple_of((2 * k + own) * part_width, HEAD)
                            lanes = slice(k * part_width, (k + 1) * part_width)
                            totals[which][:, lanes] = (
                                part[:, lanes] + bias_ref[:, pl.ds(at, part_width)]
                            )
                    touched[which] = True
        if not later:
            rest += [begin(source, target) for source, target in zip(totals, outs)]
        for copy in rest:
            copy.wait()

    outside = pl.BlockSpec(memory_space=pltpu.HBM)
    inside = pl.BlockSpec(memory_space=pltpu.VMEM)
    sums = (tokens, columns)
    if later:
        out_shape = [jax.ShapeDtypeStruct(sums, jnp.float32)] * 4
        out_shape += [jax.ShapeDtypeStruct((tokens, later * depth), jnp.bfloat16)] * 2
        out_shape += [jax.ShapeDtypeStruct((tokens, rows), jnp.bfloat16)]
        out_specs, scratch = [inside] * 7, [pltpu.VMEM(table.shape, table.dtype)]
    else:
        out_shape = [pltpu.HBM(sums, jnp.float32)] * 4
        out_specs, scratch = [outside] * 4, [pltpu.VMEM(sums, jnp.float32)] * 4
    outer = [*states, *pieces, *((bias,) if start is None else start)]
    outer += [table] if later else []
    return pl.pallas_call(
        kernel,
        out_shape=out_shape,
        in_specs=[pl.BlockSpec(memory_space=pltpu.SMEM)] + [outside] * len(outer),
        out_specs=out_specs,
        scratch_shapes=scratch
        + [
            pltpu.VMEM((2, tokens, count * depth), jnp.bfloat16),
            pltpu.VMEM((count * depth, columns), jnp.bfloat16),
            pltpu.VMEM((1, 2 * columns), jnp.float32),
            pltpu.SemaphoreType.DMA((3 * count + 2 * later + 8,)),
        ],
        compiler_params=pltpu.CompilerParams(vmem_limit_bytes=LIMIT),
        cost_estimate=pl.CostEstimate(
            flops=4 * count * tokens * depth * columns,
            bytes_accessed=count * (4 * tokens * depth + 2 * depth * columns),
            transcendentals=0,
        ),
    )(scalars, *(pltpu.with_memory_space_constraint(a, pltpu.HBM) for a in outer))


def complete(left, pieces, total):
    depth = pieces[0].shape[0]

    def kernel(left_ref, total_ref, *refs):
        out_ref = refs[-1]
        for i, piece in enumerate(refs[:-1]):
            part = jnp.dot(
                left_ref[:, i * depth : (i + 1) * depth],
                piece[...],
                preferred_element_type=jnp.float32,
            )
            out_ref[...] = (total_ref if i == 0 else out_ref)[...] + part

    inside = pl.BlockSpec(memory_space=pltpu.VMEM)
    return pl.pallas_call(
        kernel,
        out_shape=jax.ShapeDtypeStruct(total.shape, total.dtype),
        in_specs=[inside] * (2 + len(pieces)),
        out_specs=inside,
        compiler_params=pltpu.CompilerParams(vmem_limit_bytes=LIMIT),
        cost_estimate=pl.CostEstimate(
            flops=2 * left.size * total.shape[1],
            bytes_accessed=2 * left.size,
            transcendentals=0,
        ),
    )(left, total, *pieces)


def finish(own_part, peer_part, pick, earlier=None):
    tokens, columns = own_part.shape
    rows = pick.shape[1]
    last = earlier is not None

    def kernel(own_ref, peer_ref, pick_ref, *refs):
        if last:
            earlier_ref, kv_ref, out_ref, spans_ref, sems = refs
            first = pltpu.make_async_copy(
                earlier_ref, out_ref.at[:, pl.ds(0, columns)], sems.at[0]
            )
            first.start()
        else:
            kv_ref, spans_ref = refs
        kv = (own_ref[...] + peer_ref[...]).astype(jnp.bfloat16)
        kv_ref[...] = kv
        over_tokens = (((0,), (0,)), ((), ()))
        found = lax.dot_general(
            pick_ref[...],
            jnp.ones((tokens, HEAD), jnp.bfloat16),
            over_tokens,
            preferred_element_type=jnp.float32,
        )
        spans = lax.dot_general(
            pick_ref[...], kv, over_tokens, preferred_element_type=jnp.float32
        )
        spans_ref[...] = jnp.where(found[:, :1] > 0.5, spans, ABSENT).astype(jnp.bfloat16)
        if last:
            second = pltpu.make_async_copy(
                spans_ref, out_ref.at[:, pl.ds(columns, columns)], sems.at[1]
            )
            second.start()
            first.wait()
            second.wait()

    inside = pl.BlockSpec(memory_space=pltpu.VMEM)
    kv_shape = jax.ShapeDtypeStruct((tokens, columns), jnp.bfloat16)
    if last:
        out_shape = (kv_shape, pltpu.HBM((rows, 2 * columns), jnp.bfloat16))
        out_specs = (inside, pl.BlockSpec(memory_space=pltpu.HBM))
        scratch = [pltpu.VMEM((rows, columns), jnp.bfloat16), pltpu.SemaphoreType.DMA((2,))]
    else:
        out_shape = (kv_shape, jax.ShapeDtypeStruct((rows, columns), jnp.bfloat16))
        out_specs, scratch = (inside, inside), []
    more = (earlier,) if last else ()
    return pl.pallas_call(
        kernel,
        out_shape=out_shape,
        in_specs=[inside] * (3 + len(more)),
        out_specs=out_specs,
        scratch_shapes=scratch,
        compiler_params=pltpu.CompilerParams(vmem_limit_bytes=LIMIT),
        cost_estimate=pl.CostEstimate(
            flops=2 * rows * tokens * columns,
            bytes_accessed=10 * tokens * columns,
            transcendentals=0,
        ),
    )(own_part, peer_part, pick, *more)


def attend(half, flip, mask, table, queries, kv, context=None):
    tokens = queries.shape[0]
    heads = kv.shape[1] // (2 * HEAD)
    width = queries.shape[1] // (2 * heads)

    def kernel(half_ref, mask_ref, table_ref, query_ref, key_ref, value_ref, *refs):
        context_ref = refs[-1]
        scale = HEAD**-0.5 * math.log2(math.e)
        lanes = [slice(h * HEAD, (h + 1) * HEAD) for h in range(width // HEAD)]
        is_live = table_ref[:, LIVE : LIVE + 1] > 0.5
        cosine, sine = table_ref[:, : HEAD // 2], table_ref[:, HEAD // 2 : HEAD]
        cosine = jnp.concatenate([cosine, cosine], axis=1)
        sine = jnp.concatenate([-sine, sine], axis=1)
        key = jnp.where(is_live, key_ref[...].astype(jnp.float32), 0.0)
        key = (key * cosine + pltpu.roll(key, HEAD // 2, 1) * sine).astype(jnp.bfloat16)
        value = jnp.where(is_live, value_ref[...].astype(jnp.float32), 0.0).astype(jnp.bfloat16)
        scores = [
            lax.dot_general(
                query_ref[:, lane],
                key,
                (((1,), (1,)), ((), ())),
                preferred_element_type=jnp.float32,
            )
            for lane in lanes
        ]
        weights = []
        for score in scores:
            score = score * scale + mask_ref[...]
            weight = jnp.exp2(score - jnp.max(score, axis=1, keepdims=True))
            inverse = 1.0 / jnp.sum(weight, axis=1, keepdims=True)
            weights.append((weight * inverse).astype(jnp.bfloat16))
        for lane, weight in zip(lanes, weights):
            mixed = jnp.dot(weight, value, preferred_element_type=jnp.float32)
            context_ref[:, lane] = jnp.where(is_live, mixed, 0.0).astype(jnp.bfloat16)

    def wide_at(i, s):
        return (0, (1 - s[0] if flip else s[0]) * heads + i)

    in_specs = [
        pl.BlockSpec((tokens, tokens), lambda i, s: (0, 0)),
        pl.BlockSpec(table.shape, lambda i, s: (0, 0)),
        pl.BlockSpec((tokens, width), wide_at),
        pl.BlockSpec((tokens, HEAD), lambda i, s: (0, i)),
        pl.BlockSpec((tokens, HEAD), lambda i, s: (0, heads + i)),
    ]
    arguments = [half, mask, table, queries, kv, kv]
    if context is not None:
        in_specs.append(pl.BlockSpec(memory_space=pl.ANY))
        arguments.append(context)
    return pl.pallas_call(
        kernel,
        out_shape=jax.ShapeDtypeStruct(queries.shape, jnp.bfloat16),
        grid_spec=pltpu.PrefetchScalarGridSpec(
            num_scalar_prefetch=1,
            grid=(heads,),
            in_specs=in_specs,
            out_specs=pl.BlockSpec((tokens, width), wide_at),
        ),
        input_output_aliases={} if context is None else {6: 0},
        compiler_params=pltpu.CompilerParams(vmem_limit_bytes=LIMIT),
        cost_estimate=pl.CostEstimate(
            flops=4 * tokens * tokens * heads * width,
            bytes_accessed=4 * tokens * heads * width,
            transcendentals=tokens * tokens * heads * width // HEAD,
        ),
    )(*arguments)


def place(scalars, table, mine, other, spans):
    rows = WORK * SPAN
    slots, width = spans.shape
    part = width // 4

    def kernel(scalar_ref, table_ref, mine_ref, other_ref, spans_ref, out_ref, total_ref, sems):
        present = spans_ref[:, :HEAD].astype(jnp.float32)
        present = jnp.where(present > 0.5 * ABSENT, 0.0, 1.0)
        row = lax.broadcasted_iota(jnp.int32, (slots, 2 * slots), 0)
        column = lax.broadcasted_iota(jnp.int32, (slots, 2 * slots), 1)
        before = (row // SPAN < column // SPAN) & (row % SPAN == 0)
        counts = ((column < slots) & before) | (row == column - slots)
        counts = lax.dot_general(
            present.astype(jnp.bfloat16),
            jnp.where(counts, 1.0, 0.0).astype(jnp.bfloat16),
            (((0,), (0,)), ((), ())),
            preferred_element_type=jnp.float32,
        )
        rank = counts[:1, :slots].astype(jnp.int32) + scalar_ref[1]
        target = lax.broadcasted_iota(jnp.int32, (rows, slots), 0)
        sender = lax.broadcasted_iota(jnp.int32, (rows, slots), 1)
        hit = (target // SPAN == rank) & (target % SPAN == sender % SPAN)
        hit = jnp.where(hit & (counts[:1, slots:] > 0.5), 1.0, 0.0).astype(jnp.bfloat16)
        keep = table_ref[:, KEEP : KEEP + 1] > 0.5
        copies = []
        for i in range(4):
            lanes = slice(i * part, (i + 1) * part)
            came = jnp.dot(hit, spans_ref[:, lanes], preferred_element_type=jnp.float32)
            home = (mine_ref, other_ref)[i // 2][:, (i % 2) * part : (i % 2 + 1) * part]
            total_ref[i] = jnp.where(keep, home.astype(jnp.float32), came).astype(jnp.bfloat16)
            which = scalar_ref[0] if i < 2 else 1 - scalar_ref[0]
            at = pl.multiple_of((2 * (i % 2) + which) * part, HEAD)
            copies.append(
                pltpu.make_async_copy(total_ref.at[i], out_ref.at[:, pl.ds(at, part)], sems.at[i])
            )
            copies[-1].start()
        for copy in copies:
            copy.wait()

    home = pl.BlockSpec((rows, width // 2), lambda i, s: (0, 0))
    return pl.pallas_call(
        kernel,
        out_shape=jax.ShapeDtypeStruct((rows, width), jnp.bfloat16),
        grid_spec=pltpu.PrefetchScalarGridSpec(
            num_scalar_prefetch=1,
            grid=(1,),
            in_specs=[
                pl.BlockSpec((rows, table.shape[1]), lambda i, s: (0, 0)),
                home,
                home,
                pl.BlockSpec((slots, width), lambda i, s: (0, 0)),
            ],
            out_specs=pl.BlockSpec(memory_space=pl.ANY),
            scratch_shapes=[
                pltpu.VMEM((4, rows, part), jnp.bfloat16),
                pltpu.SemaphoreType.DMA((4,)),
            ],
        ),
        compiler_params=pltpu.CompilerParams(vmem_limit_bytes=LIMIT),
        cost_estimate=pl.CostEstimate(
            flops=2 * rows * slots * width,
            bytes_accessed=4 * rows * width,
            transcendentals=0,
        ),
    )(scalars, table, mine, other, spans)


def per_device(states, queries, kv_weight, kv_bias, lengths, bounds, balance):
    replicas = lax.axis_size("dp")
    own_index = lax.axis_index("dp")
    half = (lax.axis_index("group") % 2).astype(jnp.int32)[None]
    core = (own_index % 2).astype(jnp.int32)[None]
    own_y = own_index // 2 % 2
    own_z = own_index // 4
    ring = replicas // 4
    position = jnp.where(own_z % 2 == 0, own_z // 2, ring - 1 - own_z // 2)
    tokens = states.shape[0]
    depth, width = kv_weight.shape

    def block(offset, across):
        z = ring_place(ring, (position - offset + ring) % ring)
        return (z * 2 + (1 - own_y if across else own_y)).astype(jnp.int32)

    token_ids = jnp.arange(tokens, dtype=jnp.int32)
    is_live = token_ids < lengths[0] * SPAN
    owner = jnp.repeat(balance[0], SPAN)
    is_moved = is_live & (owner != own_index)
    destination = jnp.where(is_moved, owner, -1)
    keep = is_live & jnp.logical_not(is_moved)
    kept_count = jnp.sum(keep.astype(jnp.int32)) // SPAN
    chosen, rejected = bounds[0, 0], bounds[0, 1]
    segment = (token_ids >= chosen).astype(jnp.int32) + (token_ids >= rejected).astype(jnp.int32)
    place_ids = jnp.where(token_ids >= rejected, token_ids - (rejected - chosen), token_ids)
    target, source = token_ids[:, None], token_ids[None, :]
    near = (segment[None, :] == segment[:, None]) | (segment[None, :] == 0)
    allowed = ((source <= target) & is_live[None, :] & near) | (source == target)
    mask = jnp.where(allowed, 0.0, MASKED).astype(jnp.float32)
    frequency = jnp.exp(
        jnp.arange(HEAD // 2, dtype=jnp.float32) * (-2.0 * math.log(1000000.0) / HEAD)
    )
    angles = place_ids.astype(jnp.float32)[:, None] * frequency[None, :]
    columns = [jnp.cos(angles), jnp.sin(angles)]
    columns += [c.astype(jnp.float32)[:, None] for c in (is_live, destination, keep)]
    columns.append(jnp.zeros((tokens, HEAD - 3), jnp.float32))
    table = jnp.concatenate(columns, axis=1)
    scalars = jnp.stack([half[0], kept_count])
    plan = (table, mask, scalars)

    links = Links(replicas, lax.axis_size("group"))
    quarter = width // 4
    mine_weight = jnp.concatenate(
        [
            lax.dynamic_slice_in_dim(kv_weight, (2 * j + half[0]) * quarter, quarter, 1)
            for j in range(2)
        ],
        axis=1,
    )
    other_weight = head_pair(kv_weight, half, True)
    peer_columns = core_columns(states, 1 - core, depth)
    peer_states = core_swap(peer_columns, replicas)

    both = (peer_states, states)

    def listed(pieces):
        return jnp.stack([core[0], half[0]] + [b for _, b in pieces])

    fore = ring // 2
    order = [k for j in range(1, ring) for k in (j, -j)][: ring - 1]
    held = {0: mine_weight}
    mine = [(mine_weight, block(0, False))]
    other = [(other_weight, block(0, False))]
    middle, late = [], []
    crossed = links.send(mine_weight, "y")
    mine.append((crossed, block(0, True)))
    moving = other_weight
    for k in order:
        final = k == order[-1]
        nearer = held[k - 1] if k > 0 else held[k + 1]
        second = k == order[1]
        before = (peer_columns,) if second else plan if final else ()
        held[k] = links.send(nearer, "fore" if k > 0 else "back", before, lag=2 if second else None)
        mine.append((held[k], block(k, False)))
        crossed = links.send(held[k], "y")
        if 1 <= k < fore:
            swapped = links.send(held[k], "x")
            other.append((swapped, block(k, False)))
        if final:
            early = mine + other
            sums = accumulate(
                both,
                listed(early),
                [p for p, _ in early],
                [0] * len(mine) + [1] * len(other),
                bias=kv_bias[None, :],
            )
            swapped = links.send(swapped, "fore")
            middle.append((swapped, block(fore, False)))
            for j in range(1, ring - fore):
                moving = links.send(moving, "back", sums)
                (late if j == ring - fore - 1 else middle).append((moving, block(-j, False)))
            late.append((links.send(other_weight, "y"), block(0, True)))
            late.append((links.send(crossed, "x"), block(k, True)))
            middle = [(crossed, block(k, True))] + middle
            mine_peer, mine_own, other_peer, other_own, left_peer, left_own, pick = accumulate(
                both,
                listed(middle + late),
                [p for p, _ in middle],
                [0] + [1] * (len(middle) - 1),
                start=sums,
                later=len(late),
                table=table,
                rows=replicas * SPAN,
            )
        else:
            mine.append((crossed, block(k, True)))
            piece = (links.send(crossed, "x"), block(k, True))
            (middle if k == order[-2] else other).append(piece)

    mine_peer = core_swap(mine_peer, replicas)
    last = [p for p, _ in late]
    other_peer = core_swap(complete(left_peer, last, other_peer), replicas)
    other_own = complete(left_own, last, other_own)
    mine_own = after(mine_own, other_own)
    mine_kv, mine_spans = finish(mine_own, mine_peer, pick)
    other_kv, spans = finish(other_own, other_peer, pick, mine_spans)
    spans = spans.reshape(replicas, SPAN, width)
    spans = lax.all_to_all(spans, "dp", split_axis=0, concat_axis=0, tiled=True)
    spans = spans.reshape(replicas * SPAN, width)
    context = attend(half, False, mask, table, queries, mine_kv)
    context = attend(half, True, mask, table, queries, other_kv, context)
    work_rows = place(scalars, table, mine_kv, other_kv, spans)
    return (context, work_rows)


def solution(mesh):
    in_specs = (
        P(("group", "dp"), None),
        P(("group", "dp"), None),
        P("dp", None),
        P(),
        P(("group", "dp")),
        P(("group", "dp"), None),
        P(("group", "dp"), None),
    )
    out_specs = (P(("group", "dp"), None), P(("group", "dp"), None))
    return jax.shard_map(
        per_device, mesh=mesh, in_specs=in_specs, out_specs=out_specs, check_vma=False
    )
```

```python
import math

import jax
import jax.numpy as jnp
from jax import lax
from jax.experimental import pallas as pl
from jax.experimental.pallas import tpu as pltpu
from jax.sharding import PartitionSpec as P

HEAD = 128
SPAN = 8
HOME = 32
WORK = 24
ABSENT = 1e30
MASKED = -1e30
LIMIT = 18 << 20
LAG = {"x": 1, "y": 2, "z": 1}
LIVE, DESTINATION, KEEP = HEAD, HEAD + 1, HEAD + 2


def ring_place(ring, position):
    return jnp.where(2 * position < ring, 2 * position, 2 * (ring - 1 - position) + 1)


def after(value, *before):
    return lax.optimization_barrier((value, *before))[0] if before else value


class Links:
    def __init__(self, replicas, groups):
        ring = replicas // 4
        places = [p for p in range(0, ring, 2)] + [p for p in range(1, ring, 2)][::-1]
        ahead = {places[i]: places[(i + 1) % ring] for i in range(ring)}
        steps = [
            ((z * 2 + y) * 2 + c, (ahead[z] * 2 + y) * 2 + c)
            for z in range(ring)
            for y in range(2)
            for c in range(2)
        ]
        self.routes = {
            "fore": ("z", "dp", steps),
            "back": ("z", "dp", [(d, s) for s, d in steps]),
            "y": ("y", "dp", [(i, i ^ 2) for i in range(replicas)]),
            "x": ("x", "group", [(i, i ^ 1) for i in range(groups)]),
        }
        self.sent = {"x": [], "y": [], "z": []}

    def send(self, value, route, before=(), lag=None):
        link, axis, pairs = self.routes[route]
        sent = self.sent[link]
        lag = LAG[link] if lag is None else lag
        if len(sent) >= lag:
            before = (sent[-lag], *before)
        sent.append(lax.ppermute(after(value, *before), axis, pairs))
        return sent[-1]


def core_swap(value, replicas):
    return lax.ppermute(value, "dp", [(i, i ^ 1) for i in range(replicas)])


def head_pair(weight, half, flip):
    depth, width = weight.shape
    quarter = width // 4

    def kernel(half_ref, weight_ref, out_ref, sems):
        which = 1 - half_ref[0] if flip else half_ref[0]
        copies = [
            pltpu.make_async_copy(
                weight_ref.at[:, pl.ds(pl.multiple_of((2 * j + which) * quarter, HEAD), quarter)],
                out_ref.at[:, pl.ds(j * quarter, quarter)],
                sems.at[j],
            )
            for j in range(2)
        ]
        for copy in copies:
            copy.start()
        for copy in copies:
            copy.wait()

    return pl.pallas_call(
        kernel,
        out_shape=jax.ShapeDtypeStruct((depth, width // 2), weight.dtype),
        in_specs=[pl.BlockSpec(memory_space=pltpu.SMEM), pl.BlockSpec(memory_space=pl.ANY)],
        out_specs=pl.BlockSpec(memory_space=pltpu.VMEM),
        scratch_shapes=[pltpu.SemaphoreType.DMA((2,))],
        cost_estimate=pl.CostEstimate(
            flops=0, bytes_accessed=2 * depth * width, transcendentals=0
        ),
    )(half, weight)


def core_columns(states, core, depth):
    tokens, width = states.shape
    count = width // (2 * depth)

    def kernel(core_ref, states_ref, out_ref, sems):
        copies = []
        for i in range(count):
            start = pl.multiple_of((2 * i + core_ref[0]) * depth, HEAD)
            copies.append(
                pltpu.make_async_copy(
                    states_ref.at[:, pl.ds(start, depth)],
                    out_ref.at[:, pl.ds(i * depth, depth)],
                    sems.at[i],
                )
            )
        for copy in copies:
            copy.start()
        for copy in copies:
            copy.wait()

    anywhere = pl.BlockSpec(memory_space=pl.ANY)
    return pl.pallas_call(
        kernel,
        out_shape=jax.ShapeDtypeStruct((tokens, width // 2), states.dtype),
        in_specs=[pl.BlockSpec(memory_space=pltpu.SMEM), anywhere],
        out_specs=pl.BlockSpec(memory_space=pltpu.VMEM),
        scratch_shapes=[pltpu.SemaphoreType.DMA((count,))],
        cost_estimate=pl.CostEstimate(
            flops=0, bytes_accessed=2 * tokens * width, transcendentals=0
        ),
    )(core, states)


def accumulate(states, scalars, pieces, places, bias=None, start=None, later=0, table=None, rows=0):
    count = len(pieces)
    depth, columns = pieces[0].shape
    tokens = states[0].shape[0]
    batch = 5
    begun = 4 if start is not None else 1

    def kernel(scalar_ref, *refs):
        state_refs, refs = refs[:2], refs[2:]
        piece_refs, refs = refs[:count], refs[count:]
        start_refs, refs = refs[:begun], refs[begun:]
        if later:
            table_in, totals, lefts, pick_ref = refs[0], refs[1:5], refs[5:7], refs[7]
            table_ref, refs = refs[8], refs[9:]
        else:
            outs, totals, refs = refs[:4], refs[4:8], refs[8:]
        left, right, bias_ref, sems = refs
        used = 0

        def begin(source, target):
            nonlocal used
            copy = pltpu.make_async_copy(source, target, sems.at[used])
            copy.start()
            used += 1
            return copy

        def columns_at(side, index):
            at = scalar_ref[2 + index]
            at = 2 * at + scalar_ref[0] if side else at
            return state_refs[side].at[:, pl.ds(pl.multiple_of(at * depth, HEAD), depth)]

        waits = []
        if start is None:
            first = [begin(start_refs[0], bias_ref)]
        else:
            first = [begin(source, target) for source, target in zip(start_refs, totals)]
        for i in range(count):
            deep = pl.ds(i * depth, depth)
            waits.append(
                [begin(piece_refs[i], right.at[deep])]
                + [begin(columns_at(side, i), left.at[side, :, deep]) for side in range(2)]
            )
        rest = [
            begin(columns_at(side, count + i), lefts[side].at[:, pl.ds(i * depth, depth)])
            for i in range(later)
            for side in range(2)
        ]
        if later:
            table_copy = begin(table_in, table_ref)
        for copy in first:
            copy.wait()
        if later:
            table_copy.wait()
            destination = table_ref[:, DESTINATION : DESTINATION + 1].astype(jnp.int32)
            token = lax.broadcasted_iota(jnp.int32, (tokens, rows), 0)
            row = lax.broadcasted_iota(jnp.int32, (tokens, rows), 1)
            match = (destination == row // SPAN) & (token % SPAN == row % SPAN)
            pick_ref[...] = jnp.where(match, 1.0, 0.0).astype(jnp.bfloat16)
        touched = [start is not None] * 4
        for i in range(0, count, batch):
            stop = min(i + batch, count)
            for copies in waits[i:stop]:
                for copy in copies:
                    copy.wait()
            for j in range(i, stop):
                deep = slice(j * depth, (j + 1) * depth)
                for side in range(2):
                    which = 2 * places[j] + side
                    part = jnp.dot(
                        left[side, :, deep], right[deep], preferred_element_type=jnp.float32
                    )
                    if touched[which]:
                        totals[which][...] += part
                    elif side == 0:
                        totals[which][...] = part
                    else:
                        own = scalar_ref[1] if places[j] == 0 else 1 - scalar_ref[1]
                        part_width = columns // 2
                        for k in range(2):
                            at = pl.multiple_of((2 * k + own) * part_width, HEAD)
                            lanes = slice(k * part_width, (k + 1) * part_width)
                            totals[which][:, lanes] = (
                                part[:, lanes] + bias_ref[:, pl.ds(at, part_width)]
                            )
                    touched[which] = True
        if not later:
            rest += [begin(source, target) for source, target in zip(totals, outs)]
        for copy in rest:
            copy.wait()

    outside = pl.BlockSpec(memory_space=pltpu.HBM)
    inside = pl.BlockSpec(memory_space=pltpu.VMEM)
    sums = (tokens, columns)
    if later:
        out_shape = [jax.ShapeDtypeStruct(sums, jnp.float32)] * 4
        out_shape += [jax.ShapeDtypeStruct((tokens, later * depth), jnp.bfloat16)] * 2
        out_shape += [jax.ShapeDtypeStruct((tokens, rows), jnp.bfloat16)]
        out_specs, scratch = [inside] * 7, [pltpu.VMEM(table.shape, table.dtype)]
    else:
        out_shape = [pltpu.HBM(sums, jnp.float32)] * 4
        out_specs, scratch = [outside] * 4, [pltpu.VMEM(sums, jnp.float32)] * 4
    outer = [*states, *pieces, *((bias,) if start is None else start)]
    outer += [table] if later else []
    return pl.pallas_call(
        kernel,
        out_shape=out_shape,
        in_specs=[pl.BlockSpec(memory_space=pltpu.SMEM)] + [outside] * len(outer),
        out_specs=out_specs,
        scratch_shapes=scratch
        + [
            pltpu.VMEM((2, tokens, count * depth), jnp.bfloat16),
            pltpu.VMEM((count * depth, columns), jnp.bfloat16),
            pltpu.VMEM((1, 2 * columns), jnp.float32),
            pltpu.SemaphoreType.DMA((3 * count + 2 * later + 8,)),
        ],
        compiler_params=pltpu.CompilerParams(vmem_limit_bytes=LIMIT),
        cost_estimate=pl.CostEstimate(
            flops=4 * count * tokens * depth * columns,
            bytes_accessed=count * (4 * tokens * depth + 2 * depth * columns),
            transcendentals=0,
        ),
    )(scalars, *(pltpu.with_memory_space_constraint(a, pltpu.HBM) for a in outer))


def complete(left, pieces, total):
    depth = pieces[0].shape[0]

    def kernel(left_ref, total_ref, *refs):
        out_ref = refs[-1]
        for i, piece in enumerate(refs[:-1]):
            part = jnp.dot(
                left_ref[:, i * depth : (i + 1) * depth],
                piece[...],
                preferred_element_type=jnp.float32,
            )
            out_ref[...] = (total_ref if i == 0 else out_ref)[...] + part

    inside = pl.BlockSpec(memory_space=pltpu.VMEM)
    return pl.pallas_call(
        kernel,
        out_shape=jax.ShapeDtypeStruct(total.shape, total.dtype),
        in_specs=[inside] * (2 + len(pieces)),
        out_specs=inside,
        compiler_params=pltpu.CompilerParams(vmem_limit_bytes=LIMIT),
        cost_estimate=pl.CostEstimate(
            flops=2 * left.size * total.shape[1],
            bytes_accessed=2 * left.size,
            transcendentals=0,
        ),
    )(left, total, *pieces)


def finish(own_part, peer_part, pick, earlier=None):
    tokens, columns = own_part.shape
    rows = pick.shape[1]
    last = earlier is not None

    def kernel(own_ref, peer_ref, pick_ref, *refs):
        if last:
            earlier_ref, kv_ref, out_ref, spans_ref, sems = refs
            first = pltpu.make_async_copy(
                earlier_ref, out_ref.at[:, pl.ds(0, columns)], sems.at[0]
            )
            first.start()
        else:
            kv_ref, spans_ref = refs
        kv = (own_ref[...] + peer_ref[...]).astype(jnp.bfloat16)
        kv_ref[...] = kv
        over_tokens = (((0,), (0,)), ((), ()))
        found = lax.dot_general(
            pick_ref[...],
            jnp.ones((tokens, HEAD), jnp.bfloat16),
            over_tokens,
            preferred_element_type=jnp.float32,
        )
        spans = lax.dot_general(
            pick_ref[...], kv, over_tokens, preferred_element_type=jnp.float32
        )
        spans_ref[...] = jnp.where(found[:, :1] > 0.5, spans, ABSENT).astype(jnp.bfloat16)
        if last:
            second = pltpu.make_async_copy(
                spans_ref, out_ref.at[:, pl.ds(columns, columns)], sems.at[1]
            )
            second.start()
            first.wait()
            second.wait()

    inside = pl.BlockSpec(memory_space=pltpu.VMEM)
    kv_shape = jax.ShapeDtypeStruct((tokens, columns), jnp.bfloat16)
    if last:
        out_shape = (kv_shape, pltpu.HBM((rows, 2 * columns), jnp.bfloat16))
        out_specs = (inside, pl.BlockSpec(memory_space=pltpu.HBM))
        scratch = [pltpu.VMEM((rows, columns), jnp.bfloat16), pltpu.SemaphoreType.DMA((2,))]
    else:
        out_shape = (kv_shape, jax.ShapeDtypeStruct((rows, columns), jnp.bfloat16))
        out_specs, scratch = (inside, inside), []
    more = (earlier,) if last else ()
    return pl.pallas_call(
        kernel,
        out_shape=out_shape,
        in_specs=[inside] * (3 + len(more)),
        out_specs=out_specs,
        scratch_shapes=scratch,
        compiler_params=pltpu.CompilerParams(vmem_limit_bytes=LIMIT),
        cost_estimate=pl.CostEstimate(
            flops=2 * rows * tokens * columns,
            bytes_accessed=10 * tokens * columns,
            transcendentals=0,
        ),
    )(own_part, peer_part, pick, *more)


def attend(half, flip, mask, table, queries, kv, context=None):
    tokens = queries.shape[0]
    heads = kv.shape[1] // (2 * HEAD)
    width = queries.shape[1] // (2 * heads)

    def kernel(half_ref, mask_ref, table_ref, query_ref, key_ref, value_ref, *refs):
        context_ref = refs[-1]
        scale = HEAD**-0.5 * math.log2(math.e)
        lanes = [slice(h * HEAD, (h + 1) * HEAD) for h in range(width // HEAD)]
        is_live = table_ref[:, LIVE : LIVE + 1] > 0.5
        cosine, sine = table_ref[:, : HEAD // 2], table_ref[:, HEAD // 2 : HEAD]
        cosine = jnp.concatenate([cosine, cosine], axis=1)
        sine = jnp.concatenate([-sine, sine], axis=1)
        key = jnp.where(is_live, key_ref[...].astype(jnp.float32), 0.0)
        key = (key * cosine + pltpu.roll(key, HEAD // 2, 1) * sine).astype(jnp.bfloat16)
        value = jnp.where(is_live, value_ref[...].astype(jnp.float32), 0.0).astype(jnp.bfloat16)
        scores = [
            lax.dot_general(
                query_ref[:, lane],
                key,
                (((1,), (1,)), ((), ())),
                preferred_element_type=jnp.float32,
            )
            for lane in lanes
        ]
        weights = []
        for score in scores:
            score = score * scale + mask_ref[...]
            weight = jnp.exp2(score - jnp.max(score, axis=1, keepdims=True))
            inverse = 1.0 / jnp.sum(weight, axis=1, keepdims=True)
            weights.append((weight * inverse).astype(jnp.bfloat16))
        for lane, weight in zip(lanes, weights):
            mixed = jnp.dot(weight, value, preferred_element_type=jnp.float32)
            context_ref[:, lane] = jnp.where(is_live, mixed, 0.0).astype(jnp.bfloat16)

    def wide_at(i, s):
        return (0, (1 - s[0] if flip else s[0]) * heads + i)

    in_specs = [
        pl.BlockSpec((tokens, tokens), lambda i, s: (0, 0)),
        pl.BlockSpec(table.shape, lambda i, s: (0, 0)),
        pl.BlockSpec((tokens, width), wide_at),
        pl.BlockSpec((tokens, HEAD), lambda i, s: (0, i)),
        pl.BlockSpec((tokens, HEAD), lambda i, s: (0, heads + i)),
    ]
    arguments = [half, mask, table, queries, kv, kv]
    if context is not None:
        in_specs.append(pl.BlockSpec(memory_space=pl.ANY))
        arguments.append(context)
    return pl.pallas_call(
        kernel,
        out_shape=jax.ShapeDtypeStruct(queries.shape, jnp.bfloat16),
        grid_spec=pltpu.PrefetchScalarGridSpec(
            num_scalar_prefetch=1,
            grid=(heads,),
            in_specs=in_specs,
            out_specs=pl.BlockSpec((tokens, width), wide_at),
        ),
        input_output_aliases={} if context is None else {6: 0},
        compiler_params=pltpu.CompilerParams(vmem_limit_bytes=LIMIT),
        cost_estimate=pl.CostEstimate(
            flops=4 * tokens * tokens * heads * width,
            bytes_accessed=4 * tokens * heads * width,
            transcendentals=tokens * tokens * heads * width // HEAD,
        ),
    )(*arguments)


def place(scalars, table, mine, other, spans):
    rows = WORK * SPAN
    slots, width = spans.shape
    part = width // 4

    def kernel(scalar_ref, table_ref, mine_ref, other_ref, spans_ref, out_ref, total_ref, sems):
        present = spans_ref[:, :HEAD].astype(jnp.float32)
        present = jnp.where(present > 0.5 * ABSENT, 0.0, 1.0)
        row = lax.broadcasted_iota(jnp.int32, (slots, 2 * slots), 0)
        column = lax.broadcasted_iota(jnp.int32, (slots, 2 * slots), 1)
        before = (row // SPAN < column // SPAN) & (row % SPAN == 0)
        counts = ((column < slots) & before) | (row == column - slots)
        counts = lax.dot_general(
            present.astype(jnp.bfloat16),
            jnp.where(counts, 1.0, 0.0).astype(jnp.bfloat16),
            (((0,), (0,)), ((), ())),
            preferred_element_type=jnp.float32,
        )
        rank = counts[:1, :slots].astype(jnp.int32) + scalar_ref[1]
        target = lax.broadcasted_iota(jnp.int32, (rows, slots), 0)
        sender = lax.broadcasted_iota(jnp.int32, (rows, slots), 1)
        hit = (target // SPAN == rank) & (target % SPAN == sender % SPAN)
        hit = jnp.where(hit & (counts[:1, slots:] > 0.5), 1.0, 0.0).astype(jnp.bfloat16)
        keep = table_ref[:, KEEP - HEAD : KEEP - HEAD + 1] > 0.5
        arrived = jnp.dot(hit, spans_ref[...], preferred_element_type=jnp.float32)
        copies = []
        for i in range(4):
            lanes = slice(i * part, (i + 1) * part)
            came = arrived[:, lanes]
            home = (mine_ref, other_ref)[i // 2][:, (i % 2) * part : (i % 2 + 1) * part]
            total_ref[i] = jnp.where(keep, home.astype(jnp.float32), came).astype(jnp.bfloat16)
            which = scalar_ref[0] if i < 2 else 1 - scalar_ref[0]
            at = pl.multiple_of((2 * (i % 2) + which) * part, HEAD)
            copies.append(
                pltpu.make_async_copy(total_ref.at[i], out_ref.at[:, pl.ds(at, part)], sems.at[i])
            )
            copies[-1].start()
        for copy in copies:
            copy.wait()

    home = pl.BlockSpec((rows, width // 2), lambda i, s: (0, 0))
    return pl.pallas_call(
        kernel,
        out_shape=jax.ShapeDtypeStruct((rows, width), jnp.bfloat16),
        grid_spec=pltpu.PrefetchScalarGridSpec(
            num_scalar_prefetch=1,
            grid=(1,),
            in_specs=[
                pl.BlockSpec((rows, HEAD), lambda i, s: (0, 1)),
                home,
                home,
                pl.BlockSpec((slots, width), lambda i, s: (0, 0)),
            ],
            out_specs=pl.BlockSpec(memory_space=pl.ANY),
            scratch_shapes=[
                pltpu.VMEM((4, rows, part), jnp.bfloat16),
                pltpu.SemaphoreType.DMA((4,)),
            ],
        ),
        compiler_params=pltpu.CompilerParams(vmem_limit_bytes=LIMIT),
        cost_estimate=pl.CostEstimate(
            flops=2 * rows * slots * width,
            bytes_accessed=4 * rows * width,
            transcendentals=0,
        ),
    )(scalars, table, mine, other, spans)


def per_device(states, queries, kv_weight, kv_bias, lengths, bounds, balance):
    replicas = lax.axis_size("dp")
    own_index = lax.axis_index("dp")
    half = (lax.axis_index("group") % 2).astype(jnp.int32)[None]
    core = (own_index % 2).astype(jnp.int32)[None]
    own_y = own_index // 2 % 2
    own_z = own_index // 4
    ring = replicas // 4
    position = jnp.where(own_z % 2 == 0, own_z // 2, ring - 1 - own_z // 2)
    tokens = states.shape[0]
    depth, width = kv_weight.shape

    def block(offset, across):
        z = ring_place(ring, (position - offset + ring) % ring)
        return (z * 2 + (1 - own_y if across else own_y)).astype(jnp.int32)

    token_ids = jnp.arange(tokens, dtype=jnp.int32)
    is_live = token_ids < lengths[0] * SPAN
    owner = jnp.repeat(balance[0], SPAN)
    is_moved = is_live & (owner != own_index)
    destination = jnp.where(is_moved, owner, -1)
    keep = is_live & jnp.logical_not(is_moved)
    kept_count = jnp.sum(keep.astype(jnp.int32)) // SPAN
    chosen, rejected = bounds[0, 0], bounds[0, 1]
    segment = (token_ids >= chosen).astype(jnp.int32) + (token_ids >= rejected).astype(jnp.int32)
    place_ids = jnp.where(token_ids >= rejected, token_ids - (rejected - chosen), token_ids)
    target, source = token_ids[:, None], token_ids[None, :]
    near = (segment[None, :] == segment[:, None]) | (segment[None, :] == 0)
    allowed = ((source <= target) & is_live[None, :] & near) | (source == target)
    mask = jnp.where(allowed, 0.0, MASKED).astype(jnp.float32)
    frequency = jnp.exp(
        jnp.arange(HEAD // 2, dtype=jnp.float32) * (-2.0 * math.log(1000000.0) / HEAD)
    )
    angles = place_ids.astype(jnp.float32)[:, None] * frequency[None, :]
    columns = [jnp.cos(angles), jnp.sin(angles)]
    columns += [c.astype(jnp.float32)[:, None] for c in (is_live, destination, keep)]
    columns.append(jnp.zeros((tokens, HEAD - 3), jnp.float32))
    table = jnp.concatenate(columns, axis=1)
    scalars = jnp.stack([half[0], kept_count])
    plan = (table, mask, scalars)

    links = Links(replicas, lax.axis_size("group"))
    quarter = width // 4
    mine_weight = jnp.concatenate(
        [
            lax.dynamic_slice_in_dim(kv_weight, (2 * j + half[0]) * quarter, quarter, 1)
            for j in range(2)
        ],
        axis=1,
    )
    other_weight = head_pair(kv_weight, half, True)
    peer_columns = core_columns(states, 1 - core, depth)
    peer_states = core_swap(peer_columns, replicas)

    both = (peer_states, states)

    def listed(pieces):
        return jnp.stack([core[0], half[0]] + [b for _, b in pieces])

    fore = ring // 2
    order = [k for j in range(1, ring) for k in (j, -j)][: ring - 1]
    held = {0: mine_weight}
    mine = [(mine_weight, block(0, False))]
    other = [(other_weight, block(0, False))]
    middle, late = [], []
    crossed = links.send(mine_weight, "y")
    mine.append((crossed, block(0, True)))
    moving = other_weight
    for k in order:
        final = k == order[-1]
        nearer = held[k - 1] if k > 0 else held[k + 1]
        second = k == order[1]
        before = (peer_columns,) if second else plan if final else ()
        held[k] = links.send(nearer, "fore" if k > 0 else "back", before, lag=2 if second else None)
        mine.append((held[k], block(k, False)))
        crossed = links.send(held[k], "y")
        if 1 <= k < fore:
            swapped = links.send(held[k], "x")
            other.append((swapped, block(k, False)))
        if final:
            early = mine + other
            sums = accumulate(
                both,
                listed(early),
                [p for p, _ in early],
                [0] * len(mine) + [1] * len(other),
                bias=kv_bias[None, :],
            )
            swapped = links.send(swapped, "fore")
            middle.append((swapped, block(fore, False)))
            for j in range(1, ring - fore):
                moving = links.send(moving, "back", sums)
                (late if j == ring - fore - 1 else middle).append((moving, block(-j, False)))
            late.append((links.send(other_weight, "y"), block(0, True)))
            late.append((links.send(crossed, "x"), block(k, True)))
            middle = [(crossed, block(k, True))] + middle
            mine_peer, mine_own, other_peer, other_own, left_peer, left_own, pick = accumulate(
                both,
                listed(middle + late),
                [p for p, _ in middle],
                [0] + [1] * (len(middle) - 1),
                start=sums,
                later=len(late),
                table=table,
                rows=replicas * SPAN,
            )
        else:
            mine.append((crossed, block(k, True)))
            piece = (links.send(crossed, "x"), block(k, True))
            (middle if k == order[-2] else other).append(piece)

    mine_peer = core_swap(mine_peer, replicas)
    last = [p for p, _ in late]
    other_peer = core_swap(complete(left_peer, last, other_peer), replicas)
    other_own = complete(left_own, last, other_own)
    mine_own = after(mine_own, other_own)
    mine_kv, mine_spans = finish(mine_own, mine_peer, pick)
    other_kv, spans = finish(other_own, other_peer, pick, mine_spans)
    spans = spans.reshape(replicas, SPAN, width)
    spans = lax.all_to_all(spans, "dp", split_axis=0, concat_axis=0, tiled=True)
    spans = spans.reshape(replicas * SPAN, width)
    context = attend(half, False, mask, table, queries, mine_kv)
    context = attend(half, True, mask, table, queries, other_kv, context)
    work_rows = place(scalars, table, mine_kv, other_kv, spans)
    return (context, work_rows)


def solution(mesh):
    in_specs = (
        P(("group", "dp"), None),
        P(("group", "dp"), None),
        P("dp", None),
        P(),
        P(("group", "dp")),
        P(("group", "dp"), None),
        P(("group", "dp"), None),
    )
    out_specs = (P(("group", "dp"), None), P(("group", "dp"), None))
    return jax.shard_map(
        per_device, mesh=mesh, in_specs=in_specs, out_specs=out_specs, check_vma=False
    )
```
